32 devices in a mesh: mp: 2 (over x), tp: 8 (over z, core), dp: 2 (over y).
Axes of the slice: x: 2, y: 2, z: 4, core: 2. Of those that a mesh axis runs over, the one named last changes fastest.
Arguments:
- hidden: bfloat16 [2, 256, 28672], P('mp', 'dp', 'tp'), may hold values from -8 to 8
- down_weight: bfloat16 [2, 28672, 8192], P('mp', 'tp', 'dp'), may hold values from -0.03125 to 0.03125
- whitening: bfloat16 [2, 8192, 8192], P('mp', 'dp', 'tp'), may hold values from -0.0625 to 0.0625
Outputs:
- cross: float32 [8192, 8192], P(('mp', 'dp'), 'tp')
The draws below stay inside these ranges and needn't reach their ends.
All inputs are finite; a program needn't handle non-finite values.
Results may differ from the reference program's by a relative error of at most 0.0093.
Values may be sent and summed in bfloat16 or wider, within the bound.
No kernel may reach another device: no remote copies, remote signals or barrier semaphores. Data moves between devices by JAX's collectives and lax.ppermute only.
A program may use at most 128 MiB of HBM per device.

```python
import math
import jax
import jax.numpy as jnp
from jax import lax

D = 8192
FF = 28672
TOKENS = 256


def draw_hidden(key, part):
    key = jax.random.fold_in(key, 11)
    offset_key, noise_key = jax.random.split(key)
    noise = jax.random.normal(noise_key, (2, TOKENS, FF), jnp.float32)
    offsets = 0.8 * jax.random.normal(offset_key, (2, 1, FF), jnp.float32)
    return jnp.clip(noise + offsets, -8.0, 8.0).astype(jnp.bfloat16)


def level_of(stream_key, shape, cuts, smallest, largest):
    factor_of, own = 1.0, jax.random.fold_in(stream_key, 6)
    for axis_at, shards_of in cuts:
        steps = jnp.exp(jax.random.uniform(jax.random.fold_in(own, axis_at), (shards_of,), jnp.float32, smallest / len(cuts), largest / len(cuts)))
        factor_of = factor_of * jnp.repeat(steps, shape[axis_at] // shards_of).reshape([-1 if axis == axis_at else 1 for axis in range(len(shape))])
    return factor_of


def centred(rng, dims, width, reach, cuts=(), dtype=jnp.bfloat16):
    values = width * jax.random.normal(rng, dims, jnp.float32)
    if cuts:
        values = values * level_of(rng, dims, cuts, -0.22, 0.18)
    return jnp.clip(values, -reach, reach).astype(dtype)


def setup_inputs(seed: int = 0) -> dict:
    key_list = jax.random.split(jax.random.key(seed), 4)
    return {
        "hidden": draw_hidden(jax.random.fold_in(key_list[3], 71), 0),
        "down_weight": centred(key_list[1], (2, FF, D), FF ** -0.5, 0.03125, ((0, 2), (1, 8), (2, 2))),
        "whitening": centred(key_list[2], (2, D, D), D ** -0.5, 0.0625, ((0, 2), (1, 2), (2, 8))),
    }


def reference(hidden, down_weight, whitening):
    whites = []
    for model in range(2):
        outputs = jnp.dot(hidden[model], down_weight[model], preferred_element_type=jnp.float32).astype(jnp.bfloat16)
        wide = outputs.astype(jnp.float32)
        mean = lax.optimization_barrier(jnp.mean(wide, axis=0, keepdims=True))
        centered = (wide - mean).astype(jnp.bfloat16)
        white = jnp.dot(centered, whitening[model], preferred_element_type=jnp.float32).astype(jnp.bfloat16)
        whites.append(white)
    cross = lax.dot_general(whites[0], whites[1], (((0,), (0,)), ((), ())), preferred_element_type=jnp.float32)
    return cross * (1.0 / math.sqrt(TOKENS))
```

```python
import functools
import math

import jax
import jax.numpy as jnp
from jax import lax
from jax.experimental import pallas as pl
from jax.experimental.pallas import tpu as pltpu
from jax.sharding import PartitionSpec as P

F32 = jnp.float32
BF16 = jnp.bfloat16
VMEM_LIMIT = 6 * 2**20
VMEM_SMALL = 6 * 2**20


def params():
    return pltpu.CompilerParams(
        dimension_semantics=("arbitrary",), vmem_limit_bytes=VMEM_LIMIT
    )


def vmem():
    return pl.BlockSpec(memory_space=pltpu.VMEM)


def block_of(t, place):
    return t ^ (((place & 1) << 2) | (place & 2) | (place >> 2))


def held_in_vmem(block):
    return pltpu.with_memory_space_constraint(block, pltpu.VMEM)


def left_in_hbm(block):
    return pltpu.with_memory_space_constraint(block, pltpu.HBM)


def columns(i, width):
    return pl.ds(pl.multiple_of(i * width, width), width)


def own_kernel(rows, weights, send, keep, shift, held_keep, held_send, sems):
    t = lax.axis_index("tp")
    half, depth, width = held_keep.shape
    count = 2 * half
    piece = depth // 2

    def copy(held, base, i, k):
        source = weights.at[pl.ds(k * piece, piece), columns(block_of(t, base + i), width)]
        return pltpu.make_async_copy(
            source, held.at[i, pl.ds(k * piece, piece)], sems.at[base + i, k]
        )

    for held, base in ((held_keep, 0), (held_send, half)):
        for i in range(half):
            for k in range(2):
                copy(held, base, i, k).start()

    def product(held, base, i):
        copy(held, base, i, 0).wait()
        total = jnp.dot(rows[:, :piece], held[i, :piece], preferred_element_type=F32)
        copy(held, base, i, 1).wait()
        total += jnp.dot(rows[:, piece:], held[i, piece:], preferred_element_type=F32)
        mean = jnp.mean(total, axis=0, keepdims=True)
        shift[:, columns(base + i, width)] = mean
        return total - mean

    @pl.loop(0, half)
    def _(i):
        keep[:, columns(i, width)] = product(held_keep, 0, i)

    @pl.loop(0, half)
    def _(i):
        send[:, columns(i, width)] = product(held_send, half, i).astype(BF16)


def own_product(rows, weights):
    tokens, depth = rows.shape
    width = weights.shape[1] // 8
    return pl.pallas_call(
        own_kernel,
        out_shape=(
            jax.ShapeDtypeStruct((tokens, 4 * width), BF16),
            jax.ShapeDtypeStruct((tokens, 4 * width), F32),
            jax.ShapeDtypeStruct((1, 8 * width), F32),
            pltpu.VMEM((4, depth, width), BF16),
            pltpu.VMEM((4, depth, width), BF16),
        ),
        in_specs=[vmem(), pl.BlockSpec(memory_space=pltpu.HBM)],
        out_specs=(vmem(),) * 5,
        scratch_shapes=[pltpu.SemaphoreType.DMA((8, 2))],
        compiler_params=pltpu.CompilerParams(vmem_limit_bytes=VMEM_SMALL),
        cost_estimate=cheap(),
    )(rows, left_in_hbm(weights))


def first_kernel(rows, held_keep, held_send, factor, out, held_factor, sems):
    t = lax.axis_index("tp")
    half, _, width = held_keep.shape
    count = 2 * half
    depth = rows.shape[1]
    rows_of_factor = held_factor.shape[1]

    def copy(i):
        start = pl.multiple_of(block_of(t, i) * rows_of_factor, rows_of_factor)
        return pltpu.make_async_copy(
            factor.at[pl.ds(start, rows_of_factor)], held_factor.at[i], sems.at[i]
        )

    for i in range(count):
        copy(i).start()

    for held, base in ((held_keep, 0), (held_send, half)):

        @pl.loop(0, half)
        def _(i, held=held, base=base):
            out[:, columns(base + i, width)] = jnp.dot(
                rows[...], held[i, :depth], preferred_element_type=F32
            )

    for i in range(count):
        copy(i).wait()


def first_product(rows, held, factor):
    held_keep, held_send = held
    tokens = rows.shape[0]
    deep, wide = factor.shape
    return pl.pallas_call(
        first_kernel,
        out_shape=(
            jax.ShapeDtypeStruct((tokens, 8 * held_keep.shape[2]), F32),
            pltpu.VMEM((8, deep // 8, wide), BF16),
        ),
        in_specs=[vmem(), vmem(), vmem(), pl.BlockSpec(memory_space=pltpu.HBM)],
        out_specs=(vmem(), vmem()),
        scratch_shapes=[pltpu.SemaphoreType.DMA((8,))],
        compiler_params=pltpu.CompilerParams(vmem_limit_bytes=VMEM_SMALL),
        cost_estimate=cheap(),
    )(rows, held_in_vmem(held_keep), held_in_vmem(held_send), left_in_hbm(factor))


def second_kernel(rows, held_keep, held_send, start, shift, send, keep):
    half, _, width = held_keep.shape
    depth = rows.shape[1]

    def product(held, base, i):
        total = jnp.dot(rows[...], held[i, depth:], preferred_element_type=F32)
        return total + start[:, columns(base + i, width)] - shift[:, columns(base + i, width)]

    @pl.loop(0, half)
    def _(i):
        keep[:, columns(i, width)] = product(held_keep, 0, i)

    @pl.loop(0, half)
    def _(i):
        send[:, columns(i, width)] = product(held_send, half, i).astype(BF16)


def second_product(rows, held, start, shift):
    tokens = rows.shape[0]
    held_keep, held_send = held
    wide = 4 * held_keep.shape[2]
    return pl.pallas_call(
        second_kernel,
        out_shape=(
            jax.ShapeDtypeStruct((tokens, wide), BF16),
            jax.ShapeDtypeStruct((tokens, wide), F32),
        ),
        in_specs=[vmem()] * 5,
        out_specs=(vmem(), vmem()),
        compiler_params=pltpu.CompilerParams(vmem_limit_bytes=VMEM_SMALL),
        cost_estimate=cheap(),
    )(rows, held_in_vmem(held_keep), held_in_vmem(held_send), start, shift)


def white_kernel(base, rows, factor, *rest):
    *terms, out = rest
    count, depth = 4, factor.shape[1]
    total = None
    for i in range(count):
        part = jnp.dot(
            rows[:, i * depth : (i + 1) * depth], factor[base + i], preferred_element_type=F32
        )
        total = part if total is None else total + part
    for term in terms:
        total += term[...].astype(F32)
    out[...] = total.astype(out.dtype)


def white_product(rows, factor, base, dtype, *terms):
    return pl.pallas_call(
        functools.partial(white_kernel, base),
        out_shape=jax.ShapeDtypeStruct((rows.shape[0], factor.shape[2]), dtype),
        in_specs=[vmem()] * (2 + len(terms)),
        out_specs=vmem(),
        compiler_params=pltpu.CompilerParams(vmem_limit_bytes=VMEM_SMALL),
        cost_estimate=cheap(),
    )(rows, held_in_vmem(factor), *terms)


def cheap():
    return pl.CostEstimate(flops=1024, bytes_accessed=1024, transcendentals=0)


def cross_kernel(steps, scale, core, q1, q2, own1, own2, other1, other2, out, qwen):
    del core
    step = pl.program_id(0)

    @pl.when(step == 0)
    def _():
        wide = jnp.concatenate([q1[...], q2[...]], axis=0).astype(F32)
        qwen[...] = (wide - jnp.mean(wide, axis=0, keepdims=True)).astype(BF16)

    def block(first, second):
        llama = jnp.concatenate([first[...], second[...]], axis=0)
        out[...] = (
            lax.dot_general(
                llama, qwen[...], (((0,), (0,)), ((), ())), preferred_element_type=F32
            )
            * scale
        )

    @pl.when(step < steps)
    def _():
        block(own1, own2)

    @pl.when(step >= steps)
    def _():
        block(other1, other2)


def cross_product(core, q1, q2, own1, own2, other1, other2):
    half, width = q1.shape
    features = own1.shape[1]
    rows = min(256, features)
    steps = features // rows
    whole = pl.BlockSpec((half, width), lambda i, core: (0, 0))
    own = pl.BlockSpec((half, rows), lambda i, core: (0, jnp.minimum(i, steps - 1)))
    other = pl.BlockSpec((half, rows), lambda i, core: (0, jnp.maximum(i - steps, 0)))
    return pl.pallas_call(
        functools.partial(cross_kernel, steps, 1.0 / math.sqrt(2 * half)),
        out_shape=jax.ShapeDtypeStruct((2 * features, width), F32),
        grid_spec=pltpu.PrefetchScalarGridSpec(
            num_scalar_prefetch=1,
            grid=(2 * steps,),
            in_specs=[whole, whole, own, own, other, other],
            out_specs=pl.BlockSpec(
                (rows, width), lambda i, core: ((i + core[0] * steps) % (2 * steps), 0)
            ),
            scratch_shapes=[pltpu.VMEM((2 * half, width), BF16)],
        ),
        compiler_params=params(),
        cost_estimate=pl.CostEstimate(
            flops=8 * half * features * width,
            bytes_accessed=8 * features * width + 4 * half * (width + 2 * features),
            transcendentals=0,
        ),
    )(core, q1, q2, own1, own2, other1, other2)


def swapped(block, axis, mask):
    count = lax.axis_size(axis)
    return lax.ppermute(block, axis, [(i, i ^ mask) for i in range(count)])


def small_call(kernel, shapes, *args):
    return pl.pallas_call(
        kernel,
        out_shape=tuple(jax.ShapeDtypeStruct(shape, dtype) for shape, dtype in shapes),
        in_specs=[vmem()] * len(args),
        out_specs=tuple(vmem() for _ in shapes),
        compiler_params=pltpu.CompilerParams(vmem_limit_bytes=VMEM_SMALL),
        cost_estimate=cheap(),
    )(*args)


def halves(rows):
    tokens, width = rows.shape
    half = width // 2

    def kernel(whole, left, right):
        left[...] = whole[:, :half]
        right[...] = whole[:, half:]

    return small_call(kernel, [((tokens, half), rows.dtype)] * 2, rows)


def folded(keep, got):
    tokens, width = keep.shape
    half = width // 2

    def kernel(own, other, left, right):
        left[...] = own[:, :half] + other[:, :half].astype(F32)
        right[...] = (own[:, half:] + other[:, half:].astype(F32)).astype(BF16)

    return small_call(kernel, [((tokens, half), F32), ((tokens, half), BF16)], keep, got)


def total(keep, got):
    def kernel(own, other, out):
        out[...] = (own[...] + other[...].astype(F32)).astype(BF16)

    return small_call(kernel, [(keep.shape, BF16)], keep, got)[0]


def beside(left, right):
    tokens, width = left.shape

    def kernel(first, second, out):
        out[:, :width] = first[...]
        out[:, width:] = second[...]

    return small_call(kernel, [((tokens, 2 * width), left.dtype)], left, right)[0]


def sum_over_tp(send, keep):
    keep, give = folded(keep, swapped(send, "tp", 1))
    keep, give = folded(keep, swapped(give, "tp", 2))
    mine = total(keep, swapped(give, "tp", 4))
    pair = beside(mine, swapped(mine, "tp", 4))
    four = beside(pair, swapped(pair, "tp", 2))
    return four, swapped(four, "tp", 1)


MESH = ("mp", "tp", "dp")


def flat(x, t, y):
    return (x * 8 + t) * 2 + y


def route(block, moves):
    return lax.ppermute(block, MESH, [(flat(*a), flat(*b)) for a, b in moves])


def plan():
    across, along, second, far, near = [], [], [], [], []
    for t in range(8):
        z, core = t >> 1, t & 1
        tx, ty = z >> 1, z & 1
        for y in range(2):
            across.append(((1, t, y), (0, t, y)))
            along.append(((1, t, y), (1, t, 1 - y)))
            second.append(((1, t, 1 - y), (0, t, y)))
            if tx == 1:
                across.append(((0, t, y), (1, t, y)))
        if tx == 0:
            along.append(((0, t, 1 - ty), (0, t, ty)))
        else:
            second.append(((0, t, 1 - ty), (1, t, ty)))
    hops = {
        0: (((0, 2),), ((0, 1), (2, 3))),
        1: (((1, 2),), ((1, 0), (2, 3))),
        2: (((2, 1),), ((2, 3), (1, 0))),
        3: (((3, 1),), ((3, 2), (1, 0))),
    }
    for x in range(2):
        for y in range(2):
            for moves, step in zip((far, near), hops[2 * x + y]):
                for a, b in step:
                    for core in range(2):
                        moves.append(((x, 2 * a + core, y), (x, 2 * b + core, y)))
    return across, along, second, far, near


def pipelined(hidden, down_weight, whitening):
    acts, weights, factor = hidden[0], down_weight[0], whitening[0]
    x, t, y = lax.axis_index("mp"), lax.axis_index("tp"), lax.axis_index("dp")
    z, core = t >> 1, t & 1
    across, along, second, far, near = plan()

    others = [swapped(piece, "dp", 1) for piece in halves(acts)]

    send, keep, shift, *held = own_product(acts, weights)
    four, rest = sum_over_tp(send, keep)
    start, held_factor = first_product(others[0], held, factor)
    early = white_product(four, held_factor, 0, F32)
    early = white_product(rest, held_factor, 4, BF16, early)
    got = swapped(early, "dp", 1)

    four, rest = sum_over_tp(*second_product(others[1], held, start, shift))
    late = white_product(four, held_factor, 0, F32)
    half = white_product(rest, held_factor, 4, BF16, late, got)

    a = route(half, across)
    b = route(half, along)
    c = route(half, second)
    llama_side = x == 0
    l1 = jnp.where(llama_side, half, a)
    l2 = jnp.where(llama_side, b, c)
    q1 = jnp.where(llama_side, a, half)
    q2 = jnp.where(llama_side, c, b)

    source = 2 * x + y
    has = (z == source) | ((source == 0) & (z == 2)) | ((source == 3) & (z == 1))
    has = has | ((source == 1) & (z == 2)) | ((source == 2) & (z == 1))

    def spread(block):
        first = jnp.where(z == source, block, route(block, far))
        return jnp.where(has, first, route(first, near))

    l1, l2 = spread(l1), spread(l2)
    o1, o2 = swapped(l1, "tp", 1), swapped(l2, "tp", 1)
    return cross_product(core.reshape(1), q1, q2, l1, l2, o1, o2)


def general(hidden, down_weight, whitening):
    acts, weights, factor = hidden[0], down_weight[0], whitening[0]
    tokens = lax.all_gather(acts, "dp", axis=0, tiled=True)
    partial = jnp.dot(tokens, weights, preferred_element_type=F32)
    outputs = lax.psum(partial, "tp").astype(BF16).astype(F32)
    centered = (outputs - jnp.mean(outputs, axis=0, keepdims=True)).astype(BF16)
    block = lax.psum_scatter(
        jnp.dot(centered, factor, preferred_element_type=F32),
        "dp",
        scatter_dimension=0,
        tiled=True,
    ).astype(BF16)
    both = lax.all_gather(block, "mp", axis=0)
    qwen = lax.all_gather(both[1], "dp", axis=0, tiled=True)
    llama = lax.all_gather(both[0], "tp", axis=1, tiled=True)
    width = llama.shape[1] // lax.axis_size("mp")
    llama = lax.dynamic_slice_in_dim(llama, lax.axis_index("mp") * width, width, 1)
    llama = lax.all_to_all(llama, "dp", split_axis=1, concat_axis=0, tiled=True)
    cross = lax.dot_general(llama, qwen, (((0,), (0,)), ((), ())), preferred_element_type=F32)
    return cross * (1.0 / math.sqrt(qwen.shape[0]))


def solution(mesh):
    placed = (P("mp", "dp", "tp"), P("mp", "tp", "dp"), P("mp", "dp", "tp"))
    sizes = tuple(mesh.shape[axis] for axis in MESH)
    body = pipelined if sizes == (2, 8, 2) else general
    return jax.shard_map(
        body, mesh=mesh, in_specs=placed, out_specs=P(("mp", "dp"), "tp"), check_vma=False
    )
```

```python
import functools
import math

import jax
import jax.numpy as jnp
from jax import lax
from jax.experimental import pallas as pl
from jax.experimental.pallas import tpu as pltpu
from jax.sharding import PartitionSpec as P

F32 = jnp.float32
BF16 = jnp.bfloat16
VMEM_LIMIT = 6 * 2**20
VMEM_SMALL = 4 * 2**20
GROUP_TYPES = (F32, F32, BF16, BF16)


def params():
    return pltpu.CompilerParams(
        dimension_semantics=("arbitrary",), vmem_limit_bytes=VMEM_LIMIT
    )


def vmem():
    return pl.BlockSpec(memory_space=pltpu.VMEM)


def block_of(t, place):
    return t ^ (((place & 1) << 2) | (place & 2) | (place >> 2))


def held_in_vmem(block):
    return pltpu.with_memory_space_constraint(block, pltpu.VMEM)


def left_in_hbm(block):
    return pltpu.with_memory_space_constraint(block, pltpu.HBM)


def columns(i, width):
    return pl.ds(pl.multiple_of(i * width, width), width)


def each_group(groups, held_keep, held_send, product):
    half, _, width = held_keep.shape
    for number, group in enumerate(groups):
        held, base = (held_keep, 0) if number < 2 else (held_send, half)
        first = number % 2 * 2

        @pl.loop(0, 2)
        def _(i, held=held, base=base, first=first, group=group):
            group[:, columns(i, width)] = product(held, base, first + i).astype(group.dtype)


def own_kernel(left, right, weights, *rest):
    *groups, shift, held_keep, held_send, sems = rest
    t = lax.axis_index("tp")
    half, depth, width = held_keep.shape
    count = 2 * half
    cut = left.shape[1]

    def copy(held, base, i, k):
        part = pl.ds(0, cut) if k == 0 else pl.ds(cut, depth - cut)
        source = weights.at[part, columns(block_of(t, base + i), width)]
        return pltpu.make_async_copy(source, held.at[i, part], sems.at[base + i, k])

    for held, base in ((held_keep, 0), (held_send, half)):
        for i in range(half):
            for k in range(2):
                copy(held, base, i, k).start()

    def product(held, base, i):
        copy(held, base, i, 0).wait()
        total = jnp.dot(left[...], held[i, :cut], preferred_element_type=F32)
        copy(held, base, i, 1).wait()
        total += jnp.dot(right[...], held[i, cut:], preferred_element_type=F32)
        mean = jnp.mean(total, axis=0, keepdims=True)
        shift[:, columns(base + i, width)] = mean
        return total - mean

    each_group(groups, held_keep, held_send, product)


def own_product(left, right, weights):
    tokens = left.shape[0]
    depth = weights.shape[0]
    width = weights.shape[1] // 8
    return pl.pallas_call(
        own_kernel,
        out_shape=(
            *[jax.ShapeDtypeStruct((tokens, 2 * width), dtype) for dtype in GROUP_TYPES],
            jax.ShapeDtypeStruct((1, 8 * width), F32),
            pltpu.VMEM((4, depth, width), BF16),
            pltpu.VMEM((4, depth, width), BF16),
        ),
        in_specs=[vmem(), vmem(), pl.BlockSpec(memory_space=pltpu.HBM)],
        out_specs=(vmem(),) * 7,
        scratch_shapes=[pltpu.SemaphoreType.DMA((8, 2))],
        compiler_params=pltpu.CompilerParams(vmem_limit_bytes=VMEM_SMALL),
        cost_estimate=cheap(),
    )(left, right, left_in_hbm(weights))


def first_kernel(rows, held_keep, held_send, out):
    half, _, width = held_keep.shape
    depth = rows.shape[1]
    for held, base in ((held_keep, 0), (held_send, half)):

        @pl.loop(0, half)
        def _(i, held=held, base=base):
            out[:, columns(base + i, width)] = jnp.dot(
                rows[...], held[i, :depth], preferred_element_type=F32
            )


def first_product(rows, held, after=()):
    shape = (rows.shape[0], 8 * held[0].shape[2])
    args = [rows, *map(held_in_vmem, held)]
    return ordered_call(first_kernel, [(shape, F32)], args, after)[0]


def second_kernel(rows, held_keep, held_send, start, shift, *groups):
    _, depth, width = held_keep.shape
    cut = depth - rows.shape[1]

    def product(held, base, i):
        total = jnp.dot(rows[...], held[i, cut:], preferred_element_type=F32)
        return total + start[:, columns(base + i, width)] - shift[:, columns(base + i, width)]

    each_group(groups, held_keep, held_send, product)


def second_product(rows, held, start, shift, after=()):
    tokens = rows.shape[0]
    held_keep, held_send = held
    wide = 2 * held_keep.shape[2]
    return ordered_call(
        second_kernel,
        [((tokens, wide), dtype) for dtype in GROUP_TYPES],
        [rows, held_in_vmem(held_keep), held_in_vmem(held_send), start, shift],
        after,
    )


def hold_kernel(factor, *rest):
    held, sems = rest[-2:]
    t = lax.axis_index("tp")
    count, rows, _ = held.shape

    def copy(i):
        start = pl.multiple_of(block_of(t, i) * rows, rows)
        return pltpu.make_async_copy(factor.at[pl.ds(start, rows)], held.at[i], sems.at[i])

    for i in range(count):
        copy(i).start()
    for i in range(count):
        copy(i).wait()


def hold(factor, after):
    deep, wide = factor.shape
    return pl.pallas_call(
        hold_kernel,
        out_shape=pltpu.VMEM((8, deep // 8, wide), BF16),
        in_specs=[pl.BlockSpec(memory_space=pltpu.HBM)]
        + [pl.BlockSpec(memory_space=pl.ANY)] * len(after),
        out_specs=vmem(),
        scratch_shapes=[pltpu.SemaphoreType.DMA((8,))],
        compiler_params=pltpu.CompilerParams(vmem_limit_bytes=VMEM_SMALL),
        cost_estimate=cheap(),
    )(left_in_hbm(factor), *after)


def white_kernel(base, rows, factor, *rest):
    *terms, out = rest
    count, depth = 4, factor.shape[1]
    total = None
    for i in range(count):
        part = jnp.dot(
            rows[:, i * depth : (i + 1) * depth], factor[base + i], preferred_element_type=F32
        )
        total = part if total is None else total + part
    for term in terms:
        total += term[...].astype(F32)
    out[...] = total.astype(out.dtype)


def white_product(rows, factor, base, dtype, *terms, after=()):
    shape = (rows.shape[0], factor.shape[2])
    args = [rows, held_in_vmem(factor), *terms]
    return ordered_call(functools.partial(white_kernel, base), [(shape, dtype)], args, after)[0]


def cheap():
    return pl.CostEstimate(flops=1024, bytes_accessed=1024, transcendentals=0)


def cross_kernel(steps, scale, core, q1, q2, own1, own2, other1, other2, out, qwen):
    del core
    step = pl.program_id(0)

    @pl.when(step == 0)
    def _():
        wide = jnp.concatenate([q1[...], q2[...]], axis=0).astype(F32)
        qwen[...] = (scale * (wide - jnp.mean(wide, axis=0, keepdims=True))).astype(BF16)

    def block(first, second):
        llama = jnp.concatenate([first[...], second[...]], axis=0)
        out[...] = lax.dot_general(
            llama, qwen[...], (((0,), (0,)), ((), ())), preferred_element_type=F32
        )

    @pl.when(step < steps)
    def _():
        block(own1, own2)

    @pl.when(step >= steps)
    def _():
        block(other1, other2)


def cross_product(core, q1, q2, own1, own2, other1, other2):
    half, width = q1.shape
    features = own1.shape[1]
    rows = min(256, features)
    steps = features // rows
    whole = pl.BlockSpec((half, width), lambda i, core: (0, 0))
    own = pl.BlockSpec((half, rows), lambda i, core: (0, jnp.minimum(i, steps - 1)))
    other = pl.BlockSpec((half, rows), lambda i, core: (0, jnp.maximum(i - steps, 0)))
    return pl.pallas_call(
        functools.partial(cross_kernel, steps, 1.0 / math.sqrt(2 * half)),
        out_shape=jax.ShapeDtypeStruct((2 * features, width), F32),
        grid_spec=pltpu.PrefetchScalarGridSpec(
            num_scalar_prefetch=1,
            grid=(2 * steps,),
            in_specs=[whole, whole, own, own, other, other],
            out_specs=pl.BlockSpec(
                (rows, width), lambda i, core: ((i + core[0] * steps) % (2 * steps), 0)
            ),
            scratch_shapes=[pltpu.VMEM((2 * half, width), BF16)],
        ),
        compiler_params=params(),
        cost_estimate=pl.CostEstimate(
            flops=8 * half * features * width,
            bytes_accessed=8 * features * width + 4 * half * (width + 2 * features),
            transcendentals=0,
        ),
    )(core, q1, q2, own1, own2, other1, other2)


def swapped(block, axis, mask):
    count = lax.axis_size(axis)
    return lax.ppermute(block, axis, [(i, i ^ mask) for i in range(count)])


def ordered_call(kernel, shapes, args, after=()):
    def body(*refs):
        kernel(*refs[: len(args)], *refs[len(args) + len(after) :])

    return pl.pallas_call(
        body,
        out_shape=tuple(jax.ShapeDtypeStruct(shape, dtype) for shape, dtype in shapes),
        in_specs=[vmem()] * len(args) + [pl.BlockSpec(memory_space=pl.ANY)] * len(after),
        out_specs=tuple(vmem() for _ in shapes),
        compiler_params=pltpu.CompilerParams(vmem_limit_bytes=VMEM_SMALL),
        cost_estimate=cheap(),
    )(*args, *after)


def cut_at(rows, cut):
    tokens, width = rows.shape

    def kernel(whole, left, right):
        left[...] = whole[:, :cut]
        right[...] = whole[:, cut:]

    shapes = [((tokens, cut), rows.dtype), ((tokens, width - cut), rows.dtype)]
    return ordered_call(kernel, shapes, [rows])


def folded(keep, *got, after=()):
    tokens, width = keep.shape
    half = width // 2

    def kernel(*refs):
        *terms, left, right = refs
        left[...] = sum(term[:, :half].astype(F32) for term in terms)
        right[...] = sum(term[:, half:].astype(F32) for term in terms).astype(BF16)

    shapes = [((tokens, half), F32), ((tokens, half), BF16)]
    return ordered_call(kernel, shapes, [keep, *got], after)


def total(keep, got, after=()):
    def kernel(own, other, out):
        out[...] = (own[...] + other[...].astype(F32)).astype(BF16)

    return ordered_call(kernel, [(keep.shape, BF16)], [keep, got], after)[0]


def beside(left, right, after=()):
    tokens, width = left.shape

    def kernel(first, second, out):
        out[:, :width] = first[...]
        out[:, width:] = second[...]

    return ordered_call(kernel, [((tokens, 2 * width), left.dtype)], [left, right], after)[0]


MESH = ("mp", "tp", "dp")


def flat(x, t, y):
    return (x * 8 + t) * 2 + y


def route(block, moves):
    return lax.ppermute(block, MESH, [(flat(*a), flat(*b)) for a, b in moves])


def plan():
    across, along, second, far, near = [], [], [], [], []
    for t in range(8):
        z, core = t >> 1, t & 1
        tx, ty = z >> 1, z & 1
        for y in range(2):
            across.append(((1, t, y), (0, t, y)))
            along.append(((1, t, y), (1, t, 1 - y)))
            second.append(((1, t, 1 - y), (0, t, y)))
            if tx == 1:
                across.append(((0, t, y), (1, t, y)))
        if tx == 0:
            along.append(((0, t, 1 - ty), (0, t, ty)))
        else:
            second.append(((0, t, 1 - ty), (1, t, ty)))
    hops = {
        0: (((0, 2),), ((0, 1), (2, 3))),
        1: (((1, 2),), ((1, 0), (2, 3))),
        2: (((2, 1),), ((2, 3), (1, 0))),
        3: (((3, 1),), ((3, 2), (1, 0))),
    }
    for x in range(2):
        for y in range(2):
            for moves, step in zip((far, near), hops[2 * x + y]):
                for a, b in step:
                    for core in range(2):
                        moves.append(((x, 2 * a + core, y), (x, 2 * b + core, y)))
    return across, along, second, far, near


def pipelined(hidden, down_weight, whitening):
    acts, weights, factor = hidden[0], down_weight[0], whitening[0]
    x, t, y = lax.axis_index("mp"), lax.axis_index("tp"), lax.axis_index("dp")
    z, core = t >> 1, t & 1
    across, along, second, far, near = plan()

    depth = acts.shape[1]
    pieces = cut_at(acts, depth * 5 // 7 // 256 * 256)
    others = [swapped(piece, "dp", 1) for piece in pieces]
    o_keep, o_pass, o_other, o_give, shift, *held = own_product(*pieces, weights)
    o_give = total(o_pass, swapped(o_give, "tp", 1))
    o_other = swapped(o_other, "tp", 1)
    start = first_product(others[0], held, after=[o_give])
    o_keep, o_give = folded(o_keep, o_other, swapped(o_give, "tp", 2), after=[start])
    groups = second_product(others[1], held, start, shift, after=[o_give])
    p_keep, p_pass, p_other, p_give = groups
    p_give = total(p_pass, swapped(p_give, "tp", 1))
    p_other = swapped(p_other, "tp", 1)
    held_factor = hold(factor, after=[p_give])
    o_sum = total(o_keep, swapped(o_give, "tp", 4), after=[p_give])
    p_keep, p_give = folded(p_keep, p_other, swapped(p_give, "tp", 2), after=[o_sum])
    o_sum = beside(o_sum, swapped(o_sum, "tp", 4), after=[p_give])
    p_sum = total(p_keep, swapped(p_give, "tp", 4), after=[o_sum])
    o_sum = beside(o_sum, swapped(o_sum, "tp", 2), after=[p_sum])
    p_sum = beside(p_sum, swapped(p_sum, "tp", 4), after=[o_sum])
    o_white = white_product(o_sum, held_factor, 0, F32, after=[p_sum])
    o_white = white_product(swapped(o_sum, "tp", 1), held_factor, 4, BF16, o_white)
    got = swapped(o_white, "dp", 1)
    p_sum = beside(p_sum, swapped(p_sum, "tp", 2), after=[o_white])
    p_white = white_product(p_sum, held_factor, 0, F32)
    half = white_product(swapped(p_sum, "tp", 1), held_factor, 4, BF16, p_white, got)

    a = route(half, across)
    b = route(half, along)
    c = route(half, second)
    llama_side = x == 0
    l1 = jnp.where(llama_side, half, a)
    l2 = jnp.where(llama_side, b, c)
    q1 = jnp.where(llama_side, a, half)
    q2 = jnp.where(llama_side, c, b)

    source = 2 * x + y
    has = (z == source) | ((source == 0) & (z == 2)) | ((source == 3) & (z == 1))
    has = has | ((source == 1) & (z == 2)) | ((source == 2) & (z == 1))

    def spread(block):
        first = jnp.where(z == source, block, route(block, far))
        return jnp.where(has, first, route(first, near))

    l1, l2 = spread(l1), spread(l2)
    o1, o2 = swapped(l1, "tp", 1), swapped(l2, "tp", 1)
    return cross_product(core.reshape(1), q1, q2, l1, l2, o1, o2)


def general(hidden, down_weight, whitening):
    acts, weights, factor = hidden[0], down_weight[0], whitening[0]
    tokens = lax.all_gather(acts, "dp", axis=0, tiled=True)
    partial = jnp.dot(tokens, weights, preferred_element_type=F32)
    outputs = lax.psum(partial, "tp").astype(BF16).astype(F32)
    centered = (outputs - jnp.mean(outputs, axis=0, keepdims=True)).astype(BF16)
    block = lax.psum_scatter(
        jnp.dot(centered, factor, preferred_element_type=F32),
        "dp",
        scatter_dimension=0,
        tiled=True,
    ).astype(BF16)
    both = lax.all_gather(block, "mp", axis=0)
    qwen = lax.all_gather(both[1], "dp", axis=0, tiled=True)
    llama = lax.all_gather(both[0], "tp", axis=1, tiled=True)
    width = llama.shape[1] // lax.axis_size("mp")
    llama = lax.dynamic_slice_in_dim(llama, lax.axis_index("mp") * width, width, 1)
    llama = lax.all_to_all(llama, "dp", split_axis=1, concat_axis=0, tiled=True)
    cross = lax.dot_general(llama, qwen, (((0,), (0,)), ((), ())), preferred_element_type=F32)
    return cross * (1.0 / math.sqrt(qwen.shape[0]))


def solution(mesh):
    placed = (P("mp", "dp", "tp"), P("mp", "tp", "dp"), P("mp", "dp", "tp"))
    sizes = tuple(mesh.shape[axis] for axis in MESH)
    body = pipelined if sizes == (2, 8, 2) else general
    return jax.shard_map(
        body, mesh=mesh, in_specs=placed, out_specs=P(("mp", "dp"), "tp"), check_vma=False
    )
```

```python
import functools
import math

import jax
import jax.numpy as jnp
from jax import lax
from jax.experimental import pallas as pl
from jax.experimental.pallas import tpu as pltpu
from jax.sharding import PartitionSpec as P

F32 = jnp.float32
BF16 = jnp.bfloat16
VMEM_LIMIT = 6 * 2**20
VMEM_SMALL = 4 * 2**20
GROUP_TYPES = (F32, F32, BF16, BF16)


def params():
    return pltpu.CompilerParams(
        dimension_semantics=("arbitrary",), vmem_limit_bytes=VMEM_LIMIT
    )


def vmem():
    return pl.BlockSpec(memory_space=pltpu.VMEM)


def block_of(t, place):
    return t ^ (((place & 1) << 2) | (place & 2) | (place >> 2))


def held_in_vmem(block):
    return pltpu.with_memory_space_constraint(block, pltpu.VMEM)


def left_in_hbm(block):
    return pltpu.with_memory_space_constraint(block, pltpu.HBM)


def columns(i, width):
    return pl.ds(pl.multiple_of(i * width, width), width)


def each_group(groups, held_keep, held_send, product):
    half, _, width = held_keep.shape
    for number, group in enumerate(groups):
        held, base = (held_keep, 0) if number < 2 else (held_send, half)
        first = number % 2 * 2

        @pl.loop(0, 2)
        def _(i, held=held, base=base, first=first, group=group):
            group[:, columns(i, width)] = product(held, base, first + i).astype(group.dtype)


def own_kernel(left, right, weights, *rest):
    *groups, shift, held_keep, held_send, sems = rest
    t = lax.axis_index("tp")
    half, depth, width = held_keep.shape
    count = 2 * half
    cut = left.shape[1]

    def copy(held, base, i, k):
        part = pl.ds(0, cut) if k == 0 else pl.ds(cut, depth - cut)
        source = weights.at[part, columns(block_of(t, base + i), width)]
        return pltpu.make_async_copy(source, held.at[i, part], sems.at[base + i, k])

    for held, base in ((held_keep, 0), (held_send, half)):
        for i in range(half):
            for k in range(2):
                copy(held, base, i, k).start()

    def product(held, base, i):
        copy(held, base, i, 0).wait()
        total = jnp.dot(left[...], held[i, :cut], preferred_element_type=F32)
        copy(held, base, i, 1).wait()
        total += jnp.dot(right[...], held[i, cut:], preferred_element_type=F32)
        mean = jnp.mean(total, axis=0, keepdims=True)
        shift[:, columns(base + i, width)] = mean
        return total - mean

    each_group(groups, held_keep, held_send, product)


def own_product(left, right, weights):
    tokens = left.shape[0]
    depth = weights.shape[0]
    width = weights.shape[1] // 8
    return pl.pallas_call(
        own_kernel,
        out_shape=(
            *[jax.ShapeDtypeStruct((tokens, 2 * width), dtype) for dtype in GROUP_TYPES],
            jax.ShapeDtypeStruct((1, 8 * width), F32),
            pltpu.VMEM((4, depth, width), BF16),
            pltpu.VMEM((4, depth, width), BF16),
        ),
        in_specs=[vmem(), vmem(), pl.BlockSpec(memory_space=pltpu.HBM)],
        out_specs=(vmem(),) * 7,
        scratch_shapes=[pltpu.SemaphoreType.DMA((8, 2))],
        compiler_params=pltpu.CompilerParams(vmem_limit_bytes=VMEM_SMALL),
        cost_estimate=cheap(),
    )(left, right, left_in_hbm(weights))


def first_kernel(rows, held_keep, held_send, out):
    half, _, width = held_keep.shape
    depth = rows.shape[1]
    for held, base in ((held_keep, 0), (held_send, half)):

        @pl.loop(0, half)
        def _(i, held=held, base=base):
            out[:, columns(base + i, width)] = jnp.dot(
                rows[...], held[i, :depth], preferred_element_type=F32
            )


def first_product(rows, held, after=()):
    shape = (rows.shape[0], 8 * held[0].shape[2])
    args = [rows, *map(held_in_vmem, held)]
    return ordered_call(first_kernel, [(shape, F32)], args, after, cheap())[0]


def second_kernel(rows, held_keep, held_send, start, shift, *groups):
    _, depth, width = held_keep.shape
    cut = depth - rows.shape[1]

    def product(held, base, i):
        total = jnp.dot(rows[...], held[i, cut:], preferred_element_type=F32)
        return total + start[:, columns(base + i, width)] - shift[:, columns(base + i, width)]

    each_group(groups, held_keep, held_send, product)


def second_product(rows, held, start, shift, after=()):
    tokens = rows.shape[0]
    held_keep, held_send = held
    wide = 2 * held_keep.shape[2]
    return ordered_call(
        second_kernel,
        [((tokens, wide), dtype) for dtype in GROUP_TYPES],
        [rows, held_in_vmem(held_keep), held_in_vmem(held_send), start, shift],
        after,
        cheap(),
    )


def hold_kernel(factor, *rest):
    held, sems = rest[-2:]
    t = lax.axis_index("tp")
    count, rows, _ = held.shape

    def copy(i):
        start = pl.multiple_of(block_of(t, i) * rows, rows)
        return pltpu.make_async_copy(factor.at[pl.ds(start, rows)], held.at[i], sems.at[i])

    for i in range(count):
        copy(i).start()
    for i in range(count):
        copy(i).wait()


def hold(factor, after):
    deep, wide = factor.shape
    return pl.pallas_call(
        hold_kernel,
        out_shape=pltpu.VMEM((8, deep // 8, wide), BF16),
        in_specs=[pl.BlockSpec(memory_space=pltpu.HBM)]
        + [pl.BlockSpec(memory_space=pl.ANY)] * len(after),
        out_specs=vmem(),
        scratch_shapes=[pltpu.SemaphoreType.DMA((8,))],
        compiler_params=pltpu.CompilerParams(vmem_limit_bytes=VMEM_SMALL),
        cost_estimate=cheap(),
    )(left_in_hbm(factor), *after)


def white_kernel(base, rows, factor, *rest):
    *terms, out = rest
    count, depth = 4, factor.shape[1]
    total = None
    for i in range(count):
        part = jnp.dot(
            rows[:, i * depth : (i + 1) * depth], factor[base + i], preferred_element_type=F32
        )
        total = part if total is None else total + part
    for term in terms:
        total += term[...].astype(F32)
    out[...] = total.astype(out.dtype)


def white_product(rows, factor, base, dtype, *terms, after=()):
    shape = (rows.shape[0], factor.shape[2])
    args = [rows, held_in_vmem(factor), *terms]
    return ordered_call(functools.partial(white_kernel, base), [(shape, dtype)], args, after)[0]


def cheap():
    return pl.CostEstimate(flops=1024, bytes_accessed=1024, transcendentals=0)


def slow():
    return pl.CostEstimate(flops=10**11, bytes_accessed=10**8, transcendentals=0)


def cross_kernel(steps, scale, core, q1, q2, own1, own2, other1, other2, out, qwen):
    del core
    step = pl.program_id(0)

    @pl.when(step == 0)
    def _():
        wide = jnp.concatenate([q1[...], q2[...]], axis=0).astype(F32)
        qwen[...] = (scale * (wide - jnp.mean(wide, axis=0, keepdims=True))).astype(BF16)

    def block(first, second):
        llama = jnp.concatenate([first[...], second[...]], axis=0)
        out[...] = lax.dot_general(
            llama, qwen[...], (((0,), (0,)), ((), ())), preferred_element_type=F32
        )

    @pl.when(step < steps)
    def _():
        block(own1, own2)

    @pl.when(step >= steps)
    def _():
        block(other1, other2)


def cross_product(core, q1, q2, own1, own2, other1, other2):
    half, width = q1.shape
    features = own1.shape[1]
    rows = min(256, features)
    steps = features // rows
    whole = pl.BlockSpec((half, width), lambda i, core: (0, 0))
    own = pl.BlockSpec((half, rows), lambda i, core: (0, jnp.minimum(i, steps - 1)))
    other = pl.BlockSpec((half, rows), lambda i, core: (0, jnp.maximum(i - steps, 0)))
    return pl.pallas_call(
        functools.partial(cross_kernel, steps, 1.0 / math.sqrt(2 * half)),
        out_shape=jax.ShapeDtypeStruct((2 * features, width), F32),
        grid_spec=pltpu.PrefetchScalarGridSpec(
            num_scalar_prefetch=1,
            grid=(2 * steps,),
            in_specs=[whole, whole, own, own, other, other],
            out_specs=pl.BlockSpec(
                (rows, width), lambda i, core: ((i + core[0] * steps) % (2 * steps), 0)
            ),
            scratch_shapes=[pltpu.VMEM((2 * half, width), BF16)],
        ),
        compiler_params=params(),
        cost_estimate=pl.CostEstimate(
            flops=8 * half * features * width,
            bytes_accessed=8 * features * width + 4 * half * (width + 2 * features),
            transcendentals=0,
        ),
    )(core, q1, q2, own1, own2, other1, other2)


def swapped(block, axis, mask):
    count = lax.axis_size(axis)
    return lax.ppermute(block, axis, [(i, i ^ mask) for i in range(count)])


def ordered_call(kernel, shapes, args, after=(), cost=None):
    def body(*refs):
        kernel(*refs[: len(args)], *refs[len(args) + len(after) :])

    return pl.pallas_call(
        body,
        out_shape=tuple(jax.ShapeDtypeStruct(shape, dtype) for shape, dtype in shapes),
        in_specs=[vmem()] * len(args) + [pl.BlockSpec(memory_space=pl.ANY)] * len(after),
        out_specs=tuple(vmem() for _ in shapes),
        compiler_params=pltpu.CompilerParams(vmem_limit_bytes=VMEM_SMALL),
        cost_estimate=cost or slow(),
    )(*args, *after)


def cut_at(rows, cut):
    tokens, width = rows.shape

    def kernel(whole, left, right):
        left[...] = whole[:, :cut]
        right[...] = whole[:, cut:]

    shapes = [((tokens, cut), rows.dtype), ((tokens, width - cut), rows.dtype)]
    return ordered_call(kernel, shapes, [rows], cost=cheap())


def folded(keep, *got, after=()):
    tokens, width = keep.shape
    half = width // 2

    def kernel(*refs):
        *terms, left, right = refs
        left[...] = sum(term[:, :half].astype(F32) for term in terms)
        right[...] = sum(term[:, half:].astype(F32) for term in terms).astype(BF16)

    shapes = [((tokens, half), F32), ((tokens, half), BF16)]
    return ordered_call(kernel, shapes, [keep, *got], after)


def total(keep, got, after=(), cost=None):
    def kernel(own, other, out):
        out[...] = (own[...] + other[...].astype(F32)).astype(BF16)

    return ordered_call(kernel, [(keep.shape, BF16)], [keep, got], after, cost)[0]


def beside(left, right, after=()):
    tokens, width = left.shape

    def kernel(first, second, out):
        out[:, :width] = first[...]
        out[:, width:] = second[...]

    return ordered_call(kernel, [((tokens, 2 * width), left.dtype)], [left, right], after)[0]


MESH = ("mp", "tp", "dp")


def flat(x, t, y):
    return (x * 8 + t) * 2 + y


def route(block, moves):
    return lax.ppermute(block, MESH, [(flat(*a), flat(*b)) for a, b in moves])


def plan():
    across, along, second, far, near = [], [], [], [], []
    for t in range(8):
        z, core = t >> 1, t & 1
        tx, ty = z >> 1, z & 1
        for y in range(2):
            across.append(((1, t, y), (0, t, y)))
            along.append(((1, t, y), (1, t, 1 - y)))
            second.append(((1, t, 1 - y), (0, t, y)))
            if tx == 1:
                across.append(((0, t, y), (1, t, y)))
        if tx == 0:
            along.append(((0, t, 1 - ty), (0, t, ty)))
        else:
            second.append(((0, t, 1 - ty), (1, t, ty)))
    hops = {
        0: (((0, 2),), ((0, 1), (2, 3))),
        1: (((1, 2),), ((1, 0), (2, 3))),
        2: (((2, 1),), ((2, 3), (1, 0))),
        3: (((3, 1),), ((3, 2), (1, 0))),
    }
    for x in range(2):
        for y in range(2):
            for moves, step in zip((far, near), hops[2 * x + y]):
                for a, b in step:
                    for core in range(2):
                        moves.append(((x, 2 * a + core, y), (x, 2 * b + core, y)))
    return across, along, second, far, near


def pipelined(hidden, down_weight, whitening):
    acts, weights, factor = hidden[0], down_weight[0], whitening[0]
    x, t, y = lax.axis_index("mp"), lax.axis_index("tp"), lax.axis_index("dp")
    z, core = t >> 1, t & 1
    across, along, second, far, near = plan()

    depth = acts.shape[1]
    pieces = cut_at(acts, depth * 5 // 7 // 256 * 256)
    others = [swapped(piece, "dp", 1) for piece in pieces]
    o_keep, o_pass, o_other, o_give, shift, *held = own_product(*pieces, weights)
    o_give = total(o_pass, swapped(o_give, "tp", 1), cost=cheap())
    o_other = swapped(o_other, "tp", 1)
    start = first_product(others[0], held, after=[o_give])
    o_keep, o_give = folded(o_keep, o_other, swapped(o_give, "tp", 2), after=[start])
    groups = second_product(others[1], held, start, shift, after=[o_give])
    p_keep, p_pass, p_other, p_give = groups
    p_give = total(p_pass, swapped(p_give, "tp", 1))
    p_other = swapped(p_other, "tp", 1)
    o_sum = total(o_keep, swapped(o_give, "tp", 4), after=[p_give])
    p_keep, p_give = folded(p_keep, p_other, swapped(p_give, "tp", 2), after=[o_sum])
    held_factor = hold(factor, after=[p_give])
    o_sum = beside(o_sum, swapped(o_sum, "tp", 4), after=[p_give])
    p_sum = total(p_keep, swapped(p_give, "tp", 4), after=[o_sum])
    o_sum = beside(o_sum, swapped(o_sum, "tp", 2), after=[p_sum])
    p_sum = beside(p_sum, swapped(p_sum, "tp", 4), after=[o_sum])
    o_white = white_product(o_sum, held_factor, 0, F32, after=[p_sum])
    o_white = white_product(swapped(o_sum, "tp", 1), held_factor, 4, BF16, o_white)
    got = swapped(o_white, "dp", 1)
    p_sum = beside(p_sum, swapped(p_sum, "tp", 2), after=[o_white])
    p_white = white_product(p_sum, held_factor, 0, F32)
    half = white_product(swapped(p_sum, "tp", 1), held_factor, 4, BF16, p_white, got)

    a = route(half, across)
    b = route(half, along)
    c = route(half, second)
    llama_side = x == 0
    l1 = jnp.where(llama_side, half, a)
    l2 = jnp.where(llama_side, b, c)
    q1 = jnp.where(llama_side, a, half)
    q2 = jnp.where(llama_side, c, b)

    source = 2 * x + y
    has = (z == source) | ((source == 0) & (z == 2)) | ((source == 3) & (z == 1))
    has = has | ((source == 1) & (z == 2)) | ((source == 2) & (z == 1))

    def spread(block):
        first = jnp.where(z == source, block, route(block, far))
        return jnp.where(has, first, route(first, near))

    l1, l2 = spread(l1), spread(l2)
    o1, o2 = swapped(l1, "tp", 1), swapped(l2, "tp", 1)
    return cross_product(core.reshape(1), q1, q2, l1, l2, o1, o2)


def general(hidden, down_weight, whitening):
    acts, weights, factor = hidden[0], down_weight[0], whitening[0]
    tokens = lax.all_gather(acts, "dp", axis=0, tiled=True)
    partial = jnp.dot(tokens, weights, preferred_element_type=F32)
    outputs = lax.psum(partial, "tp").astype(BF16).astype(F32)
    centered = (outputs - jnp.mean(outputs, axis=0, keepdims=True)).astype(BF16)
    block = lax.psum_scatter(
        jnp.dot(centered, factor, preferred_element_type=F32),
        "dp",
        scatter_dimension=0,
        tiled=True,
    ).astype(BF16)
    both = lax.all_gather(block, "mp", axis=0)
    qwen = lax.all_gather(both[1], "dp", axis=0, tiled=True)
    llama = lax.all_gather(both[0], "tp", axis=1, tiled=True)
    width = llama.shape[1] // lax.axis_size("mp")
    llama = lax.dynamic_slice_in_dim(llama, lax.axis_index("mp") * width, width, 1)
    llama = lax.all_to_all(llama, "dp", split_axis=1, concat_axis=0, tiled=True)
    cross = lax.dot_general(llama, qwen, (((0,), (0,)), ((), ())), preferred_element_type=F32)
    return cross * (1.0 / math.sqrt(qwen.shape[0]))


def solution(mesh):
    placed = (P("mp", "dp", "tp"), P("mp", "tp", "dp"), P("mp", "dp", "tp"))
    sizes = tuple(mesh.shape[axis] for axis in MESH)
    body = pipelined if sizes == (2, 8, 2) else general
    return jax.shard_map(
        body, mesh=mesh, in_specs=placed, out_specs=P(("mp", "dp"), "tp"), check_vma=False
    )
```

```python
import functools
import math

import jax
import jax.numpy as jnp
from jax import lax
from jax.experimental import pallas as pl
from jax.experimental.pallas import tpu as pltpu
from jax.sharding import PartitionSpec as P

F32 = jnp.float32
BF16 = jnp.bfloat16
VMEM_LIMIT = 8 * 2**20
VMEM_SMALL = 4 * 2**20
MESH = ("mp", "tp", "dp")
GROUP_TYPES = (F32, F32, BF16, BF16)


def vmem():
    return pl.BlockSpec(memory_space=pltpu.VMEM)


def block_of(t, place):
    return t ^ (((place & 1) << 2) | (place & 2) | (place >> 2))


def held_in_vmem(block):
    return pltpu.with_memory_space_constraint(block, pltpu.VMEM)


def left_in_hbm(block):
    return pltpu.with_memory_space_constraint(block, pltpu.HBM)


def columns(i, width):
    return pl.ds(pl.multiple_of(i * width, width), width)


def each_group(groups, held_keep, held_send, product):
    half, _, width = held_keep.shape
    for number, group in enumerate(groups):
        held, base = (held_keep, 0) if number < 2 else (held_send, half)
        first = number % 2 * 2

        @pl.loop(0, 2)
        def _(i, held=held, base=base, first=first, group=group):
            group[:, columns(i, width)] = product(held, base, first + i).astype(group.dtype)


def own_kernel(left, right, weights, *rest):
    *groups, shift, held_keep, held_send, sems = rest
    t = lax.axis_index("tp")
    half, depth, width = held_keep.shape
    count = 2 * half
    cut = left.shape[1]

    def copy(held, base, i, k):
        part = pl.ds(0, cut) if k == 0 else pl.ds(cut, depth - cut)
        source = weights.at[part, columns(block_of(t, base + i), width)]
        return pltpu.make_async_copy(source, held.at[i, part], sems.at[base + i, k])

    for held, base in ((held_keep, 0), (held_send, half)):
        for i in range(half):
            for k in range(2):
                copy(held, base, i, k).start()

    def product(held, base, i):
        copy(held, base, i, 0).wait()
        total = jnp.dot(left[...], held[i, :cut], preferred_element_type=F32)
        copy(held, base, i, 1).wait()
        total += jnp.dot(right[...], held[i, cut:], preferred_element_type=F32)
        mean = jnp.mean(total, axis=0, keepdims=True)
        shift[:, columns(base + i, width)] = mean
        return total - mean

    each_group(groups, held_keep, held_send, product)


def own_product(left, right, weights):
    tokens = left.shape[0]
    depth = weights.shape[0]
    width = weights.shape[1] // 8
    return pl.pallas_call(
        own_kernel,
        out_shape=(
            *[jax.ShapeDtypeStruct((tokens, 2 * width), dtype) for dtype in GROUP_TYPES],
            jax.ShapeDtypeStruct((1, 8 * width), F32),
            pltpu.VMEM((4, depth, width), BF16),
            pltpu.VMEM((4, depth, width), BF16),
        ),
        in_specs=[vmem(), vmem(), pl.BlockSpec(memory_space=pltpu.HBM)],
        out_specs=(vmem(),) * 7,
        scratch_shapes=[pltpu.SemaphoreType.DMA((8, 2))],
        compiler_params=pltpu.CompilerParams(vmem_limit_bytes=VMEM_SMALL),
        cost_estimate=cheap(),
    )(left, right, left_in_hbm(weights))


def first_kernel(rows, held_keep, held_send, out):
    half, _, width = held_keep.shape
    depth = rows.shape[1]
    for held, base in ((held_keep, 0), (held_send, half)):

        @pl.loop(0, half)
        def _(i, held=held, base=base):
            out[:, columns(base + i, width)] = jnp.dot(
                rows[...], held[i, :depth], preferred_element_type=F32
            )


def first_product(rows, held, after=()):
    shape = (rows.shape[0], 8 * held[0].shape[2])
    args = [rows, *map(held_in_vmem, held)]
    return ordered_call(first_kernel, [(shape, F32)], args, after, cheap())[0]


def second_kernel(rows, held_keep, held_send, start, shift, *groups):
    _, depth, width = held_keep.shape
    cut = depth - rows.shape[1]

    def product(held, base, i):
        total = jnp.dot(rows[...], held[i, cut:], preferred_element_type=F32)
        return total + start[:, columns(base + i, width)] - shift[:, columns(base + i, width)]

    each_group(groups, held_keep, held_send, product)


def second_product(rows, held, start, shift, after=()):
    tokens = rows.shape[0]
    held_keep, held_send = held
    wide = 2 * held_keep.shape[2]
    return ordered_call(
        second_kernel,
        [((tokens, wide), dtype) for dtype in GROUP_TYPES],
        [rows, held_in_vmem(held_keep), held_in_vmem(held_send), start, shift],
        after,
        cheap(),
    )


def hold_kernel(factor, *rest):
    held, sems = rest[-2:]
    t = lax.axis_index("tp")
    count, rows, _ = held.shape

    def copy(i):
        start = pl.multiple_of(block_of(t, i) * rows, rows)
        return pltpu.make_async_copy(factor.at[pl.ds(start, rows)], held.at[i], sems.at[i])

    for i in range(count):
        copy(i).start()
    for i in range(count):
        copy(i).wait()


def hold(factor, after):
    deep, wide = factor.shape
    return pl.pallas_call(
        hold_kernel,
        out_shape=pltpu.VMEM((8, deep // 8, wide), BF16),
        in_specs=[pl.BlockSpec(memory_space=pltpu.HBM)]
        + [pl.BlockSpec(memory_space=pl.ANY)] * len(after),
        out_specs=vmem(),
        scratch_shapes=[pltpu.SemaphoreType.DMA((8,))],
        compiler_params=pltpu.CompilerParams(vmem_limit_bytes=VMEM_SMALL),
        cost_estimate=cheap(),
    )(left_in_hbm(factor), *after)


def white_kernel(base, rows, factor, *rest):
    *terms, out = rest
    count, depth = 4, factor.shape[1]
    total = None
    for i in range(count):
        part = jnp.dot(
            rows[:, i * depth : (i + 1) * depth], factor[base + i], preferred_element_type=F32
        )
        total = part if total is None else total + part
    for term in terms:
        total += term[...].astype(F32)
    out[...] = total.astype(out.dtype)


def white_product(rows, factor, base, dtype, *terms, after=()):
    shape = (rows.shape[0], factor.shape[2])
    args = [rows, held_in_vmem(factor), *terms]
    return ordered_call(functools.partial(white_kernel, base), [(shape, dtype)], args, after)[0]


def cheap():
    return pl.CostEstimate(flops=1024, bytes_accessed=1024, transcendentals=0)


def slow():
    return pl.CostEstimate(flops=10**10, bytes_accessed=10**9, transcendentals=0)


def qwen_kernel(scale, half, across, first, second, out):
    x, t, y = (lax.axis_index(axis) for axis in MESH)
    z = t >> 1
    llama_side, near = x == 0, z < 2
    other = jnp.where(llama_side, across[...], half[...])
    own = jnp.where(llama_side == near, first[...], second[...])
    flip = (z & 1) == y
    top, bottom = jnp.where(flip, other, own), jnp.where(flip, own, other)
    wide = jnp.concatenate([top, bottom], axis=0).astype(F32)
    out[...] = (scale * (wide - jnp.mean(wide, axis=0, keepdims=True))).astype(BF16)


def held_llama_kernel(half, across, first, out):
    x, t, _ = (lax.axis_index(axis) for axis in MESH)
    near = (t >> 1) < 2
    moved = jnp.where(near, first[...], across[...])
    stayed = jnp.where(near, half[...], first[...])
    out[...] = jnp.where(x == 0, stayed, moved)


def settled_kernel(held, diagonal, out):
    t, y = lax.axis_index("tp"), lax.axis_index("dp")
    out[...] = jnp.where(((t >> 1) & 1) == y, held[...], diagonal[...])


def cross_kernel(core, qwen, first, second, *rest):
    out, blocks, sems = rest[-3:]
    core = lax.axis_index("tp") & 1 if core == 0 else 1 - (lax.axis_index("tp") & 1)
    count, rows, _ = blocks.shape

    def copy(i):
        start = pl.multiple_of((core * count + i) * rows, rows)
        return pltpu.make_async_copy(blocks.at[i], out.at[pl.ds(start, rows)], sems.at[i])

    for i in range(count):
        part = slice(i * rows, (i + 1) * rows)
        llama = jnp.concatenate([first[:, part], second[:, part]], axis=0)
        blocks[i] = lax.dot_general(
            llama, qwen[...], (((0,), (0,)), ((), ())), preferred_element_type=F32
        )
        copy(i).start()
    for i in range(count):
        copy(i).wait()


def cross_product(core, qwen, first, second, out=None):
    _, width = qwen.shape
    features = first.shape[1]
    rows = min(256, features)
    steps = features // rows
    hbm = pl.BlockSpec(memory_space=pltpu.HBM)
    extra = [] if out is None else [out]
    return pl.pallas_call(
        functools.partial(cross_kernel, core),
        out_shape=jax.ShapeDtypeStruct((2 * features, width), F32),
        in_specs=[vmem()] * 3 + [hbm] * len(extra),
        out_specs=hbm,
        input_output_aliases={3: 0} if extra else {},
        scratch_shapes=[pltpu.VMEM((steps, rows, width), F32), pltpu.SemaphoreType.DMA((steps,))],
        compiler_params=pltpu.CompilerParams(vmem_limit_bytes=VMEM_LIMIT),
        cost_estimate=slow(),
    )(qwen, first, second, *extra)


def swapped(block, axis, mask):
    count = lax.axis_size(axis)
    return lax.ppermute(block, axis, [(i, i ^ mask) for i in range(count)])


def ordered_call(kernel, shapes, args, after=(), cost=None):
    def body(*refs):
        kernel(*refs[: len(args)], *refs[len(args) + len(after) :])

    return pl.pallas_call(
        body,
        out_shape=tuple(jax.ShapeDtypeStruct(shape, dtype) for shape, dtype in shapes),
        in_specs=[vmem()] * len(args) + [pl.BlockSpec(memory_space=pl.ANY)] * len(after),
        out_specs=tuple(vmem() for _ in shapes),
        compiler_params=pltpu.CompilerParams(vmem_limit_bytes=VMEM_SMALL),
        cost_estimate=cost or slow(),
    )(*args, *after)


def cut_at(rows, cut):
    tokens, width = rows.shape

    def kernel(whole, left, right):
        left[...] = whole[:, :cut]
        right[...] = whole[:, cut:]

    shapes = [((tokens, cut), rows.dtype), ((tokens, width - cut), rows.dtype)]
    return ordered_call(kernel, shapes, [rows], cost=cheap())


def folded(keep, *got, after=()):
    tokens, width = keep.shape
    half = width // 2

    def kernel(*refs):
        *terms, left, right = refs
        left[...] = sum(term[:, :half].astype(F32) for term in terms)
        right[...] = sum(term[:, half:].astype(F32) for term in terms).astype(BF16)

    shapes = [((tokens, half), F32), ((tokens, half), BF16)]
    return ordered_call(kernel, shapes, [keep, *got], after)


def total(keep, got, after=(), cost=None):
    def kernel(own, other, out):
        out[...] = (own[...] + other[...].astype(F32)).astype(BF16)

    return ordered_call(kernel, [(keep.shape, BF16)], [keep, got], after, cost)[0]


def beside(left, right, after=()):
    tokens, width = left.shape

    def kernel(first, second, out):
        out[:, :width] = first[...]
        out[:, width:] = second[...]

    return ordered_call(kernel, [((tokens, 2 * width), left.dtype)], [left, right], after)[0]


def flat(x, t, y):
    return (x * 8 + t) * 2 + y


def route(block, moves):
    return lax.ppermute(block, MESH, [(flat(*a), flat(*b)) for a, b in moves])


def plan():
    across, first, second, neighbour, diagonal = [], [], [], [], []
    for t in range(8):
        z, core = t >> 1, t & 1
        for y in range(2):
            across.append(((1, t, y), (0, t, y)))
            if z >= 2:
                across.append(((0, t, y), (1, t, y)))
                first.append(((0, t, y), (1, t - 4, y)))
                first.append(((1, t, 1 - y), (1, t, y)))
                second.append(((1, t, 1 - y), (0, t, y)))
            else:
                first.append(((0, t, y), (0, t + 4, y)))
                first.append(((1, t, 1 - y), (0, t, y)))
                second.append(((1, t, 1 - y), (1, t, y)))
            for x in range(2):
                if z & 1 == y:
                    neighbour.append(((x, t, y), (x, t ^ 2, y)))
                else:
                    neighbour.append(((x, t, y), (x, t, 1 - y)))
                    diagonal.append(((x, t, y), (x, t ^ 2, 1 - y)))
    return across, first, second, neighbour, diagonal


def pipelined(hidden, down_weight, whitening):
    acts, weights, factor = hidden[0], down_weight[0], whitening[0]
    across, first, second, neighbour, diagonal = plan()

    depth = acts.shape[1]
    pieces = cut_at(acts, depth * 5 // 7 // 256 * 256)
    others = [swapped(piece, "dp", 1) for piece in pieces]
    o_keep, o_pass, o_other, o_give, shift, *held = own_product(*pieces, weights)
    o_give = total(o_pass, swapped(o_give, "tp", 1), cost=cheap())
    o_other = swapped(o_other, "tp", 1)
    start = first_product(others[0], held, after=[o_give])
    o_keep, o_give = folded(o_keep, o_other, swapped(o_give, "tp", 2), after=[start])
    groups = second_product(others[1], held, start, shift, after=[o_give])
    p_keep, p_pass, p_other, p_give = groups
    p_give = total(p_pass, swapped(p_give, "tp", 1))
    p_other = swapped(p_other, "tp", 1)
    held_factor = hold(factor, after=[p_give])
    o_sum = total(o_keep, swapped(o_give, "tp", 4), after=[held_factor])
    p_keep, p_give = folded(p_keep, p_other, swapped(p_give, "tp", 2), after=[o_sum])
    o_sum = beside(o_sum, swapped(o_sum, "tp", 4), after=[p_give])
    p_sum = total(p_keep, swapped(p_give, "tp", 4), after=[o_sum])
    o_sum = beside(o_sum, swapped(o_sum, "tp", 2), after=[p_sum])
    p_sum = beside(p_sum, swapped(p_sum, "tp", 4), after=[o_sum])
    o_white = white_product(o_sum, held_factor, 0, F32, after=[p_sum])
    o_white = white_product(swapped(o_sum, "tp", 1), held_factor, 4, BF16, o_white)
    got = swapped(o_white, "dp", 1)
    p_sum = beside(p_sum, swapped(p_sum, "tp", 2), after=[o_white])
    p_white = white_product(p_sum, held_factor, 0, F32)
    half = white_product(swapped(p_sum, "tp", 1), held_factor, 4, BF16, p_white, got)

    tokens, width = half.shape
    across = route(half, across)
    first = route(half, first)
    second = route(half, second)
    held = ordered_call(held_llama_kernel, [(half.shape, BF16)], [half, across, first])[0]
    beside_it = route(held, neighbour)
    diagonal = route(held, diagonal)
    qwen = ordered_call(
        functools.partial(qwen_kernel, 1.0 / math.sqrt(2 * tokens)),
        [((2 * tokens, width), BF16)],
        [half, across, first, second],
        after=[held],
    )[0]
    other_beside = swapped(beside_it, "tp", 1)
    settled = ordered_call(
        settled_kernel, [(half.shape, BF16)], [held, diagonal], after=[other_beside]
    )[0]
    out = cross_product(0, qwen, settled, beside_it)
    return cross_product(1, qwen, swapped(settled, "tp", 1), other_beside, out)


def general(hidden, down_weight, whitening):
    acts, weights, factor = hidden[0], down_weight[0], whitening[0]
    tokens = lax.all_gather(acts, "dp", axis=0, tiled=True)
    partial = jnp.dot(tokens, weights, preferred_element_type=F32)
    outputs = lax.psum(partial, "tp").astype(BF16).astype(F32)
    centered = (outputs - jnp.mean(outputs, axis=0, keepdims=True)).astype(BF16)
    block = lax.psum_scatter(
        jnp.dot(centered, factor, preferred_element_type=F32),
        "dp",
        scatter_dimension=0,
        tiled=True,
    ).astype(BF16)
    both = lax.all_gather(block, "mp", axis=0)
    qwen = lax.all_gather(both[1], "dp", axis=0, tiled=True)
    llama = lax.all_gather(both[0], "tp", axis=1, tiled=True)
    width = llama.shape[1] // lax.axis_size("mp")
    llama = lax.dynamic_slice_in_dim(llama, lax.axis_index("mp") * width, width, 1)
    llama = lax.all_to_all(llama, "dp", split_axis=1, concat_axis=0, tiled=True)
    cross = lax.dot_general(llama, qwen, (((0,), (0,)), ((), ())), preferred_element_type=F32)
    return cross * (1.0 / math.sqrt(qwen.shape[0]))


def solution(mesh):
    placed = (P("mp", "dp", "tp"), P("mp", "tp", "dp"), P("mp", "dp", "tp"))
    sizes = tuple(mesh.shape[axis] for axis in MESH)
    body = pipelined if sizes == (2, 8, 2) else general
    return jax.shard_map(
        body, mesh=mesh, in_specs=placed, out_specs=P(("mp", "dp"), "tp"), check_vma=False
    )
```

```python
import functools
import math

import jax
import jax.numpy as jnp
from jax import lax
from jax.experimental import pallas as pl
from jax.experimental.pallas import tpu as pltpu
from jax.sharding import PartitionSpec as P

F32 = jnp.float32
BF16 = jnp.bfloat16
VMEM_LIMIT = 8 * 2**20
VMEM_SMALL = 3 * 2**20
MESH = ("mp", "tp", "dp")
GROUPS = ((2, F32), (2, F32), (1, BF16), (1, BF16), (1, BF16), (1, BF16))


def vmem():
    return pl.BlockSpec(memory_space=pltpu.VMEM)


def block_of(t, place):
    return (((t & 1) ^ (place >> 2)) << 2) | (place & 3)


def held_in_vmem(block):
    return pltpu.with_memory_space_constraint(block, pltpu.VMEM)


def left_in_hbm(block):
    return pltpu.with_memory_space_constraint(block, pltpu.HBM)


def columns(i, width):
    return pl.ds(pl.multiple_of(i * width, width), width)


def each_group(groups, held_keep, held_send, product):
    half, _, width = held_keep.shape
    first, second, *single = groups

    @pl.loop(0, half // 2)
    def _(i):
        first[:, columns(i, width)] = product(held_keep, 0, i)

    @pl.loop(0, half // 2)
    def _(i):
        second[:, columns(i, width)] = product(held_keep, 0, half // 2 + i)

    @pl.loop(0, half)
    def _(i):
        block = product(held_send, half, i).astype(BF16)
        for number, group in enumerate(single):

            @pl.when(i == number)
            def _(group=group):
                group[...] = block


def own_kernel(left, right, weights, *rest):
    *groups, shift, held_keep, held_send, sems = rest
    t = lax.axis_index("tp")
    half, depth, width = held_keep.shape
    count = 2 * half
    cut = left.shape[1]

    def copy(held, base, i, k):
        part = pl.ds(0, cut) if k == 0 else pl.ds(cut, depth - cut)
        source = weights.at[part, columns(block_of(t, base + i), width)]
        return pltpu.make_async_copy(source, held.at[i, part], sems.at[base + i, k])

    for held, base in ((held_keep, 0), (held_send, half)):
        for i in range(half):
            for k in range(2):
                copy(held, base, i, k).start()

    def product(held, base, i):
        copy(held, base, i, 0).wait()
        total = jnp.dot(left[...], held[i, :cut], preferred_element_type=F32)
        copy(held, base, i, 1).wait()
        total += jnp.dot(right[...], held[i, cut:], preferred_element_type=F32)
        mean = jnp.mean(total, axis=0, keepdims=True)
        shift[:, columns(base + i, width)] = mean
        return total - mean

    each_group(groups, held_keep, held_send, product)


def own_product(left, right, weights):
    tokens = left.shape[0]
    depth = weights.shape[0]
    width = weights.shape[1] // 8
    return pl.pallas_call(
        own_kernel,
        out_shape=(
            *[jax.ShapeDtypeStruct((tokens, count * width), dtype) for count, dtype in GROUPS],
            jax.ShapeDtypeStruct((1, 8 * width), F32),
            pltpu.VMEM((4, depth, width), BF16),
            pltpu.VMEM((4, depth, width), BF16),
        ),
        in_specs=[vmem(), vmem(), pl.BlockSpec(memory_space=pltpu.HBM)],
        out_specs=(vmem(),) * (len(GROUPS) + 3),
        scratch_shapes=[pltpu.SemaphoreType.DMA((8, 2))],
        compiler_params=pltpu.CompilerParams(vmem_limit_bytes=VMEM_SMALL),
        cost_estimate=cheap(),
    )(left, right, left_in_hbm(weights))


def first_kernel(rows, held_keep, held_send, out):
    half, _, width = held_keep.shape
    depth = rows.shape[1]
    for held, base in ((held_keep, 0), (held_send, half)):

        @pl.loop(0, half)
        def _(i, held=held, base=base):
            out[:, columns(base + i, width)] = jnp.dot(
                rows[...], held[i, :depth], preferred_element_type=F32
            )


def first_product(order, rows, held):
    shape = (rows.shape[0], 8 * held[0].shape[2])
    return order(first_kernel, [(shape, F32)], rows, *map(held_in_vmem, held))


def second_kernel(rows, held_keep, held_send, start, shift, *groups):
    _, depth, width = held_keep.shape
    cut = depth - rows.shape[1]

    def product(held, base, i):
        total = jnp.dot(rows[...], held[i, cut:], preferred_element_type=F32)
        return total + start[:, columns(base + i, width)] - shift[:, columns(base + i, width)]

    each_group(groups, held_keep, held_send, product)


def second_product(order, rows, held, start, shift):
    tokens, width = rows.shape[0], held[0].shape[2]
    shapes = [((tokens, count * width), dtype) for count, dtype in GROUPS]
    return order(second_kernel, shapes, rows, *map(held_in_vmem, held), start, shift)


def hold_kernel(factor, *rest):
    held, sems = rest[-2:]
    t = lax.axis_index("tp")
    count, rows, _ = held.shape

    def copy(i):
        start = pl.multiple_of(block_of(t, i) * rows, rows)
        return pltpu.make_async_copy(factor.at[pl.ds(start, rows)], held.at[i], sems.at[i])

    for i in range(count):
        copy(i).start()
    for i in range(count):
        copy(i).wait()


def hold(order, factor):
    deep, wide = factor.shape
    held = pl.pallas_call(
        hold_kernel,
        out_shape=pltpu.VMEM((8, deep // 8, wide), BF16),
        in_specs=[pl.BlockSpec(memory_space=pltpu.HBM)]
        + [pl.BlockSpec(memory_space=pl.ANY)] * len(order.last),
        out_specs=vmem(),
        scratch_shapes=[pltpu.SemaphoreType.DMA((8,))],
        compiler_params=pltpu.CompilerParams(vmem_limit_bytes=VMEM_SMALL),
        cost_estimate=cheap(),
    )(left_in_hbm(factor), *order.last)
    order.last = [held]
    return held


def white_kernel(places, *refs):
    parts = refs[: len(places)]
    factor, *terms, out = refs[len(places) :]
    sums = [term[...].astype(F32) for term in terms]
    for rows, place in zip(parts, places):
        sums.append(jnp.dot(rows[...], factor[place], preferred_element_type=F32))
    out[...] = sum(sums[1:], sums[0]).astype(out.dtype)


def white_product(order, dtype, factor, first, parts, *terms):
    kernel = functools.partial(white_kernel, range(first, first + len(parts)))
    shape = (parts[0].shape[0], factor.shape[2])
    return order(kernel, [(shape, dtype)], *parts, held_in_vmem(factor), *terms)


def cheap():
    return pl.CostEstimate(flops=1024, bytes_accessed=1024, transcendentals=0)


def slow():
    return pl.CostEstimate(flops=10**10, bytes_accessed=10**9, transcendentals=0)


def qwen_kernel(scale, half, across, first, second, out):
    x, t, y = (lax.axis_index(axis) for axis in MESH)
    z = t >> 1
    llama_side, near = x == 0, z < 2
    other = jnp.where(llama_side, across[...], half[...])
    own = jnp.where(llama_side == near, first[...], second[...])
    flip = (z & 1) == y
    top, bottom = jnp.where(flip, other, own), jnp.where(flip, own, other)
    wide = jnp.concatenate([top, bottom], axis=0).astype(F32)
    out[...] = (scale * (wide - jnp.mean(wide, axis=0, keepdims=True))).astype(BF16)


def held_llama_kernel(half, across, first, left, right):
    x, t, _ = (lax.axis_index(axis) for axis in MESH)
    near = (t >> 1) < 2
    moved = jnp.where(near, first[...], across[...])
    stayed = jnp.where(near, half[...], first[...])
    held = jnp.where(x == 0, stayed, moved)
    width = left.shape[1]
    left[...] = held[:, :width]
    right[...] = held[:, width:]


def settled_kernel(held, diagonal, out):
    t, y = lax.axis_index("tp"), lax.axis_index("dp")
    out[...] = jnp.where(((t >> 1) & 1) == y, held[...], diagonal[...])


def cross_kernel(core, pieces, qwen, *rest):
    llama, (out, blocks, sems) = rest[: 2 * pieces], rest[-3:]
    core = lax.axis_index("tp") & 1 if core == 0 else 1 - (lax.axis_index("tp") & 1)
    count, rows, _ = blocks.shape
    each = count // pieces

    def copy(i):
        start = pl.multiple_of((core * count + i) * rows, rows)
        return pltpu.make_async_copy(blocks.at[i], out.at[pl.ds(start, rows)], sems.at[i])

    for i in range(count):
        part = slice(i % each * rows, (i % each + 1) * rows)
        halves = [llama[2 * (i // each) + token_half][:, part] for token_half in range(2)]
        blocks[i] = lax.dot_general(
            jnp.concatenate(halves, axis=0),
            qwen[...],
            (((0,), (0,)), ((), ())),
            preferred_element_type=F32,
        )
        copy(i).start()
    for i in range(count):
        copy(i).wait()


def cross_product(core, qwen, settled, beside, out=None):
    width = qwen.shape[1]
    piece = settled[0].shape[1]
    features = len(settled) * piece
    rows = min(256, piece)
    steps = features // rows
    llama = [half for pair in zip(settled, beside) for half in pair]
    hbm = pl.BlockSpec(memory_space=pltpu.HBM)
    extra = [] if out is None else [out]
    return pl.pallas_call(
        functools.partial(cross_kernel, core, len(settled)),
        out_shape=jax.ShapeDtypeStruct((2 * features, width), F32),
        in_specs=[vmem()] * (1 + len(llama)) + [hbm] * len(extra),
        out_specs=hbm,
        input_output_aliases={1 + len(llama): 0} if extra else {},
        scratch_shapes=[pltpu.VMEM((steps, rows, width), F32), pltpu.SemaphoreType.DMA((steps,))],
        compiler_params=pltpu.CompilerParams(vmem_limit_bytes=VMEM_LIMIT),
        cost_estimate=slow(),
    )(qwen, *llama, *extra)


def swapped(block, axis, mask):
    count = lax.axis_size(axis)
    return lax.ppermute(block, axis, [(i, i ^ mask) for i in range(count)])


class Order:
    def __init__(self):
        self.last = []

    def __call__(self, kernel, shapes, *args):
        count, after = len(args), self.last

        def body(*refs):
            kernel(*refs[:count], *refs[count + len(after) :])

        results = pl.pallas_call(
            body,
            out_shape=tuple(jax.ShapeDtypeStruct(shape, dtype) for shape, dtype in shapes),
            in_specs=[vmem()] * count + [pl.BlockSpec(memory_space=pl.ANY)] * len(after),
            out_specs=tuple(vmem() for _ in shapes),
            compiler_params=pltpu.CompilerParams(vmem_limit_bytes=VMEM_SMALL),
            cost_estimate=cheap(),
        )(*args, *after)
        self.last = [results[-1]]
        return results if len(shapes) > 1 else results[0]


def cut_at(order, rows, cut):
    tokens, width = rows.shape

    def kernel(whole, left, right):
        left[...] = whole[:, :cut]
        right[...] = whole[:, cut:]

    shapes = [((tokens, cut), rows.dtype), ((tokens, width - cut), rows.dtype)]
    return order(kernel, shapes, rows)


def added(order, own, *got):
    width = got[0].shape[1]

    def kernel(first, *rest):
        *parts, wide, narrow = rest
        for i, part in enumerate(parts):
            at = slice(i * width, (i + 1) * width)
            wide[:, at] = first[:, at] + part[...].astype(F32)
            narrow[:, at] = wide[:, at].astype(BF16)

    return order(kernel, [(own.shape, F32), (own.shape, BF16)], own, *got)


def total(order, own, got):
    def kernel(first, second, out):
        out[...] = (first[...] + second[...].astype(F32)).astype(BF16)

    return order(kernel, [(own.shape, BF16)], own, got)


def at_ends(order, middle, end):
    tokens, width = middle.shape
    half = width // 2

    def kernel(first, second, left, right):
        z = lax.axis_index("tp") >> 1
        both = jnp.where((z == 1) | (z == 2), first[...], second[...])
        left[...] = both[:, :half]
        right[...] = both[:, half:]

    return order(kernel, [((tokens, half), BF16)] * 2, middle, end)


def cores_swapped(pieces):
    return [swapped(piece, "tp", 1) for piece in pieces]


def along_z(block, moves):
    pairs = [(2 * a + core, 2 * b + core) for a, b in moves for core in range(2)]
    return lax.ppermute(block, "tp", pairs)


def inward(block):
    return along_z(block, [(0, 1), (3, 2)])


def midway(block):
    return along_z(block, [(1, 2), (2, 1)])


def outward(block):
    return along_z(block, [(1, 0), (2, 3)])


def flat(x, t, y):
    return (x * 8 + t) * 2 + y


def route(block, moves):
    return lax.ppermute(block, MESH, [(flat(*a), flat(*b)) for a, b in moves])


def plan():
    across, first, second, neighbour, diagonal = [], [], [], [], []
    for t in range(8):
        z, core = t >> 1, t & 1
        for y in range(2):
            across.append(((1, t, y), (0, t, y)))
            if z >= 2:
                across.append(((0, t, y), (1, t, y)))
                first.append(((0, t, y), (1, t - 4, y)))
                first.append(((1, t, 1 - y), (1, t, y)))
                second.append(((1, t, 1 - y), (0, t, y)))
            else:
                first.append(((0, t, y), (0, t + 4, y)))
                first.append(((1, t, 1 - y), (0, t, y)))
                second.append(((1, t, 1 - y), (1, t, y)))
            for x in range(2):
                if z & 1 == y:
                    neighbour.append(((x, t, y), (x, t ^ 2, y)))
                else:
                    neighbour.append(((x, t, y), (x, t, 1 - y)))
                    diagonal.append(((x, t, y), (x, t ^ 2, 1 - y)))
    return across, first, second, neighbour, diagonal


def pipelined(hidden, down_weight, whitening):
    acts, weights, factor = hidden[0], down_weight[0], whitening[0]
    across, first, second, neighbour, diagonal = plan()

    order = Order()

    depth = acts.shape[1]
    pieces = cut_at(order, acts, depth * 5 // 7 // 256 * 256)
    p_rows = [swapped(piece, "dp", 1) for piece in pieces]
    oa, ob, *other, shift, held_keep, held_send = own_product(*pieces, weights)
    order.last = [shift]
    held = held_keep, held_send
    other = cores_swapped(other)
    oa, oa_in = added(order, oa, *other[:2])
    ob, ob_in = added(order, ob, *other[2:])
    start = first_product(order, p_rows[0], held)
    oa, oa_mid = added(order, oa, inward(oa_in))
    pa, pb, *other = second_product(order, p_rows[1], held, start, shift)
    other = cores_swapped(other)
    ob, ob_mid = added(order, ob, inward(ob_in))
    pa, pa_in = added(order, pa, *other[:2])
    pb, pb_in = added(order, pb, *other[2:])
    oa = total(order, oa, midway(oa_mid))
    factor = hold(order, factor)
    ob = total(order, ob, midway(ob_mid))
    pa, pa_mid = added(order, pa, inward(pa_in))
    oa = at_ends(order, oa, outward(oa))
    pb, pb_mid = added(order, pb, inward(pb_in))
    ob = at_ends(order, ob, outward(ob))
    pa = total(order, pa, midway(pa_mid))
    o_sums = [*oa, *ob]
    o_white = white_product(order, BF16, factor, 0, o_sums + cores_swapped(o_sums))
    pb = total(order, pb, midway(pb_mid))
    pa = at_ends(order, pa, outward(pa))
    half = white_product(order, F32, factor, 0, pa, swapped(o_white, "dp", 1))
    pb = at_ends(order, pb, outward(pb))
    half = white_product(order, F32, factor, 2, pb, half)
    half = white_product(order, F32, factor, 4, cores_swapped(pa), half)
    half = white_product(order, BF16, factor, 6, cores_swapped(pb), half)

    tokens, width = half.shape
    first = route(half, first)
    across = route(half, across)
    second = route(half, second)
    piece = ((tokens, width // 2), BF16)
    held = order(held_llama_kernel, [piece, piece], half, across, first)
    beside = [route(block, neighbour) for block in held]
    diagonal = [route(block, diagonal) for block in held]
    centre = functools.partial(qwen_kernel, 1.0 / math.sqrt(2 * tokens))
    qwen = order(centre, [((2 * tokens, width), BF16)], half, across, first, second)
    other_beside = cores_swapped(beside)
    settled = []
    for kept, moved, other in zip(held, diagonal, other_beside):
        order.last.append(other)
        settled.append(order(settled_kernel, [piece], kept, moved))
    out = cross_product(0, qwen, settled, beside)
    return cross_product(1, qwen, cores_swapped(settled), other_beside, out)


def general(hidden, down_weight, whitening):
    acts, weights, factor = hidden[0], down_weight[0], whitening[0]
    tokens = lax.all_gather(acts, "dp", axis=0, tiled=True)
    partial = jnp.dot(tokens, weights, preferred_element_type=F32)
    outputs = lax.psum(partial, "tp").astype(BF16).astype(F32)
    centered = (outputs - jnp.mean(outputs, axis=0, keepdims=True)).astype(BF16)
    block = lax.psum_scatter(
        jnp.dot(centered, factor, preferred_element_type=F32),
        "dp",
        scatter_dimension=0,
        tiled=True,
    ).astype(BF16)
    both = lax.all_gather(block, "mp", axis=0)
    qwen = lax.all_gather(both[1], "dp", axis=0, tiled=True)
    llama = lax.all_gather(both[0], "tp", axis=1, tiled=True)
    width = llama.shape[1] // lax.axis_size("mp")
    llama = lax.dynamic_slice_in_dim(llama, lax.axis_index("mp") * width, width, 1)
    llama = lax.all_to_all(llama, "dp", split_axis=1, concat_axis=0, tiled=True)
    cross = lax.dot_general(llama, qwen, (((0,), (0,)), ((), ())), preferred_element_type=F32)
    return cross * (1.0 / math.sqrt(qwen.shape[0]))


def solution(mesh):
    placed = (P("mp", "dp", "tp"), P("mp", "tp", "dp"), P("mp", "dp", "tp"))
    sizes = tuple(mesh.shape[axis] for axis in MESH)
    body = pipelined if sizes == (2, 8, 2) else general
    return jax.shard_map(
        body, mesh=mesh, in_specs=placed, out_specs=P(("mp", "dp"), "tp"), check_vma=False
    )
```

```python
import functools
import math

import jax
import jax.numpy as jnp
from jax import lax
from jax.experimental import pallas as pl
from jax.experimental.pallas import tpu as pltpu
from jax.sharding import PartitionSpec as P

F32 = jnp.float32
BF16 = jnp.bfloat16
VMEM_LIMIT = 8 * 2**20
VMEM_SMALL = 4 * 2**20
MESH = ("mp", "tp", "dp")
GROUP_TYPES = (F32, F32, BF16, BF16)


def vmem():
    return pl.BlockSpec(memory_space=pltpu.VMEM)


def block_of(t, place):
    return t ^ (((place & 1) << 2) | (place & 2) | (place >> 2))


def held_in_vmem(block):
    return pltpu.with_memory_space_constraint(block, pltpu.VMEM)


def left_in_hbm(block):
    return pltpu.with_memory_space_constraint(block, pltpu.HBM)


def columns(i, width):
    return pl.ds(pl.multiple_of(i * width, width), width)


def each_group(groups, held_keep, held_send, product):
    half, _, width = held_keep.shape
    for number, group in enumerate(groups):
        held, base = (held_keep, 0) if number < 2 else (held_send, half)
        first = number % 2 * 2

        @pl.loop(0, 2)
        def _(i, held=held, base=base, first=first, group=group):
            group[:, columns(i, width)] = product(held, base, first + i).astype(group.dtype)


def own_kernel(left, right, weights, *rest):
    *groups, shift, held_keep, held_send, sems = rest
    t = lax.axis_index("tp")
    half, depth, width = held_keep.shape
    count = 2 * half
    cut = left.shape[1]

    def copy(held, base, i, k):
        part = pl.ds(0, cut) if k == 0 else pl.ds(cut, depth - cut)
        source = weights.at[part, columns(block_of(t, base + i), width)]
        return pltpu.make_async_copy(source, held.at[i, part], sems.at[base + i, k])

    for held, base in ((held_keep, 0), (held_send, half)):
        for i in range(half):
            for k in range(2):
                copy(held, base, i, k).start()

    def product(held, base, i):
        copy(held, base, i, 0).wait()
        total = jnp.dot(left[...], held[i, :cut], preferred_element_type=F32)
        copy(held, base, i, 1).wait()
        total += jnp.dot(right[...], held[i, cut:], preferred_element_type=F32)
        mean = jnp.mean(total, axis=0, keepdims=True)
        shift[:, columns(base + i, width)] = mean
        return total - mean

    each_group(groups, held_keep, held_send, product)


def own_product(left, right, weights):
    tokens = left.shape[0]
    depth = weights.shape[0]
    width = weights.shape[1] // 8
    return pl.pallas_call(
        own_kernel,
        out_shape=(
            *[jax.ShapeDtypeStruct((tokens, 2 * width), dtype) for dtype in GROUP_TYPES],
            jax.ShapeDtypeStruct((1, 8 * width), F32),
            pltpu.VMEM((4, depth, width), BF16),
            pltpu.VMEM((4, depth, width), BF16),
        ),
        in_specs=[vmem(), vmem(), pl.BlockSpec(memory_space=pltpu.HBM)],
        out_specs=(vmem(),) * 7,
        scratch_shapes=[pltpu.SemaphoreType.DMA((8, 2))],
        compiler_params=pltpu.CompilerParams(vmem_limit_bytes=VMEM_SMALL),
        cost_estimate=cheap(),
    )(left, right, left_in_hbm(weights))


def first_kernel(rows, held_keep, held_send, out):
    half, _, width = held_keep.shape
    depth = rows.shape[1]
    for held, base in ((held_keep, 0), (held_send, half)):

        @pl.loop(0, half)
        def _(i, held=held, base=base):
            out[:, columns(base + i, width)] = jnp.dot(
                rows[...], held[i, :depth], preferred_element_type=F32
            )


def first_product(rows, held, after=()):
    shape = (rows.shape[0], 8 * held[0].shape[2])
    args = [rows, *map(held_in_vmem, held)]
    return ordered_call(first_kernel, [(shape, F32)], args, after, cheap())[0]


def second_kernel(rows, held_keep, held_send, start, shift, *groups):
    _, depth, width = held_keep.shape
    cut = depth - rows.shape[1]

    def product(held, base, i):
        total = jnp.dot(rows[...], held[i, cut:], preferred_element_type=F32)
        return total + start[:, columns(base + i, width)] - shift[:, columns(base + i, width)]

    each_group(groups, held_keep, held_send, product)


def second_product(rows, held, start, shift, after=()):
    tokens = rows.shape[0]
    held_keep, held_send = held
    wide = 2 * held_keep.shape[2]
    return ordered_call(
        second_kernel,
        [((tokens, wide), dtype) for dtype in GROUP_TYPES],
        [rows, held_in_vmem(held_keep), held_in_vmem(held_send), start, shift],
        after,
    )


def hold_kernel(factor, *rest):
    held, sems = rest[-2:]
    t = lax.axis_index("tp")
    count, rows, _ = held.shape

    def copy(i):
        start = pl.multiple_of(block_of(t, i) * rows, rows)
        return pltpu.make_async_copy(factor.at[pl.ds(start, rows)], held.at[i], sems.at[i])

    for i in range(count):
        copy(i).start()
    for i in range(count):
        copy(i).wait()


def hold(factor, after):
    deep, wide = factor.shape
    return pl.pallas_call(
        hold_kernel,
        out_shape=pltpu.VMEM((8, deep // 8, wide), BF16),
        in_specs=[pl.BlockSpec(memory_space=pltpu.HBM)]
        + [pl.BlockSpec(memory_space=pl.ANY)] * len(after),
        out_specs=vmem(),
        scratch_shapes=[pltpu.SemaphoreType.DMA((8,))],
        compiler_params=pltpu.CompilerParams(vmem_limit_bytes=VMEM_SMALL),
        cost_estimate=cheap(),
    )(left_in_hbm(factor), *after)


def white_kernel(base, rows, factor, *rest):
    *terms, out = rest
    count, depth = 4, factor.shape[1]
    total = None
    for i in range(count):
        part = jnp.dot(
            rows[:, i * depth : (i + 1) * depth], factor[base + i], preferred_element_type=F32
        )
        total = part if total is None else total + part
    for term in terms:
        total += term[...].astype(F32)
    out[...] = total.astype(out.dtype)


def white_product(rows, factor, base, dtype, *terms, after=()):
    shape = (rows.shape[0], factor.shape[2])
    args = [rows, held_in_vmem(factor), *terms]
    return ordered_call(functools.partial(white_kernel, base), [(shape, dtype)], args, after)[0]


def cheap():
    return pl.CostEstimate(flops=1024, bytes_accessed=1024, transcendentals=0)


def slow():
    return pl.CostEstimate(flops=10**10, bytes_accessed=10**9, transcendentals=0)


def qwen_kernel(scale, second, across, first, half, out):
    x, t, y = (lax.axis_index(axis) for axis in MESH)
    z = t >> 1
    llama_side, near = x == 0, z < 2
    other = jnp.where(llama_side, across[...], half[...])
    own = jnp.where(llama_side == near, first[...], second[...])
    flip = (z & 1) == y
    top, bottom = jnp.where(flip, other, own), jnp.where(flip, own, other)
    wide = jnp.concatenate([top, bottom], axis=0).astype(F32)
    out[...] = (scale * (wide - jnp.mean(wide, axis=0, keepdims=True))).astype(BF16)


def held_llama_kernel(half, across, first, out):
    x, t, _ = (lax.axis_index(axis) for axis in MESH)
    near = (t >> 1) < 2
    moved = jnp.where(near, first[...], across[...])
    stayed = jnp.where(near, half[...], first[...])
    out[...] = jnp.where(x == 0, stayed, moved)


def settled_kernel(held, diagonal, out):
    t, y = lax.axis_index("tp"), lax.axis_index("dp")
    out[...] = jnp.where(((t >> 1) & 1) == y, held[...], diagonal[...])


def cross_kernel(core, qwen, first, second, *rest):
    out, blocks, sems = rest[-3:]
    core = lax.axis_index("tp") & 1 if core == 0 else 1 - (lax.axis_index("tp") & 1)
    count, rows, _ = blocks.shape

    def copy(i):
        start = pl.multiple_of((core * count + i) * rows, rows)
        return pltpu.make_async_copy(blocks.at[i], out.at[pl.ds(start, rows)], sems.at[i])

    for i in range(count):
        part = slice(i * rows, (i + 1) * rows)
        llama = jnp.concatenate([first[:, part], second[:, part]], axis=0)
        blocks[i] = lax.dot_general(
            llama, qwen[...], (((0,), (0,)), ((), ())), preferred_element_type=F32
        )
        copy(i).start()
    for i in range(count):
        copy(i).wait()


def cross_product(core, qwen, first, second, out=None):
    _, width = qwen.shape
    features = first.shape[1]
    rows = min(256, features)
    steps = features // rows
    hbm = pl.BlockSpec(memory_space=pltpu.HBM)
    extra = [] if out is None else [out]
    return pl.pallas_call(
        functools.partial(cross_kernel, core),
        out_shape=jax.ShapeDtypeStruct((2 * features, width), F32),
        in_specs=[vmem()] * 3 + [hbm] * len(extra),
        out_specs=hbm,
        input_output_aliases={3: 0} if extra else {},
        scratch_shapes=[pltpu.VMEM((steps, rows, width), F32), pltpu.SemaphoreType.DMA((steps,))],
        compiler_params=pltpu.CompilerParams(vmem_limit_bytes=VMEM_LIMIT),
        cost_estimate=slow(),
    )(qwen, first, second, *extra)


def swapped(block, axis, mask):
    count = lax.axis_size(axis)
    return lax.ppermute(block, axis, [(i, i ^ mask) for i in range(count)])


def ordered_call(kernel, shapes, args, after=(), cost=None):
    def body(*refs):
        kernel(*refs[: len(args)], *refs[len(args) + len(after) :])

    return pl.pallas_call(
        body,
        out_shape=tuple(jax.ShapeDtypeStruct(shape, dtype) for shape, dtype in shapes),
        in_specs=[vmem()] * len(args) + [pl.BlockSpec(memory_space=pl.ANY)] * len(after),
        out_specs=tuple(vmem() for _ in shapes),
        compiler_params=pltpu.CompilerParams(vmem_limit_bytes=VMEM_SMALL),
        cost_estimate=cost or slow(),
    )(*args, *after)


def cut_at(rows, cut):
    tokens, width = rows.shape

    def kernel(whole, left, right):
        left[...] = whole[:, :cut]
        right[...] = whole[:, cut:]

    shapes = [((tokens, cut), rows.dtype), ((tokens, width - cut), rows.dtype)]
    return ordered_call(kernel, shapes, [rows], cost=cheap())


def folded(keep, *got, after=()):
    tokens, width = keep.shape
    half = width // 2

    def kernel(*refs):
        *terms, left, right = refs
        left[...] = sum(term[:, :half].astype(F32) for term in terms)
        right[...] = sum(term[:, half:].astype(F32) for term in terms).astype(BF16)

    shapes = [((tokens, half), F32), ((tokens, half), BF16)]
    return ordered_call(kernel, shapes, [keep, *got], after)


def total(keep, got, after=(), cost=None):
    def kernel(own, other, out):
        out[...] = (own[...] + other[...].astype(F32)).astype(BF16)

    return ordered_call(kernel, [(keep.shape, BF16)], [keep, got], after, cost)[0]


def beside(left, right, after=()):
    tokens, width = left.shape

    def kernel(first, second, out):
        out[:, :width] = first[...]
        out[:, width:] = second[...]

    return ordered_call(kernel, [((tokens, 2 * width), left.dtype)], [left, right], after)[0]


def flat(x, t, y):
    return (x * 8 + t) * 2 + y


def route(block, moves):
    return lax.ppermute(block, MESH, [(flat(*a), flat(*b)) for a, b in moves])


def plan():
    across, first, second, neighbour, diagonal = [], [], [], [], []
    for t in range(8):
        z, core = t >> 1, t & 1
        for y in range(2):
            across.append(((1, t, y), (0, t, y)))
            if z >= 2:
                across.append(((0, t, y), (1, t, y)))
                first.append(((0, t, y), (1, t - 4, y)))
                first.append(((1, t, 1 - y), (1, t, y)))
                second.append(((1, t, 1 - y), (0, t, y)))
            else:
                first.append(((0, t, y), (0, t + 4, y)))
                first.append(((1, t, 1 - y), (0, t, y)))
                second.append(((1, t, 1 - y), (1, t, y)))
            for x in range(2):
                if z & 1 == y:
                    neighbour.append(((x, t, y), (x, t ^ 2, y)))
                else:
                    neighbour.append(((x, t, y), (x, t, 1 - y)))
                    diagonal.append(((x, t, y), (x, t ^ 2, 1 - y)))
    return across, first, second, neighbour, diagonal


def pipelined(hidden, down_weight, whitening):
    acts, weights, factor = hidden[0], down_weight[0], whitening[0]
    across, first, second, neighbour, diagonal = plan()

    depth = acts.shape[1]
    pieces = cut_at(acts, depth * 5 // 7 // 256 * 256)
    others = [swapped(piece, "dp", 1) for piece in pieces]
    o_keep, o_pass, o_other, o_give, shift, *held = own_product(*pieces, weights)
    o_give = total(o_pass, swapped(o_give, "tp", 1), cost=cheap())
    o_other = swapped(o_other, "tp", 1)
    start = first_product(others[0], held, after=[o_give])
    o_keep, o_give = folded(o_keep, o_other, swapped(o_give, "tp", 2), after=[start])
    groups = second_product(others[1], held, start, shift, after=[o_give])
    p_keep, p_pass, p_other, p_give = groups
    p_give = total(p_pass, swapped(p_give, "tp", 1))
    p_other = swapped(p_other, "tp", 1)
    held_factor = hold(factor, after=[p_give])
    o_sum = total(o_keep, swapped(o_give, "tp", 4), after=[held_factor])
    p_keep, p_give = folded(p_keep, p_other, swapped(p_give, "tp", 2), after=[o_sum])
    o_sum = beside(o_sum, swapped(o_sum, "tp", 4), after=[p_give])
    p_sum = total(p_keep, swapped(p_give, "tp", 4), after=[o_sum])
    o_sum = beside(o_sum, swapped(o_sum, "tp", 2), after=[p_sum])
    p_sum = beside(p_sum, swapped(p_sum, "tp", 4), after=[o_sum])
    o_white = white_product(o_sum, held_factor, 0, F32, after=[p_sum])
    o_white = white_product(swapped(o_sum, "tp", 1), held_factor, 4, BF16, o_white)
    got = swapped(o_white, "dp", 1)
    p_sum = beside(p_sum, swapped(p_sum, "tp", 2), after=[o_white])
    p_white = white_product(p_sum, held_factor, 0, F32)
    half = white_product(swapped(p_sum, "tp", 1), held_factor, 4, BF16, p_white, got)

    tokens, width = half.shape
    across = route(half, across)
    first = route(half, first)
    second = route(half, second)
    qwen = ordered_call(
        functools.partial(qwen_kernel, 1.0 / math.sqrt(2 * tokens)),
        [((2 * tokens, width), BF16)],
        [second, across, first, half],
    )[0]
    held = ordered_call(
        held_llama_kernel, [(half.shape, BF16)], [half, across, first], after=[qwen]
    )[0]
    beside_it = route(held, neighbour)
    diagonal = route(held, diagonal)
    other_beside = swapped(beside_it, "tp", 1)
    settled = ordered_call(
        settled_kernel, [(half.shape, BF16)], [held, diagonal], after=[other_beside]
    )[0]
    out = cross_product(0, qwen, settled, beside_it)
    return cross_product(1, qwen, swapped(settled, "tp", 1), other_beside, out)


def general(hidden, down_weight, whitening):
    acts, weights, factor = hidden[0], down_weight[0], whitening[0]
    tokens = lax.all_gather(acts, "dp", axis=0, tiled=True)
    partial = jnp.dot(tokens, weights, preferred_element_type=F32)
    outputs = lax.psum(partial, "tp").astype(BF16).astype(F32)
    centered = (outputs - jnp.mean(outputs, axis=0, keepdims=True)).astype(BF16)
    block = lax.psum_scatter(
        jnp.dot(centered, factor, preferred_element_type=F32),
        "dp",
        scatter_dimension=0,
        tiled=True,
    ).astype(BF16)
    both = lax.all_gather(block, "mp", axis=0)
    qwen = lax.all_gather(both[1], "dp", axis=0, tiled=True)
    llama = lax.all_gather(both[0], "tp", axis=1, tiled=True)
    width = llama.shape[1] // lax.axis_size("mp")
    llama = lax.dynamic_slice_in_dim(llama, lax.axis_index("mp") * width, width, 1)
    llama = lax.all_to_all(llama, "dp", split_axis=1, concat_axis=0, tiled=True)
    cross = lax.dot_general(llama, qwen, (((0,), (0,)), ((), ())), preferred_element_type=F32)
    return cross * (1.0 / math.sqrt(qwen.shape[0]))


def solution(mesh):
    placed = (P("mp", "dp", "tp"), P("mp", "tp", "dp"), P("mp", "dp", "tp"))
    sizes = tuple(mesh.shape[axis] for axis in MESH)
    body = pipelined if sizes == (2, 8, 2) else general
    return jax.shard_map(
        body, mesh=mesh, in_specs=placed, out_specs=P(("mp", "dp"), "tp"), check_vma=False
    )
```

```python
import functools
import math

import jax
import jax.numpy as jnp
from jax import lax
from jax.experimental import pallas as pl
from jax.experimental.pallas import tpu as pltpu
from jax.sharding import PartitionSpec as P

F32 = jnp.float32
BF16 = jnp.bfloat16
VMEM_LIMIT = 8 * 2**20
VMEM_SMALL = 4 * 2**20
MESH = ("mp", "tp", "dp")
CUT = (6, 7)
GROUPS = ((2, F32), (2, F32), (2, BF16), (1, BF16), (1, BF16))


def vmem():
    return pl.BlockSpec(memory_space=pltpu.VMEM)


def block_of(t, place):
    core, z = (t & 1) ^ (place >> 2), ((t >> 1) & 1) ^ ((place >> 1) & 1)
    return core << 2 | z << 1 | (place & 1)


def held_in_vmem(block):
    return pltpu.with_memory_space_constraint(block, pltpu.VMEM)


def left_in_hbm(block):
    return pltpu.with_memory_space_constraint(block, pltpu.HBM)


def columns(i, width):
    return pl.ds(pl.multiple_of(i * width, width), width)


def each_group(groups, held_keep, held_send, product):
    half, _, width = held_keep.shape
    *pairs, last, end = groups
    for number, group in enumerate(pairs):
        held, base = (held_keep, 0) if number < 2 else (held_send, half)

        @pl.loop(0, 2)
        def _(i, held=held, base=base, first=number % 2 * 2, group=group):
            group[:, columns(i, width)] = product(held, base, first + i).astype(group.dtype)

    @pl.loop(0, 2)
    def _(i):
        block = product(held_send, half, 2 + i).astype(BF16)
        for number, group in enumerate((last, end)):

            @pl.when(i == number)
            def _(group=group):
                group[...] = block


def own_kernel(left, right, weights, *rest):
    *groups, shift, held_keep, held_send, sems = rest
    t = lax.axis_index("tp")
    half, depth, width = held_keep.shape
    count = 2 * half
    cut = left.shape[1]

    def copy(held, base, i, k):
        part = pl.ds(0, cut) if k == 0 else pl.ds(cut, depth - cut)
        source = weights.at[part, columns(block_of(t, base + i), width)]
        return pltpu.make_async_copy(source, held.at[i, part], sems.at[base + i, k])

    for held, base in ((held_keep, 0), (held_send, half)):
        for i in range(half):
            for k in range(2):
                copy(held, base, i, k).start()

    def product(held, base, i):
        copy(held, base, i, 0).wait()
        total = jnp.dot(left[...], held[i, :cut], preferred_element_type=F32)
        copy(held, base, i, 1).wait()
        total += jnp.dot(right[...], held[i, cut:], preferred_element_type=F32)
        mean = jnp.mean(total, axis=0, keepdims=True)
        shift[:, columns(base + i, width)] = mean
        return total - mean

    each_group(groups, held_keep, held_send, product)


def own_product(left, right, weights):
    tokens = left.shape[0]
    depth = weights.shape[0]
    width = weights.shape[1] // 8
    return pl.pallas_call(
        own_kernel,
        out_shape=(
            *[jax.ShapeDtypeStruct((tokens, count * width), dtype) for count, dtype in GROUPS],
            jax.ShapeDtypeStruct((1, 8 * width), F32),
            pltpu.VMEM((4, depth, width), BF16),
            pltpu.VMEM((4, depth, width), BF16),
        ),
        in_specs=[vmem(), vmem(), pl.BlockSpec(memory_space=pltpu.HBM)],
        out_specs=(vmem(),) * (len(GROUPS) + 3),
        scratch_shapes=[pltpu.SemaphoreType.DMA((8, 2))],
        compiler_params=pltpu.CompilerParams(vmem_limit_bytes=VMEM_SMALL),
        cost_estimate=cheap(),
    )(left, right, left_in_hbm(weights))


def first_kernel(rows, held_keep, held_send, out):
    half, _, width = held_keep.shape
    depth = rows.shape[1]
    for held, base in ((held_keep, 0), (held_send, half)):

        @pl.loop(0, half)
        def _(i, held=held, base=base):
            out[:, columns(base + i, width)] = jnp.dot(
                rows[...], held[i, :depth], preferred_element_type=F32
            )


def first_product(rows, held, after=()):
    shape = (rows.shape[0], 8 * held[0].shape[2])
    args = [rows, *map(held_in_vmem, held)]
    return ordered_call(first_kernel, [(shape, F32)], args, after, cheap())[0]


def second_kernel(rows, held_keep, held_send, start, shift, *groups):
    _, depth, width = held_keep.shape
    cut = depth - rows.shape[1]

    def product(held, base, i):
        total = jnp.dot(rows[...], held[i, cut:], preferred_element_type=F32)
        return total + start[:, columns(base + i, width)] - shift[:, columns(base + i, width)]

    each_group(groups, held_keep, held_send, product)


def second_product(rows, held, start, shift, after=()):
    tokens = rows.shape[0]
    held_keep, held_send = held
    width = held_keep.shape[2]
    return ordered_call(
        second_kernel,
        [((tokens, count * width), dtype) for count, dtype in GROUPS],
        [rows, held_in_vmem(held_keep), held_in_vmem(held_send), start, shift],
        after,
        cheap(),
    )


def hold_kernel(factor, *rest):
    held, sems = rest[-2:]
    t = lax.axis_index("tp")
    count, rows, _ = held.shape

    def copy(i):
        start = pl.multiple_of(block_of(t, i) * rows, rows)
        return pltpu.make_async_copy(factor.at[pl.ds(start, rows)], held.at[i], sems.at[i])

    for i in range(count):
        copy(i).start()
    for i in range(count):
        copy(i).wait()


def hold(factor, after):
    deep, wide = factor.shape
    return pl.pallas_call(
        hold_kernel,
        out_shape=pltpu.VMEM((8, deep // 8, wide), BF16),
        in_specs=[pl.BlockSpec(memory_space=pltpu.HBM)]
        + [pl.BlockSpec(memory_space=pl.ANY)] * len(after),
        out_specs=vmem(),
        scratch_shapes=[pltpu.SemaphoreType.DMA((8,))],
        compiler_params=pltpu.CompilerParams(vmem_limit_bytes=VMEM_SMALL),
        cost_estimate=cheap(),
    )(left_in_hbm(factor), *after)


def white_kernel(base, rows, factor, *rest):
    *terms, out = rest
    count, depth = 4, factor.shape[1]
    total = None
    for i in range(count):
        part = jnp.dot(
            rows[:, i * depth : (i + 1) * depth], factor[base + i], preferred_element_type=F32
        )
        total = part if total is None else total + part
    for term in terms:
        total += term[...].astype(F32)
    out[...] = total.astype(out.dtype)


def white_product(rows, factor, base, dtype, *terms, after=()):
    shape = (rows.shape[0], factor.shape[2])
    args = [rows, held_in_vmem(factor), *terms]
    return ordered_call(functools.partial(white_kernel, base), [(shape, dtype)], args, after)[0]


def cheap():
    return pl.CostEstimate(flops=1024, bytes_accessed=1024, transcendentals=0)


def slow():
    return pl.CostEstimate(flops=10**10, bytes_accessed=10**9, transcendentals=0)


def qwen_kernel(scale, second, across, first, half, out):
    x, t, y = (lax.axis_index(axis) for axis in MESH)
    z = t >> 1
    llama_side, near = x == 0, z < 2
    other = jnp.where(llama_side, across[...], half[...])
    own = jnp.where(llama_side == near, first[...], second[...])
    flip = (z & 1) == y
    top, bottom = jnp.where(flip, other, own), jnp.where(flip, own, other)
    wide = jnp.concatenate([top, bottom], axis=0).astype(F32)
    out[...] = (scale * (wide - jnp.mean(wide, axis=0, keepdims=True))).astype(BF16)


def held_llama_kernel(half, across, first, out):
    x, t, _ = (lax.axis_index(axis) for axis in MESH)
    near = (t >> 1) < 2
    moved = jnp.where(near, first[...], across[...])
    stayed = jnp.where(near, half[...], first[...])
    out[...] = jnp.where(x == 0, stayed, moved)


def settled_kernel(held, diagonal, out):
    t, y = lax.axis_index("tp"), lax.axis_index("dp")
    out[...] = jnp.where(((t >> 1) & 1) == y, held[...], diagonal[...])


def cross_kernel(core, qwen, first, second, *rest):
    out, blocks, sems = rest[-3:]
    core = lax.axis_index("tp") & 1 if core == 0 else 1 - (lax.axis_index("tp") & 1)
    count, rows, _ = blocks.shape

    def copy(i):
        start = pl.multiple_of((core * count + i) * rows, rows)
        return pltpu.make_async_copy(blocks.at[i], out.at[pl.ds(start, rows)], sems.at[i])

    for i in range(count):
        part = slice(i * rows, (i + 1) * rows)
        llama = jnp.concatenate([first[:, part], second[:, part]], axis=0)
        blocks[i] = lax.dot_general(
            llama, qwen[...], (((0,), (0,)), ((), ())), preferred_element_type=F32
        )
        copy(i).start()
    for i in range(count):
        copy(i).wait()


def cross_product(core, qwen, first, second, out=None):
    _, width = qwen.shape
    features = first.shape[1]
    rows = min(256, features)
    steps = features // rows
    hbm = pl.BlockSpec(memory_space=pltpu.HBM)
    extra = [] if out is None else [out]
    return pl.pallas_call(
        functools.partial(cross_kernel, core),
        out_shape=jax.ShapeDtypeStruct((2 * features, width), F32),
        in_specs=[vmem()] * 3 + [hbm] * len(extra),
        out_specs=hbm,
        input_output_aliases={3: 0} if extra else {},
        scratch_shapes=[pltpu.VMEM((steps, rows, width), F32), pltpu.SemaphoreType.DMA((steps,))],
        compiler_params=pltpu.CompilerParams(vmem_limit_bytes=VMEM_LIMIT),
        cost_estimate=slow(),
    )(qwen, first, second, *extra)


def swapped(block, axis, mask):
    count = lax.axis_size(axis)
    return lax.ppermute(block, axis, [(i, i ^ mask) for i in range(count)])


def ordered_call(kernel, shapes, args, after=(), cost=None):
    def body(*refs):
        kernel(*refs[: len(args)], *refs[len(args) + len(after) :])

    return pl.pallas_call(
        body,
        out_shape=tuple(jax.ShapeDtypeStruct(shape, dtype) for shape, dtype in shapes),
        in_specs=[vmem()] * len(args) + [pl.BlockSpec(memory_space=pl.ANY)] * len(after),
        out_specs=tuple(vmem() for _ in shapes),
        compiler_params=pltpu.CompilerParams(vmem_limit_bytes=VMEM_SMALL),
        cost_estimate=cost or slow(),
    )(*args, *after)


def cut_at(rows, cut):
    tokens, width = rows.shape

    def kernel(whole, left, right):
        left[...] = whole[:, :cut]
        right[...] = whole[:, cut:]

    shapes = [((tokens, cut), rows.dtype), ((tokens, width - cut), rows.dtype)]
    return ordered_call(kernel, shapes, [rows], cost=cheap())


def added(keep, *got, after=()):
    def kernel(*refs):
        *terms, wide, narrow = refs
        wide[...] = sum(term[...].astype(F32) for term in terms)
        narrow[...] = wide[...].astype(BF16)

    return ordered_call(kernel, [(keep.shape, F32), (keep.shape, BF16)], [keep, *got], after)


def total(keep, *got, after=(), cost=None):
    width = got[0].shape[1]

    def kernel(own, *refs):
        *parts, out = refs
        for i, part in enumerate(parts):
            at = slice(i * width, (i + 1) * width)
            out[:, at] = (own[:, at] + part[...].astype(F32)).astype(BF16)

    return ordered_call(kernel, [(keep.shape, BF16)], [keep, *got], after, cost)[0]


def beside(left, right, after=()):
    tokens, width = left.shape

    def kernel(first, second, out):
        out[:, :width] = first[...]
        out[:, width:] = second[...]

    return ordered_call(kernel, [((tokens, 2 * width), left.dtype)], [left, right], after)[0]


def flat(x, t, y):
    return (x * 8 + t) * 2 + y


def route(block, moves):
    return lax.ppermute(block, MESH, [(flat(*a), flat(*b)) for a, b in moves])


def plan():
    across, first, second, neighbour, diagonal = [], [], [], [], []
    for t in range(8):
        z, core = t >> 1, t & 1
        for y in range(2):
            across.append(((1, t, y), (0, t, y)))
            if z >= 2:
                across.append(((0, t, y), (1, t, y)))
                first.append(((0, t, y), (1, t - 4, y)))
                first.append(((1, t, 1 - y), (1, t, y)))
                second.append(((1, t, 1 - y), (0, t, y)))
            else:
                first.append(((0, t, y), (0, t + 4, y)))
                first.append(((1, t, 1 - y), (0, t, y)))
                second.append(((1, t, 1 - y), (1, t, y)))
            for x in range(2):
                if z & 1 == y:
                    neighbour.append(((x, t, y), (x, t ^ 2, y)))
                else:
                    neighbour.append(((x, t, y), (x, t, 1 - y)))
                    diagonal.append(((x, t, y), (x, t ^ 2, 1 - y)))
    return across, first, second, neighbour, diagonal


def pipelined(hidden, down_weight, whitening):
    acts, weights, factor = hidden[0], down_weight[0], whitening[0]
    across, first, second, neighbour, diagonal = plan()

    depth = acts.shape[1]
    pieces = cut_at(acts, depth * CUT[0] // CUT[1] // 256 * 256)
    others = [swapped(piece, "dp", 1) for piece in pieces]
    o_keep, o_pass, o_other, *o_give, shift, held_keep, held_send = own_product(*pieces, weights)
    held = held_keep, held_send
    o_give = total(o_pass, *[swapped(piece, "tp", 1) for piece in o_give], cost=cheap())
    o_other = swapped(o_other, "tp", 1)
    start = first_product(others[0], held, after=[o_give])
    o_keep, o_give = added(o_keep, o_other, swapped(o_give, "tp", 2), after=[start])
    p_keep, p_pass, p_other, *p_give = second_product(
        others[1], held, start, shift, after=[o_give]
    )
    p_give = total(p_pass, *[swapped(piece, "tp", 1) for piece in p_give], cost=cheap())
    p_other = swapped(p_other, "tp", 1)
    held_factor = hold(factor, after=[p_give])
    o_sum = total(o_keep, swapped(o_give, "tp", 4), after=[held_factor])
    p_keep, p_give = added(p_keep, p_other, swapped(p_give, "tp", 2), after=[o_sum])
    o_sum = beside(o_sum, swapped(o_sum, "tp", 2))
    o_white = white_product(o_sum, held_factor, 0, F32)
    o_white = white_product(swapped(o_sum, "tp", 1), held_factor, 4, BF16, o_white)
    got = swapped(o_white, "dp", 1)
    p_sum = total(p_keep, swapped(p_give, "tp", 4), after=[o_white])
    p_sum = beside(p_sum, swapped(p_sum, "tp", 2))
    p_white = white_product(p_sum, held_factor, 0, F32)
    half = white_product(swapped(p_sum, "tp", 1), held_factor, 4, BF16, p_white, got)

    tokens, width = half.shape
    across = route(half, across)
    first = route(half, first)
    second = route(half, second)
    qwen = ordered_call(
        functools.partial(qwen_kernel, 1.0 / math.sqrt(2 * tokens)),
        [((2 * tokens, width), BF16)],
        [second, across, first, half],
    )[0]
    held = ordered_call(
        held_llama_kernel, [(half.shape, BF16)], [half, across, first], after=[qwen]
    )[0]
    beside_it = route(held, neighbour)
    diagonal = route(held, diagonal)
    other_beside = swapped(beside_it, "tp", 1)
    settled = ordered_call(
        settled_kernel, [(half.shape, BF16)], [held, diagonal], after=[other_beside]
    )[0]
    out = cross_product(0, qwen, settled, beside_it)
    return cross_product(1, qwen, swapped(settled, "tp", 1), other_beside, out)


def general(hidden, down_weight, whitening):
    acts, weights, factor = hidden[0], down_weight[0], whitening[0]
    tokens = lax.all_gather(acts, "dp", axis=0, tiled=True)
    partial = jnp.dot(tokens, weights, preferred_element_type=F32)
    outputs = lax.psum(partial, "tp").astype(BF16).astype(F32)
    centered = (outputs - jnp.mean(outputs, axis=0, keepdims=True)).astype(BF16)
    block = lax.psum_scatter(
        jnp.dot(centered, factor, preferred_element_type=F32),
        "dp",
        scatter_dimension=0,
        tiled=True,
    ).astype(BF16)
    both = lax.all_gather(block, "mp", axis=0)
    qwen = lax.all_gather(both[1], "dp", axis=0, tiled=True)
    llama = lax.all_gather(both[0], "tp", axis=1, tiled=True)
    width = llama.shape[1] // lax.axis_size("mp")
    llama = lax.dynamic_slice_in_dim(llama, lax.axis_index("mp") * width, width, 1)
    llama = lax.all_to_all(llama, "dp", split_axis=1, concat_axis=0, tiled=True)
    cross = lax.dot_general(llama, qwen, (((0,), (0,)), ((), ())), preferred_element_type=F32)
    return cross * (1.0 / math.sqrt(qwen.shape[0]))


def solution(mesh):
    placed = (P("mp", "dp", "tp"), P("mp", "tp", "dp"), P("mp", "dp", "tp"))
    sizes = tuple(mesh.shape[axis] for axis in MESH)
    body = pipelined if sizes == (2, 8, 2) else general
    return jax.shard_map(
        body, mesh=mesh, in_specs=placed, out_specs=P(("mp", "dp"), "tp"), check_vma=False
    )
```

```python
import functools
import math

import jax
import jax.numpy as jnp
from jax import lax
from jax.experimental import pallas as pl
from jax.experimental.pallas import tpu as pltpu
from jax.sharding import PartitionSpec as P

F32 = jnp.float32
BF16 = jnp.bfloat16
VMEM_LIMIT = 8 * 2**20
VMEM_SMALL = 3 * 2**20
MESH = ("mp", "tp", "dp")
CUT = (5, 7)
GROUPS = ((2, F32), (2, F32), (2, BF16), (1, BF16), (1, BF16))


def vmem():
    return pl.BlockSpec(memory_space=pltpu.VMEM)


def block_of(t, place):
    core, z = (t & 1) ^ (place >> 2), ((t >> 1) & 1) ^ ((place >> 1) & 1)
    return core << 2 | z << 1 | (place & 1)


def held_in_vmem(block):
    return pltpu.with_memory_space_constraint(block, pltpu.VMEM)


def left_in_hbm(block):
    return pltpu.with_memory_space_constraint(block, pltpu.HBM)


def columns(i, width):
    return pl.ds(pl.multiple_of(i * width, width), width)


def each_group(groups, held_keep, held_send, product):
    half, _, width = held_keep.shape
    *pairs, last, end = groups
    for number, group in enumerate(pairs):
        held, base = (held_keep, 0) if number < 2 else (held_send, half)

        @pl.loop(0, 2)
        def _(i, held=held, base=base, first=number % 2 * 2, group=group):
            group[:, columns(i, width)] = product(held, base, first + i).astype(group.dtype)

    @pl.loop(0, 2)
    def _(i):
        block = product(held_send, half, 2 + i).astype(BF16)
        for number, group in enumerate((last, end)):

            @pl.when(i == number)
            def _(group=group):
                group[...] = block


def own_kernel(left, right, weights, *rest):
    *groups, shift, held_keep, held_send, sems = rest
    t = lax.axis_index("tp")
    half, depth, width = held_keep.shape
    count = 2 * half
    cut = left.shape[1]

    def copy(held, base, i, k):
        part = pl.ds(0, cut) if k == 0 else pl.ds(cut, depth - cut)
        source = weights.at[part, columns(block_of(t, base + i), width)]
        return pltpu.make_async_copy(source, held.at[i, part], sems.at[base + i, k])

    for held, base in ((held_keep, 0), (held_send, half)):
        for i in range(half):
            for k in range(2):
                copy(held, base, i, k).start()

    def product(held, base, i):
        copy(held, base, i, 0).wait()
        total = jnp.dot(left[...], held[i, :cut], preferred_element_type=F32)
        copy(held, base, i, 1).wait()
        total += jnp.dot(right[...], held[i, cut:], preferred_element_type=F32)
        mean = jnp.mean(total, axis=0, keepdims=True)
        shift[:, columns(base + i, width)] = mean
        return total - mean

    each_group(groups, held_keep, held_send, product)


def own_product(left, right, weights):
    tokens = left.shape[0]
    depth = weights.shape[0]
    width = weights.shape[1] // 8
    return pl.pallas_call(
        own_kernel,
        out_shape=(
            *[jax.ShapeDtypeStruct((tokens, count * width), dtype) for count, dtype in GROUPS],
            jax.ShapeDtypeStruct((1, 8 * width), F32),
            pltpu.VMEM((4, depth, width), BF16),
            pltpu.VMEM((4, depth, width), BF16),
        ),
        in_specs=[vmem(), vmem(), pl.BlockSpec(memory_space=pltpu.HBM)],
        out_specs=(vmem(),) * (len(GROUPS) + 3),
        scratch_shapes=[pltpu.SemaphoreType.DMA((8, 2))],
        compiler_params=pltpu.CompilerParams(vmem_limit_bytes=VMEM_SMALL),
        cost_estimate=cheap(),
    )(left, right, left_in_hbm(weights))


def first_kernel(rows, held_keep, held_send, out):
    half, _, width = held_keep.shape
    depth = rows.shape[1]
    for held, base in ((held_keep, 0), (held_send, half)):

        @pl.loop(0, half)
        def _(i, held=held, base=base):
            out[:, columns(base + i, width)] = jnp.dot(
                rows[...], held[i, :depth], preferred_element_type=F32
            )


def first_product(rows, held, after=()):
    shape = (rows.shape[0], 8 * held[0].shape[2])
    args = [rows, *map(held_in_vmem, held)]
    return ordered_call(first_kernel, [(shape, F32)], args, after, cheap())[0]


def second_kernel(rows, held_keep, held_send, start, shift, *groups):
    _, depth, width = held_keep.shape
    cut = depth - rows.shape[1]

    def product(held, base, i):
        total = jnp.dot(rows[...], held[i, cut:], preferred_element_type=F32)
        return total + start[:, columns(base + i, width)] - shift[:, columns(base + i, width)]

    each_group(groups, held_keep, held_send, product)


def second_product(rows, held, start, shift, after=()):
    tokens = rows.shape[0]
    held_keep, held_send = held
    width = held_keep.shape[2]
    return ordered_call(
        second_kernel,
        [((tokens, count * width), dtype) for count, dtype in GROUPS],
        [rows, held_in_vmem(held_keep), held_in_vmem(held_send), start, shift],
        after,
        cheap(),
    )


def hold_kernel(factor, *rest):
    held, sems = rest[-2:]
    t = lax.axis_index("tp")
    count, rows, _ = held.shape

    def copy(i):
        start = pl.multiple_of(block_of(t, i) * rows, rows)
        return pltpu.make_async_copy(factor.at[pl.ds(start, rows)], held.at[i], sems.at[i])

    for i in range(count):
        copy(i).start()
    for i in range(count):
        copy(i).wait()


def hold(factor, after):
    deep, wide = factor.shape
    return pl.pallas_call(
        hold_kernel,
        out_shape=pltpu.VMEM((8, deep // 8, wide), BF16),
        in_specs=[pl.BlockSpec(memory_space=pltpu.HBM)]
        + [pl.BlockSpec(memory_space=pl.ANY)] * len(after),
        out_specs=vmem(),
        scratch_shapes=[pltpu.SemaphoreType.DMA((8,))],
        compiler_params=pltpu.CompilerParams(vmem_limit_bytes=VMEM_SMALL),
        cost_estimate=cheap(),
    )(left_in_hbm(factor), *after)


def white_kernel(base, rows, factor, *rest):
    *terms, out = rest
    count, depth = 4, factor.shape[1]
    total = None
    for i in range(count):
        part = jnp.dot(
            rows[:, i * depth : (i + 1) * depth], factor[base + i], preferred_element_type=F32
        )
        total = part if total is None else total + part
    for term in terms:
        total += term[...].astype(F32)
    out[...] = total.astype(out.dtype)


def white_product(rows, factor, base, dtype, *terms, after=()):
    shape = (rows.shape[0], factor.shape[2])
    args = [rows, held_in_vmem(factor), *terms]
    return ordered_call(functools.partial(white_kernel, base), [(shape, dtype)], args, after)[0]


def cheap():
    return pl.CostEstimate(flops=1024, bytes_accessed=1024, transcendentals=0)


def slow():
    return pl.CostEstimate(flops=10**10, bytes_accessed=10**9, transcendentals=0)


def qwen_kernel(scale, second, across, first, half, out):
    x, t, y = (lax.axis_index(axis) for axis in MESH)
    z = t >> 1
    llama_side, near = x == 0, z < 2
    other = jnp.where(llama_side, across[...], half[...])
    own = jnp.where(llama_side == near, first[...], second[...])
    flip = (z & 1) == y
    top, bottom = jnp.where(flip, other, own), jnp.where(flip, own, other)
    wide = jnp.concatenate([top, bottom], axis=0).astype(F32)
    out[...] = (scale * (wide - jnp.mean(wide, axis=0, keepdims=True))).astype(BF16)


def held_llama_kernel(half, across, first, out):
    x, t, _ = (lax.axis_index(axis) for axis in MESH)
    near = (t >> 1) < 2
    moved = jnp.where(near, first[...], across[...])
    stayed = jnp.where(near, half[...], first[...])
    out[...] = jnp.where(x == 0, stayed, moved)


def settled_kernel(held, diagonal, out):
    t, y = lax.axis_index("tp"), lax.axis_index("dp")
    out[...] = jnp.where(((t >> 1) & 1) == y, held[...], diagonal[...])


def cross_kernel(core, qwen, first, second, *rest):
    out, blocks, sems = rest[-3:]
    core = lax.axis_index("tp") & 1 if core == 0 else 1 - (lax.axis_index("tp") & 1)
    count, rows, _ = blocks.shape

    def copy(i):
        start = pl.multiple_of((core * count + i) * rows, rows)
        return pltpu.make_async_copy(blocks.at[i], out.at[pl.ds(start, rows)], sems.at[i])

    for i in range(count):
        part = slice(i * rows, (i + 1) * rows)
        llama = jnp.concatenate([first[:, part], second[:, part]], axis=0)
        blocks[i] = lax.dot_general(
            llama, qwen[...], (((0,), (0,)), ((), ())), preferred_element_type=F32
        )
        copy(i).start()
    for i in range(count):
        copy(i).wait()


def cross_product(core, qwen, first, second, out=None):
    _, width = qwen.shape
    features = first.shape[1]
    rows = min(256, features)
    steps = features // rows
    hbm = pl.BlockSpec(memory_space=pltpu.HBM)
    extra = [] if out is None else [out]
    return pl.pallas_call(
        functools.partial(cross_kernel, core),
        out_shape=jax.ShapeDtypeStruct((2 * features, width), F32),
        in_specs=[vmem()] * 3 + [hbm] * len(extra),
        out_specs=hbm,
        input_output_aliases={3: 0} if extra else {},
        scratch_shapes=[pltpu.VMEM((steps, rows, width), F32), pltpu.SemaphoreType.DMA((steps,))],
        compiler_params=pltpu.CompilerParams(vmem_limit_bytes=VMEM_LIMIT),
        cost_estimate=slow(),
    )(qwen, first, second, *extra)


def swapped(block, axis, mask):
    count = lax.axis_size(axis)
    return lax.ppermute(block, axis, [(i, i ^ mask) for i in range(count)])


def ordered_call(kernel, shapes, args, after=(), cost=None):
    def body(*refs):
        kernel(*refs[: len(args)], *refs[len(args) + len(after) :])

    return pl.pallas_call(
        body,
        out_shape=tuple(jax.ShapeDtypeStruct(shape, dtype) for shape, dtype in shapes),
        in_specs=[vmem()] * len(args) + [pl.BlockSpec(memory_space=pl.ANY)] * len(after),
        out_specs=tuple(vmem() for _ in shapes),
        compiler_params=pltpu.CompilerParams(vmem_limit_bytes=VMEM_SMALL),
        cost_estimate=cost or slow(),
    )(*args, *after)


def cut_at(rows, cut):
    tokens, width = rows.shape

    def kernel(whole, left, right):
        left[...] = whole[:, :cut]
        right[...] = whole[:, cut:]

    shapes = [((tokens, cut), rows.dtype), ((tokens, width - cut), rows.dtype)]
    return ordered_call(kernel, shapes, [rows], cost=cheap())


def added(keep, *got, after=()):
    def kernel(*refs):
        *terms, wide, narrow = refs
        wide[...] = sum(term[...].astype(F32) for term in terms)
        narrow[...] = wide[...].astype(BF16)

    return ordered_call(kernel, [(keep.shape, F32), (keep.shape, BF16)], [keep, *got], after)


def total(keep, *got, after=(), cost=None):
    width = got[0].shape[1]

    def kernel(own, *refs):
        *parts, out = refs
        for i, part in enumerate(parts):
            at = slice(i * width, (i + 1) * width)
            out[:, at] = (own[:, at] + part[...].astype(F32)).astype(BF16)

    return ordered_call(kernel, [(keep.shape, BF16)], [keep, *got], after, cost)[0]


def beside(left, right, after=()):
    tokens, width = left.shape

    def kernel(first, second, out):
        out[:, :width] = first[...]
        out[:, width:] = second[...]

    return ordered_call(kernel, [((tokens, 2 * width), left.dtype)], [left, right], after)[0]


def flat(x, t, y):
    return (x * 8 + t) * 2 + y


def route(block, moves):
    return lax.ppermute(block, MESH, [(flat(*a), flat(*b)) for a, b in moves])


def plan():
    across, first, second, neighbour, diagonal = [], [], [], [], []
    for t in range(8):
        z, core = t >> 1, t & 1
        for y in range(2):
            across.append(((1, t, y), (0, t, y)))
            if z >= 2:
                across.append(((0, t, y), (1, t, y)))
                first.append(((0, t, y), (1, t - 4, y)))
                first.append(((1, t, 1 - y), (1, t, y)))
                second.append(((1, t, 1 - y), (0, t, y)))
            else:
                first.append(((0, t, y), (0, t + 4, y)))
                first.append(((1, t, 1 - y), (0, t, y)))
                second.append(((1, t, 1 - y), (1, t, y)))
            for x in range(2):
                if z & 1 == y:
                    neighbour.append(((x, t, y), (x, t ^ 2, y)))
                else:
                    neighbour.append(((x, t, y), (x, t, 1 - y)))
                    diagonal.append(((x, t, y), (x, t ^ 2, 1 - y)))
    return across, first, second, neighbour, diagonal


def pipelined(hidden, down_weight, whitening):
    acts, weights, factor = hidden[0], down_weight[0], whitening[0]
    across, first, second, neighbour, diagonal = plan()

    depth = acts.shape[1]
    pieces = cut_at(acts, depth * CUT[0] // CUT[1] // 256 * 256)
    others = [swapped(piece, "dp", 1) for piece in pieces]
    o_keep, o_pass, o_other, *o_give, shift, held_keep, held_send = own_product(*pieces, weights)
    held = held_keep, held_send
    o_give = total(o_pass, *[swapped(piece, "tp", 1) for piece in o_give], cost=cheap())
    o_other = swapped(o_other, "tp", 1)
    start = first_product(others[0], held, after=[o_give])
    o_keep, o_give = added(o_keep, o_other, swapped(o_give, "tp", 2), after=[start])
    p_keep, p_pass, p_other, *p_give = second_product(
        others[1], held, start, shift, after=[o_give]
    )
    p_give = total(p_pass, *[swapped(piece, "tp", 1) for piece in p_give], cost=cheap())
    p_other = swapped(p_other, "tp", 1)
    held_factor = hold(factor, after=[p_give])
    o_sum = total(o_keep, swapped(o_give, "tp", 4), after=[held_factor])
    p_keep, p_give = added(p_keep, p_other, swapped(p_give, "tp", 2), after=[o_sum])
    o_sum = beside(o_sum, swapped(o_sum, "tp", 2))
    o_white = white_product(o_sum, held_factor, 0, F32)
    o_white = white_product(swapped(o_sum, "tp", 1), held_factor, 4, BF16, o_white)
    got = swapped(o_white, "dp", 1)
    p_sum = total(p_keep, swapped(p_give, "tp", 4), after=[o_white])
    p_sum = beside(p_sum, swapped(p_sum, "tp", 2))
    p_white = white_product(p_sum, held_factor, 0, F32)
    half = white_product(swapped(p_sum, "tp", 1), held_factor, 4, BF16, p_white, got)

    tokens, width = half.shape
    across = route(half, across)
    first = route(half, first)
    second = route(half, second)
    qwen = ordered_call(
        functools.partial(qwen_kernel, 1.0 / math.sqrt(2 * tokens)),
        [((2 * tokens, width), BF16)],
        [second, across, first, half],
    )[0]
    held = ordered_call(
        held_llama_kernel, [(half.shape, BF16)], [half, across, first], after=[qwen]
    )[0]
    beside_it = route(held, neighbour)
    diagonal = route(held, diagonal)
    other_beside = swapped(beside_it, "tp", 1)
    settled = ordered_call(
        settled_kernel, [(half.shape, BF16)], [held, diagonal], after=[other_beside]
    )[0]
    out = cross_product(0, qwen, settled, beside_it)
    return cross_product(1, qwen, swapped(settled, "tp", 1), other_beside, out)


def general(hidden, down_weight, whitening):
    acts, weights, factor = hidden[0], down_weight[0], whitening[0]
    tokens = lax.all_gather(acts, "dp", axis=0, tiled=True)
    partial = jnp.dot(tokens, weights, preferred_element_type=F32)
    outputs = lax.psum(partial, "tp").astype(BF16).astype(F32)
    centered = (outputs - jnp.mean(outputs, axis=0, keepdims=True)).astype(BF16)
    block = lax.psum_scatter(
        jnp.dot(centered, factor, preferred_element_type=F32),
        "dp",
        scatter_dimension=0,
        tiled=True,
    ).astype(BF16)
    both = lax.all_gather(block, "mp", axis=0)
    qwen = lax.all_gather(both[1], "dp", axis=0, tiled=True)
    llama = lax.all_gather(both[0], "tp", axis=1, tiled=True)
    width = llama.shape[1] // lax.axis_size("mp")
    llama = lax.dynamic_slice_in_dim(llama, lax.axis_index("mp") * width, width, 1)
    llama = lax.all_to_all(llama, "dp", split_axis=1, concat_axis=0, tiled=True)
    cross = lax.dot_general(llama, qwen, (((0,), (0,)), ((), ())), preferred_element_type=F32)
    return cross * (1.0 / math.sqrt(qwen.shape[0]))


def solution(mesh):
    placed = (P("mp", "dp", "tp"), P("mp", "tp", "dp"), P("mp", "dp", "tp"))
    sizes = tuple(mesh.shape[axis] for axis in MESH)
    body = pipelined if sizes == (2, 8, 2) else general
    return jax.shard_map(
        body, mesh=mesh, in_specs=placed, out_specs=P(("mp", "dp"), "tp"), check_vma=False
    )
```

```python
import functools
import math

import jax
import jax.numpy as jnp
from jax import lax
from jax.experimental import pallas as pl
from jax.experimental.pallas import tpu as pltpu
from jax.sharding import PartitionSpec as P

F32 = jnp.float32
BF16 = jnp.bfloat16
VMEM_LIMIT = 8 * 2**20
VMEM_SMALL = 3 * 2**20
MESH = ("mp", "tp", "dp")
CUT = (5, 7)


def vmem():
    return pl.BlockSpec(memory_space=pltpu.VMEM)


def block_of(t, place):
    core, z = (t & 1) ^ (place >> 2), ((t >> 1) & 1) ^ ((place >> 1) & 1)
    return core << 2 | z << 1 | (place & 1)


def held_in_vmem(block):
    return pltpu.with_memory_space_constraint(block, pltpu.VMEM)


def left_in_hbm(block):
    return pltpu.with_memory_space_constraint(block, pltpu.HBM)


def columns(i, width):
    return pl.ds(pl.multiple_of(i * width, width), width)


def place_of(part, i):
    return i + 2 * (1 - part) + 2 * (i >> 1)


def group_shapes(part, tokens, width):
    own = [((tokens, 2 * width), F32)]
    return own + ([((tokens, width), BF16)] * 2 if part == 0 else [((tokens, 2 * width), BF16)])


def each_group(groups, width, product):
    own, *other = groups

    @pl.loop(0, 2)
    def _(i):
        own[:, columns(i, width)] = product(i)

    @pl.loop(0, 2)
    def _(i):
        block = product(2 + i).astype(BF16)
        if len(other) == 1:
            other[0][:, columns(i, width)] = block
            return
        for number, group in enumerate(other):

            @pl.when(i == number)
            def _(group=group):
                group[...] = block


def own_kernel(part, extra, left, right, weights, *rest):
    *groups, shift, held, sems = rest[extra:]
    t = lax.axis_index("tp")
    count, depth, width = held.shape
    cut = left.shape[1]

    def copy(i, k):
        rows = pl.ds(0, cut) if k == 0 else pl.ds(cut, depth - cut)
        source = weights.at[rows, columns(block_of(t, place_of(part, i)), width)]
        return pltpu.make_async_copy(source, held.at[i, rows], sems.at[i, k])

    for i in range(count):
        for k in range(2):
            copy(i, k).start()

    def product(i):
        copy(i, 0).wait()
        total = jnp.dot(left[...], held[i, :cut], preferred_element_type=F32)
        copy(i, 1).wait()
        total += jnp.dot(right[...], held[i, cut:], preferred_element_type=F32)
        mean = jnp.mean(total, axis=0, keepdims=True)
        shift[:, columns(i, width)] = mean
        return total - mean

    each_group(groups, width, product)


def own_product(part, left, right, weights, after=()):
    tokens, depth, width = left.shape[0], weights.shape[0], weights.shape[1] // 8
    shapes = group_shapes(part, tokens, width) + [((1, 4 * width), F32)]
    return pl.pallas_call(
        functools.partial(own_kernel, part, len(after)),
        out_shape=(
            *[jax.ShapeDtypeStruct(shape, dtype) for shape, dtype in shapes],
            pltpu.VMEM((4, depth, width), BF16),
        ),
        in_specs=[vmem(), vmem(), pl.BlockSpec(memory_space=pltpu.HBM)]
        + [pl.BlockSpec(memory_space=pl.ANY)] * len(after),
        out_specs=(vmem(),) * (len(shapes) + 1),
        scratch_shapes=[pltpu.SemaphoreType.DMA((4, 2))],
        compiler_params=pltpu.CompilerParams(vmem_limit_bytes=VMEM_SMALL),
        cost_estimate=cheap(),
    )(left, right, left_in_hbm(weights), *after)


def first_kernel(rows, *rest):
    *parts, out = rest
    count, _, width = parts[0].shape
    depth = rows.shape[1]
    for part, held in enumerate(parts):

        @pl.loop(0, count)
        def _(i, part=part, held=held):
            out[:, columns(count * part + i, width)] = jnp.dot(
                rows[...], held[i, :depth], preferred_element_type=F32
            )


def first_product(rows, held, after=()):
    shape = (rows.shape[0], 8 * held[0].shape[2])
    args = [rows, *map(held_in_vmem, held)]
    return ordered_call(first_kernel, [(shape, F32)], args, after, cheap())[0]


def second_kernel(counts, rows, start, *rest):
    parts, shifts, groups = rest[:2], rest[2:4], rest[4:]
    count, depth, width = parts[0].shape
    cut = depth - rows.shape[1]
    for part, (held, shift) in enumerate(zip(parts, shifts)):

        def product(i, part=part, held=held, shift=shift):
            total = jnp.dot(rows[...], held[i, cut:], preferred_element_type=F32)
            return total + start[:, columns(count * part + i, width)] - shift[:, columns(i, width)]

        first = sum(counts[:part])
        each_group(groups[first : first + counts[part]], width, product)


def second_product(rows, held, start, shifts, after=()):
    tokens, width = rows.shape[0], held[0].shape[2]
    shapes = [group_shapes(part, tokens, width) for part in range(2)]
    kernel = functools.partial(second_kernel, [len(part) for part in shapes])
    args = [rows, start, *map(held_in_vmem, held), *shifts]
    return ordered_call(kernel, shapes[0] + shapes[1], args, after, cheap())


def hold_kernel(factor, *rest):
    held, sems = rest[-2:]
    t = lax.axis_index("tp")
    count, rows, _ = held.shape

    def copy(i):
        start = pl.multiple_of(block_of(t, i) * rows, rows)
        return pltpu.make_async_copy(factor.at[pl.ds(start, rows)], held.at[i], sems.at[i])

    for i in range(count):
        copy(i).start()
    for i in range(count):
        copy(i).wait()


def hold(factor, after):
    deep, wide = factor.shape
    return pl.pallas_call(
        hold_kernel,
        out_shape=pltpu.VMEM((8, deep // 8, wide), BF16),
        in_specs=[pl.BlockSpec(memory_space=pltpu.HBM)]
        + [pl.BlockSpec(memory_space=pl.ANY)] * len(after),
        out_specs=vmem(),
        scratch_shapes=[pltpu.SemaphoreType.DMA((8,))],
        compiler_params=pltpu.CompilerParams(vmem_limit_bytes=VMEM_SMALL),
        cost_estimate=cheap(),
    )(left_in_hbm(factor), *after)


def white_kernel(base, rows, factor, *rest):
    *terms, out = rest
    count, depth = 4, factor.shape[1]
    total = None
    for i in range(count):
        part = jnp.dot(
            rows[:, i * depth : (i + 1) * depth], factor[base + i], preferred_element_type=F32
        )
        total = part if total is None else total + part
    for term in terms:
        total += term[...].astype(F32)
    out[...] = total.astype(out.dtype)


def white_product(rows, factor, base, dtype, *terms, after=()):
    shape = (rows.shape[0], factor.shape[2])
    args = [rows, held_in_vmem(factor), *terms]
    return ordered_call(functools.partial(white_kernel, base), [(shape, dtype)], args, after)[0]


def cheap():
    return pl.CostEstimate(flops=1024, bytes_accessed=1024, transcendentals=0)


def slow():
    return pl.CostEstimate(flops=10**10, bytes_accessed=10**9, transcendentals=0)


def qwen_kernel(scale, second, across, first, half, out):
    x, t, y = (lax.axis_index(axis) for axis in MESH)
    z = t >> 1
    llama_side, near = x == 0, z < 2
    other = jnp.where(llama_side, across[...], half[...])
    own = jnp.where(llama_side == near, first[...], second[...])
    flip = (z & 1) == y
    top, bottom = jnp.where(flip, other, own), jnp.where(flip, own, other)
    wide = jnp.concatenate([top, bottom], axis=0).astype(F32)
    out[...] = (scale * (wide - jnp.mean(wide, axis=0, keepdims=True))).astype(BF16)


def held_llama_kernel(half, across, first, out):
    x, t, _ = (lax.axis_index(axis) for axis in MESH)
    near = (t >> 1) < 2
    moved = jnp.where(near, first[...], across[...])
    stayed = jnp.where(near, half[...], first[...])
    out[...] = jnp.where(x == 0, stayed, moved)


def settled_kernel(held, diagonal, out):
    t, y = lax.axis_index("tp"), lax.axis_index("dp")
    out[...] = jnp.where(((t >> 1) & 1) == y, held[...], diagonal[...])


def cross_kernel(core, qwen, first, second, *rest):
    out, blocks, sems = rest[-3:]
    core = lax.axis_index("tp") & 1 if core == 0 else 1 - (lax.axis_index("tp") & 1)
    count, rows, _ = blocks.shape

    def copy(i):
        start = pl.multiple_of((core * count + i) * rows, rows)
        return pltpu.make_async_copy(blocks.at[i], out.at[pl.ds(start, rows)], sems.at[i])

    for i in range(count):
        part = slice(i * rows, (i + 1) * rows)
        llama = jnp.concatenate([first[:, part], second[:, part]], axis=0)
        blocks[i] = lax.dot_general(
            llama, qwen[...], (((0,), (0,)), ((), ())), preferred_element_type=F32
        )
        copy(i).start()
    for i in range(count):
        copy(i).wait()


def cross_product(core, qwen, first, second, out=None):
    _, width = qwen.shape
    features = first.shape[1]
    rows = min(256, features)
    steps = features // rows
    hbm = pl.BlockSpec(memory_space=pltpu.HBM)
    extra = [] if out is None else [out]
    return pl.pallas_call(
        functools.partial(cross_kernel, core),
        out_shape=jax.ShapeDtypeStruct((2 * features, width), F32),
        in_specs=[vmem()] * 3 + [hbm] * len(extra),
        out_specs=hbm,
        input_output_aliases={3: 0} if extra else {},
        scratch_shapes=[pltpu.VMEM((steps, rows, width), F32), pltpu.SemaphoreType.DMA((steps,))],
        compiler_params=pltpu.CompilerParams(vmem_limit_bytes=VMEM_LIMIT),
        cost_estimate=slow(),
    )(qwen, first, second, *extra)


def swapped(block, axis, mask):
    count = lax.axis_size(axis)
    return lax.ppermute(block, axis, [(i, i ^ mask) for i in range(count)])


def ordered_call(kernel, shapes, args, after=(), cost=None):
    def body(*refs):
        kernel(*refs[: len(args)], *refs[len(args) + len(after) :])

    return pl.pallas_call(
        body,
        out_shape=tuple(jax.ShapeDtypeStruct(shape, dtype) for shape, dtype in shapes),
        in_specs=[vmem()] * len(args) + [pl.BlockSpec(memory_space=pl.ANY)] * len(after),
        out_specs=tuple(vmem() for _ in shapes),
        compiler_params=pltpu.CompilerParams(vmem_limit_bytes=VMEM_SMALL),
        cost_estimate=cost or slow(),
    )(*args, *after)


def cut_at(rows, cut):
    tokens, width = rows.shape

    def kernel(whole, left, right):
        left[...] = whole[:, :cut]
        right[...] = whole[:, cut:]

    shapes = [((tokens, cut), rows.dtype), ((tokens, width - cut), rows.dtype)]
    return ordered_call(kernel, shapes, [rows], cost=cheap())


def added(keep, *got, after=()):
    def kernel(*refs):
        *terms, wide, narrow = refs
        wide[...] = sum(term[...].astype(F32) for term in terms)
        narrow[...] = wide[...].astype(BF16)

    return ordered_call(kernel, [(keep.shape, F32), (keep.shape, BF16)], [keep, *got], after)


def total(keep, *got, after=(), cost=None):
    width = got[0].shape[1]

    def kernel(own, *refs):
        *parts, out = refs
        for i, part in enumerate(parts):
            at = slice(i * width, (i + 1) * width)
            out[:, at] = (own[:, at] + part[...].astype(F32)).astype(BF16)

    return ordered_call(kernel, [(keep.shape, BF16)], [keep, *got], after, cost)[0]


def beside(left, right, after=()):
    tokens, width = left.shape

    def kernel(first, second, out):
        out[:, :width] = first[...]
        out[:, width:] = second[...]

    return ordered_call(kernel, [((tokens, 2 * width), left.dtype)], [left, right], after)[0]


def flat(x, t, y):
    return (x * 8 + t) * 2 + y


def route(block, moves):
    return lax.ppermute(block, MESH, [(flat(*a), flat(*b)) for a, b in moves])


def plan():
    across, first, second, neighbour, diagonal = [], [], [], [], []
    for t in range(8):
        z, core = t >> 1, t & 1
        for y in range(2):
            across.append(((1, t, y), (0, t, y)))
            if z >= 2:
                across.append(((0, t, y), (1, t, y)))
                first.append(((0, t, y), (1, t - 4, y)))
                first.append(((1, t, 1 - y), (1, t, y)))
                second.append(((1, t, 1 - y), (0, t, y)))
            else:
                first.append(((0, t, y), (0, t + 4, y)))
                first.append(((1, t, 1 - y), (0, t, y)))
                second.append(((1, t, 1 - y), (1, t, y)))
            for x in range(2):
                if z & 1 == y:
                    neighbour.append(((x, t, y), (x, t ^ 2, y)))
                else:
                    neighbour.append(((x, t, y), (x, t, 1 - y)))
                    diagonal.append(((x, t, y), (x, t ^ 2, 1 - y)))
    return across, first, second, neighbour, diagonal


def pipelined(hidden, down_weight, whitening):
    acts, weights, factor = hidden[0], down_weight[0], whitening[0]
    across, first, second, neighbour, diagonal = plan()

    depth = acts.shape[1]
    pieces = cut_at(acts, depth * CUT[0] // CUT[1] // 256 * 256)
    others = [swapped(piece, "dp", 1) for piece in pieces]
    o_pass, *o_give, shift_0, held_0 = own_product(0, *pieces, weights)
    o_give = total(o_pass, *[swapped(piece, "tp", 1) for piece in o_give], cost=cheap())
    o_keep, o_other, shift_1, held_1 = own_product(1, *pieces, weights, after=[o_give])
    held, shifts = (held_0, held_1), (shift_0, shift_1)
    o_other = swapped(o_other, "tp", 1)
    start = first_product(others[0], held)
    o_keep, o_give = added(o_keep, o_other, swapped(o_give, "tp", 2), after=[start])
    p_pass, *p_give, p_keep, p_other = second_product(
        others[1], held, start, shifts, after=[o_give]
    )
    p_give = total(p_pass, *[swapped(piece, "tp", 1) for piece in p_give], cost=cheap())
    p_other = swapped(p_other, "tp", 1)
    held_factor = hold(factor, after=[p_give])
    o_sum = total(o_keep, swapped(o_give, "tp", 4), after=[held_factor])
    p_keep, p_give = added(p_keep, p_other, swapped(p_give, "tp", 2), after=[o_sum])
    o_sum = beside(o_sum, swapped(o_sum, "tp", 2))
    o_white = white_product(o_sum, held_factor, 0, F32)
    o_white = white_product(swapped(o_sum, "tp", 1), held_factor, 4, BF16, o_white)
    got = swapped(o_white, "dp", 1)
    p_sum = total(p_keep, swapped(p_give, "tp", 4), after=[o_white])
    p_sum = beside(p_sum, swapped(p_sum, "tp", 2))
    p_white = white_product(p_sum, held_factor, 0, F32)
    half = white_product(swapped(p_sum, "tp", 1), held_factor, 4, BF16, p_white, got)

    tokens, width = half.shape
    across = route(half, across)
    first = route(half, first)
    second = route(half, second)
    qwen = ordered_call(
        functools.partial(qwen_kernel, 1.0 / math.sqrt(2 * tokens)),
        [((2 * tokens, width), BF16)],
        [second, across, first, half],
    )[0]
    held = ordered_call(
        held_llama_kernel, [(half.shape, BF16)], [half, across, first], after=[qwen]
    )[0]
    beside_it = route(held, neighbour)
    diagonal = route(held, diagonal)
    other_beside = swapped(beside_it, "tp", 1)
    settled = ordered_call(
        settled_kernel, [(half.shape, BF16)], [held, diagonal], after=[other_beside]
    )[0]
    out = cross_product(0, qwen, settled, beside_it)
    return cross_product(1, qwen, swapped(settled, "tp", 1), other_beside, out)


def general(hidden, down_weight, whitening):
    acts, weights, factor = hidden[0], down_weight[0], whitening[0]
    tokens = lax.all_gather(acts, "dp", axis=0, tiled=True)
    partial = jnp.dot(tokens, weights, preferred_element_type=F32)
    outputs = lax.psum(partial, "tp").astype(BF16).astype(F32)
    centered = (outputs - jnp.mean(outputs, axis=0, keepdims=True)).astype(BF16)
    block = lax.psum_scatter(
        jnp.dot(centered, factor, preferred_element_type=F32),
        "dp",
        scatter_dimension=0,
        tiled=True,
    ).astype(BF16)
    both = lax.all_gather(block, "mp", axis=0)
    qwen = lax.all_gather(both[1], "dp", axis=0, tiled=True)
    llama = lax.all_gather(both[0], "tp", axis=1, tiled=True)
    width = llama.shape[1] // lax.axis_size("mp")
    llama = lax.dynamic_slice_in_dim(llama, lax.axis_index("mp") * width, width, 1)
    llama = lax.all_to_all(llama, "dp", split_axis=1, concat_axis=0, tiled=True)
    cross = lax.dot_general(llama, qwen, (((0,), (0,)), ((), ())), preferred_element_type=F32)
    return cross * (1.0 / math.sqrt(qwen.shape[0]))


def solution(mesh):
    placed = (P("mp", "dp", "tp"), P("mp", "tp", "dp"), P("mp", "dp", "tp"))
    sizes = tuple(mesh.shape[axis] for axis in MESH)
    body = pipelined if sizes == (2, 8, 2) else general
    return jax.shard_map(
        body, mesh=mesh, in_specs=placed, out_specs=P(("mp", "dp"), "tp"), check_vma=False
    )
```

```python
import functools
import math

import jax
import jax.numpy as jnp
from jax import lax
from jax.experimental import pallas as pl
from jax.experimental.pallas import tpu as pltpu
from jax.sharding import PartitionSpec as P

F32 = jnp.float32
BF16 = jnp.bfloat16
VMEM_LIMIT = 8 * 2**20
VMEM_SMALL = 3 * 2**20
MESH = ("mp", "tp", "dp")
CUT = (5, 7)
GROUPS = ((2, F32), (2, F32), (2, BF16), (1, BF16), (1, BF16))


def vmem():
    return pl.BlockSpec(memory_space=pltpu.VMEM)


def block_of(t, place):
    core, z = (t & 1) ^ (place >> 2), ((t >> 1) & 1) ^ ((place >> 1) & 1)
    return core << 2 | z << 1 | (place & 1)


def held_in_vmem(block):
    return pltpu.with_memory_space_constraint(block, pltpu.VMEM)


def left_in_hbm(block):
    return pltpu.with_memory_space_constraint(block, pltpu.HBM)


def columns(i, width):
    return pl.ds(pl.multiple_of(i * width, width), width)


def each_group(groups, held_keep, held_send, product):
    half, _, width = held_keep.shape
    *pairs, last, end = groups
    for number, group in enumerate(pairs):
        held, base = (held_keep, 0) if number < 2 else (held_send, half)

        @pl.loop(0, 2)
        def _(i, held=held, base=base, first=number % 2 * 2, group=group):
            group[:, columns(i, width)] = product(held, base, first + i).astype(group.dtype)

    @pl.loop(0, 2)
    def _(i):
        block = product(held_send, half, 2 + i).astype(BF16)
        for number, group in enumerate((last, end)):

            @pl.when(i == number)
            def _(group=group):
                group[...] = block


def own_kernel(left, right, weights, *rest):
    *groups, shift, held_keep, held_send, sems = rest
    t = lax.axis_index("tp")
    half, depth, width = held_keep.shape
    count = 2 * half
    cut = left.shape[1]

    def copy(held, base, i, k):
        part = pl.ds(0, cut) if k == 0 else pl.ds(cut, depth - cut)
        source = weights.at[part, columns(block_of(t, base + i), width)]
        return pltpu.make_async_copy(source, held.at[i, part], sems.at[base + i, k])

    for held, base in ((held_keep, 0), (held_send, half)):
        for i in range(half):
            for k in range(2):
                copy(held, base, i, k).start()

    def product(held, base, i):
        copy(held, base, i, 0).wait()
        total = jnp.dot(left[...], held[i, :cut], preferred_element_type=F32)
        copy(held, base, i, 1).wait()
        total += jnp.dot(right[...], held[i, cut:], preferred_element_type=F32)
        mean = jnp.mean(total, axis=0, keepdims=True)
        shift[:, columns(base + i, width)] = mean
        return total - mean

    each_group(groups, held_keep, held_send, product)


def own_product(left, right, weights):
    tokens = left.shape[0]
    depth = weights.shape[0]
    width = weights.shape[1] // 8
    return pl.pallas_call(
        own_kernel,
        out_shape=(
            *[jax.ShapeDtypeStruct((tokens, count * width), dtype) for count, dtype in GROUPS],
            jax.ShapeDtypeStruct((1, 8 * width), F32),
            pltpu.VMEM((4, depth, width), BF16),
            pltpu.VMEM((4, depth, width), BF16),
        ),
        in_specs=[vmem(), vmem(), pl.BlockSpec(memory_space=pltpu.HBM)],
        out_specs=(vmem(),) * (len(GROUPS) + 3),
        scratch_shapes=[pltpu.SemaphoreType.DMA((8, 2))],
        compiler_params=pltpu.CompilerParams(vmem_limit_bytes=VMEM_SMALL),
        cost_estimate=cheap(),
    )(left, right, left_in_hbm(weights))


def first_kernel(rows, held_keep, held_send, out):
    half, _, width = held_keep.shape
    depth = rows.shape[1]
    for held, base in ((held_keep, 0), (held_send, half)):

        @pl.loop(0, half)
        def _(i, held=held, base=base):
            out[:, columns(base + i, width)] = jnp.dot(
                rows[...], held[i, :depth], preferred_element_type=F32
            )


def first_product(rows, held, after=()):
    shape = (rows.shape[0], 8 * held[0].shape[2])
    args = [rows, *map(held_in_vmem, held)]
    return ordered_call(first_kernel, [(shape, F32)], args, after, cheap())[0]


def second_kernel(rows, held_keep, held_send, start, shift, *groups):
    _, depth, width = held_keep.shape
    cut = depth - rows.shape[1]

    def product(held, base, i):
        total = jnp.dot(rows[...], held[i, cut:], preferred_element_type=F32)
        return total + start[:, columns(base + i, width)] - shift[:, columns(base + i, width)]

    each_group(groups, held_keep, held_send, product)


def second_product(rows, held, start, shift, after=()):
    tokens = rows.shape[0]
    held_keep, held_send = held
    width = held_keep.shape[2]
    return ordered_call(
        second_kernel,
        [((tokens, count * width), dtype) for count, dtype in GROUPS],
        [rows, held_in_vmem(held_keep), held_in_vmem(held_send), start, shift],
        after,
        cheap(),
    )


def hold_kernel(factor, *rest):
    held, sems = rest[-2:]
    t = lax.axis_index("tp")
    count, rows, _ = held.shape

    def copy(i):
        start = pl.multiple_of(block_of(t, i) * rows, rows)
        return pltpu.make_async_copy(factor.at[pl.ds(start, rows)], held.at[i], sems.at[i])

    for i in range(count):
        copy(i).start()
    for i in range(count):
        copy(i).wait()


def hold(factor, after):
    deep, wide = factor.shape
    return pl.pallas_call(
        hold_kernel,
        out_shape=pltpu.VMEM((8, deep // 8, wide), BF16),
        in_specs=[pl.BlockSpec(memory_space=pltpu.HBM)]
        + [pl.BlockSpec(memory_space=pl.ANY)] * len(after),
        out_specs=vmem(),
        scratch_shapes=[pltpu.SemaphoreType.DMA((8,))],
        compiler_params=pltpu.CompilerParams(vmem_limit_bytes=VMEM_SMALL),
        cost_estimate=cheap(),
    )(left_in_hbm(factor), *after)


def white_kernel(places, *refs):
    parts = refs[: len(places)]
    factor, *terms, out = refs[len(places) :]
    depth = factor.shape[1]
    sums = [term[...].astype(F32) for term in terms]
    for rows, place in zip(parts, places):
        for i in range(rows.shape[1] // depth):
            block = rows[:, i * depth : (i + 1) * depth]
            sums.append(jnp.dot(block, factor[place + i], preferred_element_type=F32))
    out[...] = sum(sums[1:], sums[0]).astype(out.dtype)


def white_product(dtype, factor, parts, *terms, cost=None):
    rows = list(parts.values())
    shape = (rows[0].shape[0], factor.shape[2])
    kernel = functools.partial(white_kernel, tuple(parts))
    args = [*rows, held_in_vmem(factor), *terms]
    return ordered_call(kernel, [(shape, dtype)], args, cost=cost)[0]


def cheap():
    return pl.CostEstimate(flops=1024, bytes_accessed=1024, transcendentals=0)


def slow():
    return pl.CostEstimate(flops=10**10, bytes_accessed=10**9, transcendentals=0)


def qwen_kernel(scale, second, across, first, half, out):
    x, t, y = (lax.axis_index(axis) for axis in MESH)
    z = t >> 1
    llama_side, near = x == 0, z < 2
    other = jnp.where(llama_side, across[...], half[...])
    own = jnp.where(llama_side == near, first[...], second[...])
    flip = (z & 1) == y
    top, bottom = jnp.where(flip, other, own), jnp.where(flip, own, other)
    wide = jnp.concatenate([top, bottom], axis=0).astype(F32)
    out[...] = (scale * (wide - jnp.mean(wide, axis=0, keepdims=True))).astype(BF16)


def held_llama_kernel(half, across, first, out):
    x, t, _ = (lax.axis_index(axis) for axis in MESH)
    near = (t >> 1) < 2
    moved = jnp.where(near, first[...], across[...])
    stayed = jnp.where(near, half[...], first[...])
    out[...] = jnp.where(x == 0, stayed, moved)


def settled_kernel(held, diagonal, out):
    t, y = lax.axis_index("tp"), lax.axis_index("dp")
    out[...] = jnp.where(((t >> 1) & 1) == y, held[...], diagonal[...])


def cross_kernel(core, qwen, first, second, *rest):
    out, blocks, sems = rest[-3:]
    core = lax.axis_index("tp") & 1 if core == 0 else 1 - (lax.axis_index("tp") & 1)
    count, rows, _ = blocks.shape

    def copy(i):
        start = pl.multiple_of((core * count + i) * rows, rows)
        return pltpu.make_async_copy(blocks.at[i], out.at[pl.ds(start, rows)], sems.at[i])

    for i in range(count):
        part = slice(i * rows, (i + 1) * rows)
        llama = jnp.concatenate([first[:, part], second[:, part]], axis=0)
        blocks[i] = lax.dot_general(
            llama, qwen[...], (((0,), (0,)), ((), ())), preferred_element_type=F32
        )
        copy(i).start()
    for i in range(count):
        copy(i).wait()


def cross_product(core, qwen, first, second, out=None):
    _, width = qwen.shape
    features = first.shape[1]
    rows = min(128, features)
    steps = features // rows
    hbm = pl.BlockSpec(memory_space=pltpu.HBM)
    extra = [] if out is None else [out]
    return pl.pallas_call(
        functools.partial(cross_kernel, core),
        out_shape=jax.ShapeDtypeStruct((2 * features, width), F32),
        in_specs=[vmem()] * 3 + [hbm] * len(extra),
        out_specs=hbm,
        input_output_aliases={3: 0} if extra else {},
        scratch_shapes=[pltpu.VMEM((steps, rows, width), F32), pltpu.SemaphoreType.DMA((steps,))],
        compiler_params=pltpu.CompilerParams(vmem_limit_bytes=VMEM_LIMIT),
        cost_estimate=slow(),
    )(qwen, first, second, *extra)


def swapped(block, axis, mask):
    count = lax.axis_size(axis)
    return lax.ppermute(block, axis, [(i, i ^ mask) for i in range(count)])


def ordered_call(kernel, shapes, args, after=(), cost=None):
    def body(*refs):
        kernel(*refs[: len(args)], *refs[len(args) + len(after) :])

    return pl.pallas_call(
        body,
        out_shape=tuple(jax.ShapeDtypeStruct(shape, dtype) for shape, dtype in shapes),
        in_specs=[vmem()] * len(args) + [pl.BlockSpec(memory_space=pl.ANY)] * len(after),
        out_specs=tuple(vmem() for _ in shapes),
        compiler_params=pltpu.CompilerParams(vmem_limit_bytes=VMEM_SMALL),
        cost_estimate=cost or slow(),
    )(*args, *after)


def cut_at(rows, cut):
    tokens, width = rows.shape

    def kernel(whole, left, right):
        left[...] = whole[:, :cut]
        right[...] = whole[:, cut:]

    shapes = [((tokens, cut), rows.dtype), ((tokens, width - cut), rows.dtype)]
    return ordered_call(kernel, shapes, [rows], cost=cheap())


def added(keep, *got, after=()):
    def kernel(*refs):
        *terms, wide, narrow = refs
        wide[...] = sum(term[...].astype(F32) for term in terms)
        narrow[...] = wide[...].astype(BF16)

    return ordered_call(kernel, [(keep.shape, F32), (keep.shape, BF16)], [keep, *got], after)


def total(keep, *got, after=(), cost=None):
    width = got[0].shape[1]

    def kernel(own, *refs):
        *parts, out = refs
        for i, part in enumerate(parts):
            at = slice(i * width, (i + 1) * width)
            out[:, at] = (own[:, at] + part[...].astype(F32)).astype(BF16)

    return ordered_call(kernel, [(keep.shape, BF16)], [keep, *got], after, cost)[0]


def beside(left, right, after=()):
    tokens, width = left.shape

    def kernel(first, second, out):
        out[:, :width] = first[...]
        out[:, width:] = second[...]

    return ordered_call(kernel, [((tokens, 2 * width), left.dtype)], [left, right], after)[0]


def total_cut(keep, got, after=()):
    tokens, width = keep.shape
    half = width // 2

    def kernel(own, other, out, left, right):
        out[...] = (own[...] + other[...].astype(F32)).astype(BF16)
        left[...] = out[:, :half]
        right[...] = out[:, half:]

    shapes = [((tokens, width), BF16)] + [((tokens, half), BF16)] * 2
    return ordered_call(kernel, shapes, [keep, got], after)


def flat(x, t, y):
    return (x * 8 + t) * 2 + y


def route(block, moves):
    return lax.ppermute(block, MESH, [(flat(*a), flat(*b)) for a, b in moves])


def plan():
    across, first, second, neighbour, diagonal = [], [], [], [], []
    for t in range(8):
        z, core = t >> 1, t & 1
        for y in range(2):
            across.append(((1, t, y), (0, t, y)))
            if z >= 2:
                across.append(((0, t, y), (1, t, y)))
                first.append(((0, t, y), (1, t - 4, y)))
                first.append(((1, t, 1 - y), (1, t, y)))
                second.append(((1, t, 1 - y), (0, t, y)))
            else:
                first.append(((0, t, y), (0, t + 4, y)))
                first.append(((1, t, 1 - y), (0, t, y)))
                second.append(((1, t, 1 - y), (1, t, y)))
            for x in range(2):
                if z & 1 == y:
                    neighbour.append(((x, t, y), (x, t ^ 2, y)))
                else:
                    neighbour.append(((x, t, y), (x, t, 1 - y)))
                    diagonal.append(((x, t, y), (x, t ^ 2, 1 - y)))
    return across, first, second, neighbour, diagonal


def pipelined(hidden, down_weight, whitening):
    acts, weights, factor = hidden[0], down_weight[0], whitening[0]
    across, first, second, neighbour, diagonal = plan()

    depth = acts.shape[1]
    pieces = cut_at(acts, depth * CUT[0] // CUT[1] // 256 * 256)
    others = [swapped(piece, "dp", 1) for piece in pieces]
    o_keep, o_pass, o_other, *o_give, shift, held_keep, held_send = own_product(*pieces, weights)
    held = held_keep, held_send
    o_give = total(o_pass, *[swapped(piece, "tp", 1) for piece in o_give], cost=cheap())
    o_other = swapped(o_other, "tp", 1)
    start = first_product(others[0], held, after=[o_give])
    o_keep, o_give = added(o_keep, o_other, swapped(o_give, "tp", 2), after=[start])
    p_keep, p_pass, p_other, *p_give = second_product(
        others[1], held, start, shift, after=[o_give]
    )
    p_give = total(p_pass, *[swapped(piece, "tp", 1) for piece in p_give], cost=cheap())
    p_other = swapped(p_other, "tp", 1)
    held_factor = hold(factor, after=[p_give])
    o_sum = total(o_keep, swapped(o_give, "tp", 4), after=[held_factor])
    p_keep, p_give = added(p_keep, p_other, swapped(p_give, "tp", 2), after=[o_sum])
    o_sum = beside(o_sum, swapped(o_sum, "tp", 2))
    o_white = white_product(F32, held_factor, {0: o_sum})
    o_white = white_product(BF16, held_factor, {4: swapped(o_sum, "tp", 1)}, o_white)
    got = swapped(o_white, "dp", 1)
    p_sum, *p_pieces = total_cut(p_keep, swapped(p_give, "tp", 4), after=[o_white])
    p_near = swapped(p_sum, "tp", 2)
    p_left, p_right = [swapped(piece, "tp", 1) for piece in p_pieces]
    half = white_product(
        F32, held_factor, {0: p_sum, 4: p_left, 5: p_right}, cost=cheap()
    )
    half = white_product(F32, held_factor, {2: p_near}, half)
    half = white_product(BF16, held_factor, {6: swapped(p_near, "tp", 1)}, half, got)

    tokens, width = half.shape
    across = route(half, across)
    first = route(half, first)
    second = route(half, second)
    qwen = ordered_call(
        functools.partial(qwen_kernel, 1.0 / math.sqrt(2 * tokens)),
        [((2 * tokens, width), BF16)],
        [second, across, first, half],
    )[0]
    held = ordered_call(
        held_llama_kernel, [(half.shape, BF16)], [half, across, first], after=[qwen]
    )[0]
    beside_it = route(held, neighbour)
    diagonal = route(held, diagonal)
    other_beside = swapped(beside_it, "tp", 1)
    settled = ordered_call(
        settled_kernel, [(half.shape, BF16)], [held, diagonal], after=[other_beside]
    )[0]
    out = cross_product(0, qwen, settled, beside_it)
    return cross_product(1, qwen, swapped(settled, "tp", 1), other_beside, out)


def general(hidden, down_weight, whitening):
    acts, weights, factor = hidden[0], down_weight[0], whitening[0]
    tokens = lax.all_gather(acts, "dp", axis=0, tiled=True)
    partial = jnp.dot(tokens, weights, preferred_element_type=F32)
    outputs = lax.psum(partial, "tp").astype(BF16).astype(F32)
    centered = (outputs - jnp.mean(outputs, axis=0, keepdims=True)).astype(BF16)
    block = lax.psum_scatter(
        jnp.dot(centered, factor, preferred_element_type=F32),
        "dp",
        scatter_dimension=0,
        tiled=True,
    ).astype(BF16)
    both = lax.all_gather(block, "mp", axis=0)
    qwen = lax.all_gather(both[1], "dp", axis=0, tiled=True)
    llama = lax.all_gather(both[0], "tp", axis=1, tiled=True)
    width = llama.shape[1] // lax.axis_size("mp")
    llama = lax.dynamic_slice_in_dim(llama, lax.axis_index("mp") * width, width, 1)
    llama = lax.all_to_all(llama, "dp", split_axis=1, concat_axis=0, tiled=True)
    cross = lax.dot_general(llama, qwen, (((0,), (0,)), ((), ())), preferred_element_type=F32)
    return cross * (1.0 / math.sqrt(qwen.shape[0]))


def solution(mesh):
    placed = (P("mp", "dp", "tp"), P("mp", "tp", "dp"), P("mp", "dp", "tp"))
    sizes = tuple(mesh.shape[axis] for axis in MESH)
    body = pipelined if sizes == (2, 8, 2) else general
    return jax.shard_map(
        body, mesh=mesh, in_specs=placed, out_specs=P(("mp", "dp"), "tp"), check_vma=False
    )
```

```python
import functools
import math

import jax
import jax.numpy as jnp
from jax import lax
from jax.experimental import pallas as pl
from jax.experimental.pallas import tpu as pltpu
from jax.sharding import PartitionSpec as P

F32 = jnp.float32
BF16 = jnp.bfloat16
VMEM_LIMIT = 8 * 2**20
VMEM_SMALL = 3 * 2**20
MESH = ("mp", "tp", "dp")
CUT = (5, 7)
GROUPS = ((2, F32), (2, F32), (2, BF16), (1, BF16), (1, BF16))


def vmem():
    return pl.BlockSpec(memory_space=pltpu.VMEM)


def block_of(t, place):
    core, z = (t & 1) ^ (place >> 2), ((t >> 1) & 1) ^ ((place >> 1) & 1)
    return core << 2 | z << 1 | (place & 1)


def held_in_vmem(block):
    return pltpu.with_memory_space_constraint(block, pltpu.VMEM)


def left_in_hbm(block):
    return pltpu.with_memory_space_constraint(block, pltpu.HBM)


def columns(i, width):
    return pl.ds(pl.multiple_of(i * width, width), width)


def each_group(groups, held_keep, held_send, product):
    half, _, width = held_keep.shape
    *pairs, last, end = groups
    for number, group in enumerate(pairs):
        held, base = (held_keep, 0) if number < 2 else (held_send, half)

        @pl.loop(0, 2)
        def _(i, held=held, base=base, first=number % 2 * 2, group=group):
            group[:, columns(i, width)] = product(held, base, first + i).astype(group.dtype)

    @pl.loop(0, 2)
    def _(i):
        block = product(held_send, half, 2 + i).astype(BF16)
        for number, group in enumerate((last, end)):

            @pl.when(i == number)
            def _(group=group):
                group[...] = block


def own_kernel(left, right, weights, *rest):
    *groups, shift, held_keep, held_send, sems = rest
    t = lax.axis_index("tp")
    half, depth, width = held_keep.shape
    count = 2 * half
    cut = left.shape[1]

    def copy(held, base, i, k):
        part = pl.ds(0, cut) if k == 0 else pl.ds(cut, depth - cut)
        source = weights.at[part, columns(block_of(t, base + i), width)]
        return pltpu.make_async_copy(source, held.at[i, part], sems.at[base + i, k])

    for held, base in ((held_keep, 0), (held_send, half)):
        for i in range(half):
            for k in range(2):
                copy(held, base, i, k).start()

    def product(held, base, i):
        copy(held, base, i, 0).wait()
        total = jnp.dot(left[...], held[i, :cut], preferred_element_type=F32)
        copy(held, base, i, 1).wait()
        total += jnp.dot(right[...], held[i, cut:], preferred_element_type=F32)
        mean = jnp.mean(total, axis=0, keepdims=True)
        shift[:, columns(base + i, width)] = mean
        return total - mean

    each_group(groups, held_keep, held_send, product)


def own_product(left, right, weights):
    tokens = left.shape[0]
    depth = weights.shape[0]
    width = weights.shape[1] // 8
    return pl.pallas_call(
        own_kernel,
        out_shape=(
            *[jax.ShapeDtypeStruct((tokens, count * width), dtype) for count, dtype in GROUPS],
            jax.ShapeDtypeStruct((1, 8 * width), F32),
            pltpu.VMEM((4, depth, width), BF16),
            pltpu.VMEM((4, depth, width), BF16),
        ),
        in_specs=[vmem(), vmem(), pl.BlockSpec(memory_space=pltpu.HBM)],
        out_specs=(vmem(),) * (len(GROUPS) + 3),
        scratch_shapes=[pltpu.SemaphoreType.DMA((8, 2))],
        compiler_params=pltpu.CompilerParams(vmem_limit_bytes=VMEM_SMALL),
        cost_estimate=cheap(),
    )(left, right, left_in_hbm(weights))


def first_kernel(rows, held_keep, held_send, out):
    half, _, width = held_keep.shape
    depth = rows.shape[1]
    for held, base in ((held_keep, 0), (held_send, half)):

        @pl.loop(0, half)
        def _(i, held=held, base=base):
            out[:, columns(base + i, width)] = jnp.dot(
                rows[...], held[i, :depth], preferred_element_type=F32
            )


def first_product(rows, held, after=()):
    shape = (rows.shape[0], 8 * held[0].shape[2])
    args = [rows, *map(held_in_vmem, held)]
    return ordered_call(first_kernel, [(shape, F32)], args, after, cheap())[0]


def second_kernel(rows, held_keep, held_send, start, shift, *groups):
    _, depth, width = held_keep.shape
    cut = depth - rows.shape[1]

    def product(held, base, i):
        total = jnp.dot(rows[...], held[i, cut:], preferred_element_type=F32)
        return total + start[:, columns(base + i, width)] - shift[:, columns(base + i, width)]

    each_group(groups, held_keep, held_send, product)


def second_product(rows, held, start, shift, after=()):
    tokens = rows.shape[0]
    held_keep, held_send = held
    width = held_keep.shape[2]
    return ordered_call(
        second_kernel,
        [((tokens, count * width), dtype) for count, dtype in GROUPS],
        [rows, held_in_vmem(held_keep), held_in_vmem(held_send), start, shift],
        after,
        cheap(),
    )


def hold_kernel(factor, *rest):
    held, sems = rest[-2:]
    t = lax.axis_index("tp")
    count, rows, _ = held.shape

    def copy(i):
        start = pl.multiple_of(block_of(t, i) * rows, rows)
        return pltpu.make_async_copy(factor.at[pl.ds(start, rows)], held.at[i], sems.at[i])

    for i in range(count):
        copy(i).start()
    for i in range(count):
        copy(i).wait()


def hold(factor, after):
    deep, wide = factor.shape
    return pl.pallas_call(
        hold_kernel,
        out_shape=pltpu.VMEM((8, deep // 8, wide), BF16),
        in_specs=[pl.BlockSpec(memory_space=pltpu.HBM)]
        + [pl.BlockSpec(memory_space=pl.ANY)] * len(after),
        out_specs=vmem(),
        scratch_shapes=[pltpu.SemaphoreType.DMA((8,))],
        compiler_params=pltpu.CompilerParams(vmem_limit_bytes=VMEM_SMALL),
        cost_estimate=cheap(),
    )(left_in_hbm(factor), *after)


def white_kernel(places, *refs):
    parts = refs[: len(places)]
    factor, *terms, out = refs[len(places) :]
    depth = factor.shape[1]
    sums = [term[...].astype(F32) for term in terms]
    for rows, place in zip(parts, places):
        for i in range(rows.shape[1] // depth):
            block = rows[:, i * depth : (i + 1) * depth]
            sums.append(jnp.dot(block, factor[place + i], preferred_element_type=F32))
    out[...] = sum(sums[1:], sums[0]).astype(out.dtype)


def white_product(dtype, factor, parts, *terms, cost=None):
    rows = list(parts.values())
    shape = (rows[0].shape[0], factor.shape[2])
    kernel = functools.partial(white_kernel, tuple(parts))
    args = [*rows, held_in_vmem(factor), *terms]
    return ordered_call(kernel, [(shape, dtype)], args, cost=cost)[0]


def cheap():
    return pl.CostEstimate(flops=1024, bytes_accessed=1024, transcendentals=0)


def slow():
    return pl.CostEstimate(flops=10**10, bytes_accessed=10**9, transcendentals=0)


def qwen_kernel(scale, mine, first, swap, out):
    x, t, y = (lax.axis_index(axis) for axis in MESH)
    z = t >> 1
    theirs = jnp.where((x == 1) & (z >= 2), first[...], swap[...])
    flip = (z & 1) == y
    top = jnp.where(flip, mine[...], theirs)
    bottom = jnp.where(flip, theirs, mine[...])
    wide = jnp.concatenate([top, bottom], axis=0).astype(F32)
    out[...] = (scale * (wide - jnp.mean(wide, axis=0, keepdims=True))).astype(BF16)


def held_kernel(half, across, first, mine, out):
    x, t, _ = (lax.axis_index(axis) for axis in MESH)
    near = (t >> 1) < 2
    moved = jnp.where(near, first[...], across[...])
    stayed = jnp.where(near, half[...], first[...])
    out[...] = jnp.where(x == 0, stayed, moved)
    mine[...] = jnp.where(x == 0, across[...], half[...])


def settled_kernel(held, diagonal, out):
    t, y = lax.axis_index("tp"), lax.axis_index("dp")
    out[...] = jnp.where(((t >> 1) & 1) == y, held[...], diagonal[...])


def cross_kernel(core, qwen, first, second, *rest):
    out, blocks, sems = rest[-3:]
    core = lax.axis_index("tp") & 1 if core == 0 else 1 - (lax.axis_index("tp") & 1)
    count, rows, _ = blocks.shape

    def copy(i):
        start = pl.multiple_of((core * count + i) * rows, rows)
        return pltpu.make_async_copy(blocks.at[i], out.at[pl.ds(start, rows)], sems.at[i])

    for i in range(count):
        part = slice(i * rows, (i + 1) * rows)
        llama = jnp.concatenate([first[:, part], second[:, part]], axis=0)
        blocks[i] = lax.dot_general(
            llama, qwen[...], (((0,), (0,)), ((), ())), preferred_element_type=F32
        )
        copy(i).start()
    for i in range(count):
        copy(i).wait()


def cross_product(core, qwen, first, second, out=None):
    _, width = qwen.shape
    features = first.shape[1]
    rows = min(128, features)
    steps = features // rows
    hbm = pl.BlockSpec(memory_space=pltpu.HBM)
    extra = [] if out is None else [out]
    return pl.pallas_call(
        functools.partial(cross_kernel, core),
        out_shape=jax.ShapeDtypeStruct((2 * features, width), F32),
        in_specs=[vmem()] * 3 + [hbm] * len(extra),
        out_specs=hbm,
        input_output_aliases={3: 0} if extra else {},
        scratch_shapes=[pltpu.VMEM((steps, rows, width), F32), pltpu.SemaphoreType.DMA((steps,))],
        compiler_params=pltpu.CompilerParams(vmem_limit_bytes=VMEM_LIMIT),
        cost_estimate=slow(),
    )(qwen, first, second, *extra)


def swapped(block, axis, mask):
    count = lax.axis_size(axis)
    return lax.ppermute(block, axis, [(i, i ^ mask) for i in range(count)])


def ordered_call(kernel, shapes, args, after=(), cost=None):
    def body(*refs):
        kernel(*refs[: len(args)], *refs[len(args) + len(after) :])

    return pl.pallas_call(
        body,
        out_shape=tuple(jax.ShapeDtypeStruct(shape, dtype) for shape, dtype in shapes),
        in_specs=[vmem()] * len(args) + [pl.BlockSpec(memory_space=pl.ANY)] * len(after),
        out_specs=tuple(vmem() for _ in shapes),
        compiler_params=pltpu.CompilerParams(vmem_limit_bytes=VMEM_SMALL),
        cost_estimate=cost or slow(),
    )(*args, *after)


def cut_at(rows, cut):
    tokens, width = rows.shape

    def kernel(whole, left, right):
        left[...] = whole[:, :cut]
        right[...] = whole[:, cut:]

    shapes = [((tokens, cut), rows.dtype), ((tokens, width - cut), rows.dtype)]
    return ordered_call(kernel, shapes, [rows], cost=cheap())


def added(keep, *got, after=()):
    def kernel(*refs):
        *terms, wide, narrow = refs
        wide[...] = sum(term[...].astype(F32) for term in terms)
        narrow[...] = wide[...].astype(BF16)

    return ordered_call(kernel, [(keep.shape, F32), (keep.shape, BF16)], [keep, *got], after)


def total(keep, *got, after=(), cost=None):
    width = got[0].shape[1]

    def kernel(own, *refs):
        *parts, out = refs
        for i, part in enumerate(parts):
            at = slice(i * width, (i + 1) * width)
            out[:, at] = (own[:, at] + part[...].astype(F32)).astype(BF16)

    return ordered_call(kernel, [(keep.shape, BF16)], [keep, *got], after, cost)[0]


def beside(left, right, after=()):
    tokens, width = left.shape

    def kernel(first, second, out):
        out[:, :width] = first[...]
        out[:, width:] = second[...]

    return ordered_call(kernel, [((tokens, 2 * width), left.dtype)], [left, right], after)[0]


def total_cut(keep, got, after=()):
    tokens, width = keep.shape
    half = width // 2

    def kernel(own, other, out, left, right):
        out[...] = (own[...] + other[...].astype(F32)).astype(BF16)
        left[...] = out[:, :half]
        right[...] = out[:, half:]

    shapes = [((tokens, width), BF16)] + [((tokens, half), BF16)] * 2
    return ordered_call(kernel, shapes, [keep, got], after)


def flat(x, t, y):
    return (x * 8 + t) * 2 + y


def route(block, moves):
    return lax.ppermute(block, MESH, [(flat(*a), flat(*b)) for a, b in moves])


def plan():
    across, first, swap, neighbour, diagonal = [], [], [], [], []
    for t in range(8):
        z = t >> 1
        for y in range(2):
            across.append(((1, t, y), (0, t, y)))
            swap.append(((0, t, 1 - y), (0, t, y)))
            if z >= 2:
                across.append(((0, t, y), (1, t, y)))
                first.append(((0, t, y), (1, t - 4, y)))
                first.append(((1, t, 1 - y), (1, t, y)))
            else:
                first.append(((0, t, y), (0, t + 4, y)))
                swap.append(((1, t, 1 - y), (1, t, y)))
            for x in range(2):
                if z & 1 == y:
                    neighbour.append(((x, t, y), (x, t ^ 2, y)))
                else:
                    neighbour.append(((x, t, y), (x, t, 1 - y)))
                    diagonal.append(((x, t, y), (x, t ^ 2, 1 - y)))
    return across, first, swap, neighbour, diagonal


def pipelined(hidden, down_weight, whitening):
    acts, weights, factor = hidden[0], down_weight[0], whitening[0]
    across, first, swap, neighbour, diagonal = plan()

    depth = acts.shape[1]
    pieces = cut_at(acts, depth * CUT[0] // CUT[1] // 256 * 256)
    others = [swapped(piece, "dp", 1) for piece in pieces]
    o_keep, o_pass, o_other, *o_give, shift, held_keep, held_send = own_product(*pieces, weights)
    held = held_keep, held_send
    o_give = total(o_pass, *[swapped(piece, "tp", 1) for piece in o_give], cost=cheap())
    o_other = swapped(o_other, "tp", 1)
    start = first_product(others[0], held, after=[o_give])
    o_keep, o_give = added(o_keep, o_other, swapped(o_give, "tp", 2), after=[start])
    p_keep, p_pass, p_other, *p_give = second_product(
        others[1], held, start, shift, after=[o_give]
    )
    p_give = total(p_pass, *[swapped(piece, "tp", 1) for piece in p_give], cost=cheap())
    p_other = swapped(p_other, "tp", 1)
    held_factor = hold(factor, after=[p_give])
    o_sum = total(o_keep, swapped(o_give, "tp", 4), after=[held_factor])
    p_keep, p_give = added(p_keep, p_other, swapped(p_give, "tp", 2), after=[o_sum])
    o_sum = beside(o_sum, swapped(o_sum, "tp", 2))
    o_white = white_product(F32, held_factor, {0: o_sum})
    o_white = white_product(BF16, held_factor, {4: swapped(o_sum, "tp", 1)}, o_white)
    got = swapped(o_white, "dp", 1)
    p_sum, *p_pieces = total_cut(p_keep, swapped(p_give, "tp", 4), after=[o_white])
    p_near = swapped(p_sum, "tp", 2)
    p_left, p_right = [swapped(piece, "tp", 1) for piece in p_pieces]
    half = white_product(
        F32, held_factor, {0: p_sum, 4: p_left, 5: p_right}, cost=cheap()
    )
    half = white_product(F32, held_factor, {2: p_near}, half)
    half = white_product(BF16, held_factor, {6: swapped(p_near, "tp", 1)}, half, got)

    tokens, width = half.shape
    across = route(half, across)
    first = route(half, first)
    mine, held = ordered_call(held_kernel, [(half.shape, BF16)] * 2, [half, across, first])
    beside_it = route(held, neighbour)
    diagonal = route(held, diagonal)
    swap = route(mine, swap)
    other_beside = swapped(beside_it, "tp", 1)
    settled = ordered_call(settled_kernel, [(half.shape, BF16)], [held, diagonal])[0]
    qwen = ordered_call(
        functools.partial(qwen_kernel, 1.0 / math.sqrt(2 * tokens)),
        [((2 * tokens, width), BF16)],
        [mine, first, swap],
        after=[settled, other_beside],
    )[0]
    out = cross_product(0, qwen, settled, beside_it)
    return cross_product(1, qwen, swapped(settled, "tp", 1), other_beside, out)


def general(hidden, down_weight, whitening):
    acts, weights, factor = hidden[0], down_weight[0], whitening[0]
    tokens = lax.all_gather(acts, "dp", axis=0, tiled=True)
    partial = jnp.dot(tokens, weights, preferred_element_type=F32)
    outputs = lax.psum(partial, "tp").astype(BF16).astype(F32)
    centered = (outputs - jnp.mean(outputs, axis=0, keepdims=True)).astype(BF16)
    block = lax.psum_scatter(
        jnp.dot(centered, factor, preferred_element_type=F32),
        "dp",
        scatter_dimension=0,
        tiled=True,
    ).astype(BF16)
    both = lax.all_gather(block, "mp", axis=0)
    qwen = lax.all_gather(both[1], "dp", axis=0, tiled=True)
    llama = lax.all_gather(both[0], "tp", axis=1, tiled=True)
    width = llama.shape[1] // lax.axis_size("mp")
    llama = lax.dynamic_slice_in_dim(llama, lax.axis_index("mp") * width, width, 1)
    llama = lax.all_to_all(llama, "dp", split_axis=1, concat_axis=0, tiled=True)
    cross = lax.dot_general(llama, qwen, (((0,), (0,)), ((), ())), preferred_element_type=F32)
    return cross * (1.0 / math.sqrt(qwen.shape[0]))


def solution(mesh):
    placed = (P("mp", "dp", "tp"), P("mp", "tp", "dp"), P("mp", "dp", "tp"))
    sizes = tuple(mesh.shape[axis] for axis in MESH)
    body = pipelined if sizes == (2, 8, 2) else general
    return jax.shard_map(
        body, mesh=mesh, in_specs=placed, out_specs=P(("mp", "dp"), "tp"), check_vma=False
    )
```

```python
import functools
import math

import jax
import jax.numpy as jnp
from jax import lax
from jax.experimental import pallas as pl
from jax.experimental.pallas import tpu as pltpu
from jax.sharding import PartitionSpec as P

F32 = jnp.float32
BF16 = jnp.bfloat16
VMEM_LIMIT = 8 * 2**20
VMEM_SMALL = 3 * 2**20
MESH = ("mp", "tp", "dp")
CUT = (5, 7)
GROUPS = ((2, F32), (2, F32), (2, BF16), (1, BF16), (1, BF16))


def vmem():
    return pl.BlockSpec(memory_space=pltpu.VMEM)


def block_of(t, place):
    core, z = (t & 1) ^ (place >> 2), ((t >> 1) & 1) ^ ((place >> 1) & 1)
    return core << 2 | z << 1 | (place & 1)


def held_in_vmem(block):
    return pltpu.with_memory_space_constraint(block, pltpu.VMEM)


def left_in_hbm(block):
    return pltpu.with_memory_space_constraint(block, pltpu.HBM)


def columns(i, width):
    return pl.ds(pl.multiple_of(i * width, width), width)


def each_group(groups, held_keep, held_send, product):
    half, _, width = held_keep.shape
    *pairs, last, end = groups
    for number, group in enumerate(pairs):
        held, base = (held_keep, 0) if number < 2 else (held_send, half)

        @pl.loop(0, 2)
        def _(i, held=held, base=base, first=number % 2 * 2, group=group):
            group[:, columns(i, width)] = product(held, base, first + i).astype(group.dtype)

    @pl.loop(0, 2)
    def _(i):
        block = product(held_send, half, 2 + i).astype(BF16)
        for number, group in enumerate((last, end)):

            @pl.when(i == number)
            def _(group=group):
                group[...] = block


def own_kernel(left, right, weights, *rest):
    *groups, shift, held_keep, held_send, sems = rest
    t = lax.axis_index("tp")
    half, depth, width = held_keep.shape
    count = 2 * half
    cut = left.shape[1]

    def copy(held, base, i, k):
        part = pl.ds(0, cut) if k == 0 else pl.ds(cut, depth - cut)
        source = weights.at[part, columns(block_of(t, base + i), width)]
        return pltpu.make_async_copy(source, held.at[i, part], sems.at[base + i, k])

    for held, base in ((held_keep, 0), (held_send, half)):
        for i in range(half):
            for k in range(2):
                copy(held, base, i, k).start()

    def product(held, base, i):
        copy(held, base, i, 0).wait()
        total = jnp.dot(left[...], held[i, :cut], preferred_element_type=F32)
        copy(held, base, i, 1).wait()
        total += jnp.dot(right[...], held[i, cut:], preferred_element_type=F32)
        mean = jnp.mean(total, axis=0, keepdims=True)
        shift[:, columns(base + i, width)] = mean
        return total - mean

    each_group(groups, held_keep, held_send, product)


def own_product(left, right, weights):
    tokens = left.shape[0]
    depth = weights.shape[0]
    width = weights.shape[1] // 8
    return pl.pallas_call(
        own_kernel,
        out_shape=(
            *[jax.ShapeDtypeStruct((tokens, count * width), dtype) for count, dtype in GROUPS],
            jax.ShapeDtypeStruct((1, 8 * width), F32),
            pltpu.VMEM((4, depth, width), BF16),
            pltpu.VMEM((4, depth, width), BF16),
        ),
        in_specs=[vmem(), vmem(), pl.BlockSpec(memory_space=pltpu.HBM)],
        out_specs=(vmem(),) * (len(GROUPS) + 3),
        scratch_shapes=[pltpu.SemaphoreType.DMA((8, 2))],
        compiler_params=pltpu.CompilerParams(vmem_limit_bytes=VMEM_SMALL),
        cost_estimate=cheap(),
    )(left, right, left_in_hbm(weights))


def first_kernel(rows, held_keep, held_send, out):
    half, _, width = held_keep.shape
    depth = rows.shape[1]
    for held, base in ((held_keep, 0), (held_send, half)):

        @pl.loop(0, half)
        def _(i, held=held, base=base):
            out[:, columns(base + i, width)] = jnp.dot(
                rows[...], held[i, :depth], preferred_element_type=F32
            )


def first_product(rows, held, after=()):
    shape = (rows.shape[0], 8 * held[0].shape[2])
    args = [rows, *map(held_in_vmem, held)]
    return ordered_call(first_kernel, [(shape, F32)], args, after, cheap())[0]


def second_kernel(rows, held_keep, held_send, start, shift, *groups):
    _, depth, width = held_keep.shape
    cut = depth - rows.shape[1]

    def product(held, base, i):
        total = jnp.dot(rows[...], held[i, cut:], preferred_element_type=F32)
        return total + start[:, columns(base + i, width)] - shift[:, columns(base + i, width)]

    each_group(groups, held_keep, held_send, product)


def second_product(rows, held, start, shift, after=()):
    tokens = rows.shape[0]
    held_keep, held_send = held
    width = held_keep.shape[2]
    return ordered_call(
        second_kernel,
        [((tokens, count * width), dtype) for count, dtype in GROUPS],
        [rows, held_in_vmem(held_keep), held_in_vmem(held_send), start, shift],
        after,
        cheap(),
    )


def hold_kernel(factor, *rest):
    held, sems = rest[-2:]
    t = lax.axis_index("tp")
    count, rows, _ = held.shape

    def copy(i):
        start = pl.multiple_of(block_of(t, i) * rows, rows)
        return pltpu.make_async_copy(factor.at[pl.ds(start, rows)], held.at[i], sems.at[i])

    for i in range(count):
        copy(i).start()
    for i in range(count):
        copy(i).wait()


def hold(factor, after):
    deep, wide = factor.shape
    return pl.pallas_call(
        hold_kernel,
        out_shape=pltpu.VMEM((8, deep // 8, wide), BF16),
        in_specs=[pl.BlockSpec(memory_space=pltpu.HBM)]
        + [pl.BlockSpec(memory_space=pl.ANY)] * len(after),
        out_specs=vmem(),
        scratch_shapes=[pltpu.SemaphoreType.DMA((8,))],
        compiler_params=pltpu.CompilerParams(vmem_limit_bytes=VMEM_SMALL),
        cost_estimate=cheap(),
    )(left_in_hbm(factor), *after)


def white_kernel(places, *refs):
    parts = refs[: len(places)]
    factor, *terms, out = refs[len(places) :]
    depth = factor.shape[1]
    sums = [term[...].astype(F32) for term in terms]
    for rows, place in zip(parts, places):
        for i in range(rows.shape[1] // depth):
            block = rows[:, i * depth : (i + 1) * depth]
            sums.append(jnp.dot(block, factor[place + i], preferred_element_type=F32))
    out[...] = sum(sums[1:], sums[0]).astype(out.dtype)


def white_product(dtype, factor, parts, *terms, cost=None):
    rows = list(parts.values())
    shape = (rows[0].shape[0], factor.shape[2])
    kernel = functools.partial(white_kernel, tuple(parts))
    args = [*rows, held_in_vmem(factor), *terms]
    return ordered_call(kernel, [(shape, dtype)], args, cost=cost)[0]


def cheap():
    return pl.CostEstimate(flops=1024, bytes_accessed=1024, transcendentals=0)


def slow():
    return pl.CostEstimate(flops=10**10, bytes_accessed=10**9, transcendentals=0)


def qwen_kernel(scale, second, across, first, half, out):
    x, t, y = (lax.axis_index(axis) for axis in MESH)
    z = t >> 1
    llama_side, near = x == 0, z < 2
    other = jnp.where(llama_side, across[...], half[...])
    own = jnp.where(llama_side == near, first[...], second[...])
    flip = (z & 1) == y
    top, bottom = jnp.where(flip, other, own), jnp.where(flip, own, other)
    wide = jnp.concatenate([top, bottom], axis=0).astype(F32)
    out[...] = (scale * (wide - jnp.mean(wide, axis=0, keepdims=True))).astype(BF16)


def held_llama_kernel(half, across, first, out):
    x, t, _ = (lax.axis_index(axis) for axis in MESH)
    near = (t >> 1) < 2
    moved = jnp.where(near, first[...], across[...])
    stayed = jnp.where(near, half[...], first[...])
    out[...] = jnp.where(x == 0, stayed, moved)


def settled_kernel(held, diagonal, out):
    t, y = lax.axis_index("tp"), lax.axis_index("dp")
    out[...] = jnp.where(((t >> 1) & 1) == y, held[...], diagonal[...])


def cross_kernel(core, qwen, first, second, *rest):
    out, blocks, sems = rest[-3:]
    core = lax.axis_index("tp") & 1 if core == 0 else 1 - (lax.axis_index("tp") & 1)
    count, rows, _ = blocks.shape

    def copy(i):
        start = pl.multiple_of((core * count + i) * rows, rows)
        return pltpu.make_async_copy(blocks.at[i], out.at[pl.ds(start, rows)], sems.at[i])

    for i in range(count):
        part = slice(i * rows, (i + 1) * rows)
        llama = jnp.concatenate([first[:, part], second[:, part]], axis=0)
        blocks[i] = lax.dot_general(
            llama, qwen[...], (((0,), (0,)), ((), ())), preferred_element_type=F32
        )
        copy(i).start()
    for i in range(count):
        copy(i).wait()


def cross_product(core, qwen, first, second, out=None):
    _, width = qwen.shape
    features = first.shape[1]
    rows = min(128, features)
    steps = features // rows
    hbm = pl.BlockSpec(memory_space=pltpu.HBM)
    extra = [] if out is None else [out]
    return pl.pallas_call(
        functools.partial(cross_kernel, core),
        out_shape=jax.ShapeDtypeStruct((2 * features, width), F32),
        in_specs=[vmem()] * 3 + [hbm] * len(extra),
        out_specs=hbm,
        input_output_aliases={3: 0} if extra else {},
        scratch_shapes=[pltpu.VMEM((steps, rows, width), F32), pltpu.SemaphoreType.DMA((steps,))],
        compiler_params=pltpu.CompilerParams(vmem_limit_bytes=VMEM_LIMIT),
        cost_estimate=slow(),
    )(qwen, first, second, *extra)


def swapped(block, axis, mask):
    count = lax.axis_size(axis)
    return lax.ppermute(block, axis, [(i, i ^ mask) for i in range(count)])


def ordered_call(kernel, shapes, args, after=(), cost=None):
    def body(*refs):
        kernel(*refs[: len(args)], *refs[len(args) + len(after) :])

    return pl.pallas_call(
        body,
        out_shape=tuple(jax.ShapeDtypeStruct(shape, dtype) for shape, dtype in shapes),
        in_specs=[vmem()] * len(args) + [pl.BlockSpec(memory_space=pl.ANY)] * len(after),
        out_specs=tuple(vmem() for _ in shapes),
        compiler_params=pltpu.CompilerParams(vmem_limit_bytes=VMEM_SMALL),
        cost_estimate=cost or slow(),
    )(*args, *after)


def cut_at(rows, cut):
    tokens, width = rows.shape

    def kernel(whole, left, right):
        left[...] = whole[:, :cut]
        right[...] = whole[:, cut:]

    shapes = [((tokens, cut), rows.dtype), ((tokens, width - cut), rows.dtype)]
    return ordered_call(kernel, shapes, [rows], cost=cheap())


def added(keep, *got, after=()):
    def kernel(*refs):
        *terms, wide, narrow = refs
        wide[...] = sum(term[...].astype(F32) for term in terms)
        narrow[...] = wide[...].astype(BF16)

    return ordered_call(kernel, [(keep.shape, F32), (keep.shape, BF16)], [keep, *got], after)


def total(keep, *got, after=(), cost=None):
    width = got[0].shape[1]

    def kernel(own, *refs):
        *parts, out = refs
        for i, part in enumerate(parts):
            at = slice(i * width, (i + 1) * width)
            out[:, at] = (own[:, at] + part[...].astype(F32)).astype(BF16)

    return ordered_call(kernel, [(keep.shape, BF16)], [keep, *got], after, cost)[0]


def beside(left, right, after=()):
    tokens, width = left.shape

    def kernel(first, second, out):
        out[:, :width] = first[...]
        out[:, width:] = second[...]

    return ordered_call(kernel, [((tokens, 2 * width), left.dtype)], [left, right], after)[0]


def total_cut(keep, got, after=()):
    tokens, width = keep.shape
    half = width // 2

    def kernel(own, other, out, left, right):
        out[...] = (own[...] + other[...].astype(F32)).astype(BF16)
        left[...] = out[:, :half]
        right[...] = out[:, half:]

    shapes = [((tokens, width), BF16)] + [((tokens, half), BF16)] * 2
    return ordered_call(kernel, shapes, [keep, got], after)


def flat(x, t, y):
    return (x * 8 + t) * 2 + y


def route(block, moves):
    return lax.ppermute(block, MESH, [(flat(*a), flat(*b)) for a, b in moves])


def plan():
    across, first, second, neighbour, diagonal = [], [], [], [], []
    for t in range(8):
        z, core = t >> 1, t & 1
        for y in range(2):
            across.append(((1, t, y), (0, t, y)))
            if z >= 2:
                across.append(((0, t, y), (1, t, y)))
                first.append(((0, t, y), (1, t - 4, y)))
                first.append(((1, t, 1 - y), (1, t, y)))
                second.append(((1, t, 1 - y), (0, t, y)))
            else:
                first.append(((0, t, y), (0, t + 4, y)))
                first.append(((1, t, 1 - y), (0, t, y)))
                second.append(((1, t, 1 - y), (1, t, y)))
            for x in range(2):
                if z & 1 == y:
                    neighbour.append(((x, t, y), (x, t ^ 2, y)))
                else:
                    neighbour.append(((x, t, y), (x, t, 1 - y)))
                    diagonal.append(((x, t, y), (x, t ^ 2, 1 - y)))
    return across, first, second, neighbour, diagonal


def pipelined(hidden, down_weight, whitening):
    acts, weights, factor = hidden[0], down_weight[0], whitening[0]
    across, first, second, neighbour, diagonal = plan()

    depth = acts.shape[1]
    pieces = cut_at(acts, depth * CUT[0] // CUT[1] // 256 * 256)
    others = [swapped(piece, "dp", 1) for piece in pieces]
    o_keep, o_pass, o_other, *o_give, shift, held_keep, held_send = own_product(*pieces, weights)
    held = held_keep, held_send
    o_give = total(o_pass, *[swapped(piece, "tp", 1) for piece in o_give], cost=cheap())
    o_other = swapped(o_other, "tp", 1)
    start = first_product(others[0], held, after=[o_give])
    o_keep, o_give = added(o_keep, o_other, swapped(o_give, "tp", 2), after=[start])
    p_keep, p_pass, p_other, *p_give = second_product(
        others[1], held, start, shift, after=[o_give]
    )
    p_give = total(p_pass, *[swapped(piece, "tp", 1) for piece in p_give])
    p_other = swapped(p_other, "tp", 1)
    held_factor = hold(factor, after=[p_give])
    o_sum = total(o_keep, swapped(o_give, "tp", 4), after=[held_factor])
    p_keep, p_give = added(p_keep, p_other, swapped(p_give, "tp", 2), after=[o_sum])
    o_sum = beside(o_sum, swapped(o_sum, "tp", 2))
    o_white = white_product(F32, held_factor, {0: o_sum})
    o_white = white_product(BF16, held_factor, {4: swapped(o_sum, "tp", 1)}, o_white)
    got = swapped(o_white, "dp", 1)
    p_sum, *p_pieces = total_cut(p_keep, swapped(p_give, "tp", 4), after=[o_white])
    p_near = swapped(p_sum, "tp", 2)
    p_left, p_right = [swapped(piece, "tp", 1) for piece in p_pieces]
    half = white_product(
        F32, held_factor, {0: p_sum, 4: p_left, 5: p_right}, cost=cheap()
    )
    half = white_product(F32, held_factor, {2: p_near}, half)
    half = white_product(BF16, held_factor, {6: swapped(p_near, "tp", 1)}, half, got)

    tokens, width = half.shape
    across = route(half, across)
    first = route(half, first)
    second = route(half, second)
    qwen = ordered_call(
        functools.partial(qwen_kernel, 1.0 / math.sqrt(2 * tokens)),
        [((2 * tokens, width), BF16)],
        [second, across, first, half],
    )[0]
    held = ordered_call(
        held_llama_kernel, [(half.shape, BF16)], [half, across, first], after=[qwen]
    )[0]
    beside_it = route(held, neighbour)
    diagonal = route(held, diagonal)
    other_beside = swapped(beside_it, "tp", 1)
    settled = ordered_call(
        settled_kernel, [(half.shape, BF16)], [held, diagonal], after=[other_beside]
    )[0]
    out = cross_product(0, qwen, settled, beside_it)
    return cross_product(1, qwen, swapped(settled, "tp", 1), other_beside, out)


def general(hidden, down_weight, whitening):
    acts, weights, factor = hidden[0], down_weight[0], whitening[0]
    tokens = lax.all_gather(acts, "dp", axis=0, tiled=True)
    partial = jnp.dot(tokens, weights, preferred_element_type=F32)
    outputs = lax.psum(partial, "tp").astype(BF16).astype(F32)
    centered = (outputs - jnp.mean(outputs, axis=0, keepdims=True)).astype(BF16)
    block = lax.psum_scatter(
        jnp.dot(centered, factor, preferred_element_type=F32),
        "dp",
        scatter_dimension=0,
        tiled=True,
    ).astype(BF16)
    both = lax.all_gather(block, "mp", axis=0)
    qwen = lax.all_gather(both[1], "dp", axis=0, tiled=True)
    llama = lax.all_gather(both[0], "tp", axis=1, tiled=True)
    width = llama.shape[1] // lax.axis_size("mp")
    llama = lax.dynamic_slice_in_dim(llama, lax.axis_index("mp") * width, width, 1)
    llama = lax.all_to_all(llama, "dp", split_axis=1, concat_axis=0, tiled=True)
    cross = lax.dot_general(llama, qwen, (((0,), (0,)), ((), ())), preferred_element_type=F32)
    return cross * (1.0 / math.sqrt(qwen.shape[0]))


def solution(mesh):
    placed = (P("mp", "dp", "tp"), P("mp", "tp", "dp"), P("mp", "dp", "tp"))
    sizes = tuple(mesh.shape[axis] for axis in MESH)
    body = pipelined if sizes == (2, 8, 2) else general
    return jax.shard_map(
        body, mesh=mesh, in_specs=placed, out_specs=P(("mp", "dp"), "tp"), check_vma=False
    )
```

```python
import functools
import math

import jax
import jax.numpy as jnp
from jax import lax
from jax.experimental import pallas as pl
from jax.experimental.pallas import tpu as pltpu
from jax.sharding import PartitionSpec as P

F32 = jnp.float32
BF16 = jnp.bfloat16
VMEM_LIMIT = 8 * 2**20
VMEM_SMALL = int(3.5 * 2**20)
MESH = ("mp", "tp", "dp")
CUT = (11, 14)
GROUPS = ((2, F32), (2, F32), (2, BF16), (1, BF16), (1, BF16))


def vmem():
    return pl.BlockSpec(memory_space=pltpu.VMEM)


def block_of(t, place):
    core, z = (t & 1) ^ (place >> 2), ((t >> 1) & 1) ^ ((place >> 1) & 1)
    return core << 2 | z << 1 | (place & 1)


def held_in_vmem(block):
    return pltpu.with_memory_space_constraint(block, pltpu.VMEM)


def left_in_hbm(block):
    return pltpu.with_memory_space_constraint(block, pltpu.HBM)


def columns(i, width):
    return pl.ds(pl.multiple_of(i * width, width), width)


def each_group(groups, held_keep, held_send, product):
    half, _, width = held_keep.shape
    *pairs, last, end = groups
    for number, group in enumerate(pairs):
        held, base = (held_keep, 0) if number < 2 else (held_send, half)

        @pl.loop(0, 2)
        def _(i, held=held, base=base, first=number % 2 * 2, group=group):
            group[:, columns(i, width)] = product(held, base, first + i).astype(group.dtype)

    @pl.loop(0, 2)
    def _(i):
        block = product(held_send, half, 2 + i).astype(BF16)
        for number, group in enumerate((last, end)):

            @pl.when(i == number)
            def _(group=group):
                group[...] = block


def own_kernel(left, right, weights, *rest):
    *groups, shift, held_keep, held_send, sems = rest
    t = lax.axis_index("tp")
    half, depth, width = held_keep.shape
    count = 2 * half
    cut = left.shape[1]

    def copy(held, base, i, k):
        part = pl.ds(0, cut) if k == 0 else pl.ds(cut, depth - cut)
        source = weights.at[part, columns(block_of(t, base + i), width)]
        return pltpu.make_async_copy(source, held.at[i, part], sems.at[base + i, k])

    for held, base in ((held_keep, 0), (held_send, half)):
        for i in range(half):
            for k in range(2):
                copy(held, base, i, k).start()

    def product(held, base, i):
        copy(held, base, i, 0).wait()
        total = jnp.dot(left[...], held[i, :cut], preferred_element_type=F32)
        copy(held, base, i, 1).wait()
        total += jnp.dot(right[...], held[i, cut:], preferred_element_type=F32)
        mean = jnp.mean(total, axis=0, keepdims=True)
        shift[:, columns(base + i, width)] = mean
        return total - mean

    each_group(groups, held_keep, held_send, product)


def own_product(left, right, weights):
    tokens = left.shape[0]
    depth = weights.shape[0]
    width = weights.shape[1] // 8
    return pl.pallas_call(
        own_kernel,
        out_shape=(
            *[jax.ShapeDtypeStruct((tokens, count * width), dtype) for count, dtype in GROUPS],
            jax.ShapeDtypeStruct((1, 8 * width), F32),
            pltpu.VMEM((4, depth, width), BF16),
            pltpu.VMEM((4, depth, width), BF16),
        ),
        in_specs=[vmem(), vmem(), pl.BlockSpec(memory_space=pltpu.HBM)],
        out_specs=(vmem(),) * (len(GROUPS) + 3),
        scratch_shapes=[pltpu.SemaphoreType.DMA((8, 2))],
        compiler_params=pltpu.CompilerParams(vmem_limit_bytes=VMEM_SMALL),
        cost_estimate=cheap(),
    )(left, right, left_in_hbm(weights))


def first_kernel(rows, held_keep, held_send, out):
    half, _, width = held_keep.shape
    depth = rows.shape[1]
    for held, base in ((held_keep, 0), (held_send, half)):

        @pl.loop(0, half)
        def _(i, held=held, base=base):
            out[:, columns(base + i, width)] = jnp.dot(
                rows[...], held[i, :depth], preferred_element_type=F32
            )


def first_product(rows, held, after=()):
    shape = (rows.shape[0], 8 * held[0].shape[2])
    args = [rows, *map(held_in_vmem, held)]
    return ordered_call(first_kernel, [(shape, F32)], args, after, cheap())[0]


def second_kernel(rows, held_keep, held_send, start, shift, *groups):
    _, depth, width = held_keep.shape
    cut = depth - rows.shape[1]

    def product(held, base, i):
        total = jnp.dot(rows[...], held[i, cut:], preferred_element_type=F32)
        return total + start[:, columns(base + i, width)] - shift[:, columns(base + i, width)]

    each_group(groups, held_keep, held_send, product)


def second_product(rows, held, start, shift, after=()):
    tokens = rows.shape[0]
    held_keep, held_send = held
    width = held_keep.shape[2]
    return ordered_call(
        second_kernel,
        [((tokens, count * width), dtype) for count, dtype in GROUPS],
        [rows, held_in_vmem(held_keep), held_in_vmem(held_send), start, shift],
        after,
        cheap(),
    )


def hold_kernel(factor, *rest):
    held, sems = rest[-2:]
    t = lax.axis_index("tp")
    count, rows, _ = held.shape

    def copy(i):
        start = pl.multiple_of(block_of(t, i) * rows, rows)
        return pltpu.make_async_copy(factor.at[pl.ds(start, rows)], held.at[i], sems.at[i])

    for i in range(count):
        copy(i).start()
    for i in range(count):
        copy(i).wait()


def hold(factor, after):
    deep, wide = factor.shape
    return pl.pallas_call(
        hold_kernel,
        out_shape=pltpu.VMEM((8, deep // 8, wide), BF16),
        in_specs=[pl.BlockSpec(memory_space=pltpu.HBM)]
        + [pl.BlockSpec(memory_space=pl.ANY)] * len(after),
        out_specs=vmem(),
        scratch_shapes=[pltpu.SemaphoreType.DMA((8,))],
        compiler_params=pltpu.CompilerParams(vmem_limit_bytes=VMEM_SMALL),
        cost_estimate=cheap(),
    )(left_in_hbm(factor), *after)


def white_kernel(places, *refs):
    parts = refs[: len(places)]
    factor, *terms, out = refs[len(places) :]
    depth = factor.shape[1]
    sums = [term[...].astype(F32) for term in terms]
    for rows, place in zip(parts, places):
        for i in range(rows.shape[1] // depth):
            block = rows[:, i * depth : (i + 1) * depth]
            sums.append(jnp.dot(block, factor[place + i], preferred_element_type=F32))
    out[...] = sum(sums[1:], sums[0]).astype(out.dtype)


def white_product(dtype, factor, parts, *terms, cost=None):
    rows = list(parts.values())
    shape = (rows[0].shape[0], factor.shape[2])
    kernel = functools.partial(white_kernel, tuple(parts))
    args = [*rows, held_in_vmem(factor), *terms]
    return ordered_call(kernel, [(shape, dtype)], args, cost=cost)[0]


def cheap():
    return pl.CostEstimate(flops=1024, bytes_accessed=1024, transcendentals=0)


def slow():
    return pl.CostEstimate(flops=10**10, bytes_accessed=10**9, transcendentals=0)


def qwen_kernel(scale, second, across, first, half, out):
    x, t, y = (lax.axis_index(axis) for axis in MESH)
    z = t >> 1
    llama_side, near = x == 0, z < 2
    other = jnp.where(llama_side, across[...], half[...])
    own = jnp.where(llama_side == near, first[...], second[...])
    flip = (z & 1) == y
    top, bottom = jnp.where(flip, other, own), jnp.where(flip, own, other)
    wide = jnp.concatenate([top, bottom], axis=0).astype(F32)
    out[...] = (scale * (wide - jnp.mean(wide, axis=0, keepdims=True))).astype(BF16)


def held_llama_kernel(half, across, first, out):
    x, t, _ = (lax.axis_index(axis) for axis in MESH)
    near = (t >> 1) < 2
    moved = jnp.where(near, first[...], across[...])
    stayed = jnp.where(near, half[...], first[...])
    out[...] = jnp.where(x == 0, stayed, moved)


def settled_kernel(held, diagonal, out):
    t, y = lax.axis_index("tp"), lax.axis_index("dp")
    out[...] = jnp.where(((t >> 1) & 1) == y, held[...], diagonal[...])


def cross_kernel(core, qwen, first, second, *rest):
    out, blocks, sems = rest[-3:]
    core = lax.axis_index("tp") & 1 if core == 0 else 1 - (lax.axis_index("tp") & 1)
    count, rows, _ = blocks.shape

    def copy(i):
        start = pl.multiple_of((core * count + i) * rows, rows)
        return pltpu.make_async_copy(blocks.at[i], out.at[pl.ds(start, rows)], sems.at[i])

    for i in range(count):
        part = slice(i * rows, (i + 1) * rows)
        llama = jnp.concatenate([first[:, part], second[:, part]], axis=0)
        blocks[i] = lax.dot_general(
            llama, qwen[...], (((0,), (0,)), ((), ())), preferred_element_type=F32
        )
        copy(i).start()
    for i in range(count):
        copy(i).wait()


def cross_product(core, qwen, first, second, out=None):
    _, width = qwen.shape
    features = first.shape[1]
    rows = min(128, features)
    steps = features // rows
    hbm = pl.BlockSpec(memory_space=pltpu.HBM)
    extra = [] if out is None else [out]
    return pl.pallas_call(
        functools.partial(cross_kernel, core),
        out_shape=jax.ShapeDtypeStruct((2 * features, width), F32),
        in_specs=[vmem()] * 3 + [hbm] * len(extra),
        out_specs=hbm,
        input_output_aliases={3: 0} if extra else {},
        scratch_shapes=[pltpu.VMEM((steps, rows, width), F32), pltpu.SemaphoreType.DMA((steps,))],
        compiler_params=pltpu.CompilerParams(vmem_limit_bytes=VMEM_LIMIT),
        cost_estimate=slow(),
    )(qwen, first, second, *extra)


def swapped(block, axis, mask):
    count = lax.axis_size(axis)
    return lax.ppermute(block, axis, [(i, i ^ mask) for i in range(count)])


def ordered_call(kernel, shapes, args, after=(), cost=None):
    def body(*refs):
        kernel(*refs[: len(args)], *refs[len(args) + len(after) :])

    return pl.pallas_call(
        body,
        out_shape=tuple(jax.ShapeDtypeStruct(shape, dtype) for shape, dtype in shapes),
        in_specs=[vmem()] * len(args) + [pl.BlockSpec(memory_space=pl.ANY)] * len(after),
        out_specs=tuple(vmem() for _ in shapes),
        compiler_params=pltpu.CompilerParams(vmem_limit_bytes=VMEM_SMALL),
        cost_estimate=cost or slow(),
    )(*args, *after)


def cut_at(rows, cut):
    tokens, width = rows.shape

    def kernel(whole, left, right):
        left[...] = whole[:, :cut]
        right[...] = whole[:, cut:]

    shapes = [((tokens, cut), rows.dtype), ((tokens, width - cut), rows.dtype)]
    return ordered_call(kernel, shapes, [rows], cost=cheap())


def added(keep, *got, after=()):
    def kernel(*refs):
        *terms, wide, narrow = refs
        wide[...] = sum(term[...].astype(F32) for term in terms)
        narrow[...] = wide[...].astype(BF16)

    return ordered_call(kernel, [(keep.shape, F32), (keep.shape, BF16)], [keep, *got], after)


def total(keep, *got, after=(), cost=None):
    width = got[0].shape[1]

    def kernel(own, *refs):
        *parts, out = refs
        for i, part in enumerate(parts):
            at = slice(i * width, (i + 1) * width)
            out[:, at] = (own[:, at] + part[...].astype(F32)).astype(BF16)

    return ordered_call(kernel, [(keep.shape, BF16)], [keep, *got], after, cost)[0]


def beside(left, right, after=()):
    tokens, width = left.shape

    def kernel(first, second, out):
        out[:, :width] = first[...]
        out[:, width:] = second[...]

    return ordered_call(kernel, [((tokens, 2 * width), left.dtype)], [left, right], after)[0]


def total_cut(keep, got, after=()):
    tokens, width = keep.shape
    half = width // 2

    def kernel(own, other, out, left, right):
        out[...] = (own[...] + other[...].astype(F32)).astype(BF16)
        left[...] = out[:, :half]
        right[...] = out[:, half:]

    shapes = [((tokens, width), BF16)] + [((tokens, half), BF16)] * 2
    return ordered_call(kernel, shapes, [keep, got], after)


def flat(x, t, y):
    return (x * 8 + t) * 2 + y


def route(block, moves):
    return lax.ppermute(block, MESH, [(flat(*a), flat(*b)) for a, b in moves])


def plan():
    across, first, second, neighbour, diagonal = [], [], [], [], []
    for t in range(8):
        z, core = t >> 1, t & 1
        for y in range(2):
            across.append(((1, t, y), (0, t, y)))
            if z >= 2:
                across.append(((0, t, y), (1, t, y)))
                first.append(((0, t, y), (1, t - 4, y)))
                first.append(((1, t, 1 - y), (1, t, y)))
                second.append(((1, t, 1 - y), (0, t, y)))
            else:
                first.append(((0, t, y), (0, t + 4, y)))
                first.append(((1, t, 1 - y), (0, t, y)))
                second.append(((1, t, 1 - y), (1, t, y)))
            for x in range(2):
                if z & 1 == y:
                    neighbour.append(((x, t, y), (x, t ^ 2, y)))
                else:
                    neighbour.append(((x, t, y), (x, t, 1 - y)))
                    diagonal.append(((x, t, y), (x, t ^ 2, 1 - y)))
    return across, first, second, neighbour, diagonal


def pipelined(hidden, down_weight, whitening):
    acts, weights, factor = hidden[0], down_weight[0], whitening[0]
    across, first, second, neighbour, diagonal = plan()

    depth = acts.shape[1]
    pieces = cut_at(acts, depth * CUT[0] // CUT[1] // 256 * 256)
    others = [swapped(piece, "dp", 1) for piece in pieces]
    o_keep, o_pass, o_other, *o_give, shift, held_keep, held_send = own_product(*pieces, weights)
    held = held_keep, held_send
    o_give = total(o_pass, *[swapped(piece, "tp", 1) for piece in o_give], cost=cheap())
    o_other = swapped(o_other, "tp", 1)
    start = first_product(others[0], held, after=[o_give])
    o_keep, o_give = added(o_keep, o_other, swapped(o_give, "tp", 2), after=[start])
    p_keep, p_pass, p_other, *p_give = second_product(
        others[1], held, start, shift, after=[o_give]
    )
    p_give = total(p_pass, *[swapped(piece, "tp", 1) for piece in p_give])
    p_other = swapped(p_other, "tp", 1)
    held_factor = hold(factor, after=[p_give])
    o_sum = total(o_keep, swapped(o_give, "tp", 4), after=[held_factor])
    p_keep, p_give = added(p_keep, p_other, swapped(p_give, "tp", 2), after=[o_sum])
    o_sum = beside(o_sum, swapped(o_sum, "tp", 2))
    o_white = white_product(F32, held_factor, {0: o_sum})
    o_white = white_product(BF16, held_factor, {4: swapped(o_sum, "tp", 1)}, o_white)
    got = swapped(o_white, "dp", 1)
    p_sum, *p_pieces = total_cut(p_keep, swapped(p_give, "tp", 4), after=[o_white])
    p_near = swapped(p_sum, "tp", 2)
    p_left, p_right = [swapped(piece, "tp", 1) for piece in p_pieces]
    half = white_product(
        F32, held_factor, {0: p_sum, 4: p_left, 5: p_right}, cost=cheap()
    )
    half = white_product(F32, held_factor, {2: p_near}, half)
    half = white_product(BF16, held_factor, {6: swapped(p_near, "tp", 1)}, half, got)

    tokens, width = half.shape
    across = route(half, across)
    first = route(half, first)
    second = route(half, second)
    qwen = ordered_call(
        functools.partial(qwen_kernel, 1.0 / math.sqrt(2 * tokens)),
        [((2 * tokens, width), BF16)],
        [second, across, first, half],
    )[0]
    held = ordered_call(
        held_llama_kernel, [(half.shape, BF16)], [half, across, first], after=[qwen]
    )[0]
    beside_it = route(held, neighbour)
    diagonal = route(held, diagonal)
    other_beside = swapped(beside_it, "tp", 1)
    settled = ordered_call(
        settled_kernel, [(half.shape, BF16)], [held, diagonal], after=[other_beside]
    )[0]
    out = cross_product(0, qwen, settled, beside_it)
    return cross_product(1, qwen, swapped(settled, "tp", 1), other_beside, out)


def general(hidden, down_weight, whitening):
    acts, weights, factor = hidden[0], down_weight[0], whitening[0]
    tokens = lax.all_gather(acts, "dp", axis=0, tiled=True)
    partial = jnp.dot(tokens, weights, preferred_element_type=F32)
    outputs = lax.psum(partial, "tp").astype(BF16).astype(F32)
    centered = (outputs - jnp.mean(outputs, axis=0, keepdims=True)).astype(BF16)
    block = lax.psum_scatter(
        jnp.dot(centered, factor, preferred_element_type=F32),
        "dp",
        scatter_dimension=0,
        tiled=True,
    ).astype(BF16)
    both = lax.all_gather(block, "mp", axis=0)
    qwen = lax.all_gather(both[1], "dp", axis=0, tiled=True)
    llama = lax.all_gather(both[0], "tp", axis=1, tiled=True)
    width = llama.shape[1] // lax.axis_size("mp")
    llama = lax.dynamic_slice_in_dim(llama, lax.axis_index("mp") * width, width, 1)
    llama = lax.all_to_all(llama, "dp", split_axis=1, concat_axis=0, tiled=True)
    cross = lax.dot_general(llama, qwen, (((0,), (0,)), ((), ())), preferred_element_type=F32)
    return cross * (1.0 / math.sqrt(qwen.shape[0]))


def solution(mesh):
    placed = (P("mp", "dp", "tp"), P("mp", "tp", "dp"), P("mp", "dp", "tp"))
    sizes = tuple(mesh.shape[axis] for axis in MESH)
    body = pipelined if sizes == (2, 8, 2) else general
    return jax.shard_map(
        body, mesh=mesh, in_specs=placed, out_specs=P(("mp", "dp"), "tp"), check_vma=False
    )
```
